32 devices in a mesh: dp: 8 (over z, y), seq: 4 (over x, core).
Axes of the slice: x: 2, y: 2, z: 4, core: 2. Of those that a mesh axis runs over, the one named last changes fastest.
Arguments:
- tokens: bfloat16 [8, 512, 768], P('dp', 'seq'), may hold values from -6 to 6
- seg_ids: int32 [8, 512], P('dp', 'seq'), may hold values from 0 to 7, as said below
- slot_doc: int32 [8, 256], P('dp'), may hold values from 0 to 7, as said below
- proj_e: bfloat16 [512, 256], P('seq'), may hold values from -0.25 to 0.25
- g_attn: bfloat16 [768], replicated, may hold values from 0.5 to 1.5
- w_query: bfloat16 [768, 768], replicated, may hold values from -0.21875 to 0.21875
- w_key: bfloat16 [768, 768], replicated, may hold values from -0.21875 to 0.21875
- w_value: bfloat16 [768, 768], replicated, may hold values from -0.21875 to 0.21875
- w_out: bfloat16 [768, 768], replicated, may hold values from -0.875 to 0.875
- g_ffn: bfloat16 [768], replicated, may hold values from 0.5 to 1.5
- w_in: bfloat16 [768, 3072], replicated, may hold values from -0.21875 to 0.21875
- w_back: bfloat16 [3072, 768], replicated, may hold values from -0.109375 to 0.109375
- cotangent: bfloat16 [8, 512, 768], P('dp', 'seq'), may hold values from -6 to 6
Outputs:
- layer_out: bfloat16 [8, 512, 768], P('dp', 'seq')
- x_grad: float32 [8, 512, 768], P('dp', 'seq')
- g_attn_grad: float32 [768], P(('dp', 'seq'))
- w_query_grad: float32 [768, 768], P(('dp', 'seq'))
- w_key_grad: float32 [768, 768], P(('dp', 'seq'))
- w_value_grad: float32 [768, 768], P(('dp', 'seq'))
- w_out_grad: float32 [768, 768], P(('dp', 'seq'))
- g_ffn_grad: float32 [768], P(('dp', 'seq'))
- w_in_grad: float32 [768, 3072], P(('dp', 'seq'))
- w_back_grad: float32 [3072, 768], P(('dp', 'seq'))
- proj_e_grad: float32 [512, 256], P('seq', 'dp')
The draws below stay inside these ranges and needn't reach their ends.
Inputs may be any that keep to these rules, and one draw needn't show every extreme that they name: `seg_ids`: along each row the ids never fall, and every id from 0 to 7 holds one position or more. `slot_doc`: in each row the ids 0 to 7 own consecutive blocks of slots in increasing order, each of one slot or more.
All inputs are finite; a program needn't handle non-finite values.
Results may differ from the reference program's by a relative error of at most 0.022.
Values may be sent and summed in bfloat16 or wider, within the bound.
A program may use at most 128 MiB of HBM per device.

```python
import jax
import jax.numpy as jnp
from jax import lax

D = 768
HEADS = 12
HEAD_DIM = 64
FF = 3072
K_SLOTS = 256
S = 512
DOCS = 8
ROWS = 8
N_SEQ = 4


def draw_seg_ids(key, part):
    left_key, right_key, count_key = jax.random.split(key, 3)
    step_len = S // (4 * DOCS)
    left_count = jax.random.randint(count_key, (ROWS, 1), 0, DOCS)
    slot_index = jnp.arange(DOCS - 1)[None, :]
    left_cut = 1 + slot_index * step_len + jax.random.randint(left_key, (ROWS, DOCS - 1), 0, step_len)
    mirror = DOCS - 2 - slot_index
    right_cut = S - 1 - mirror * step_len - jax.random.randint(right_key, (ROWS, DOCS - 1), 0, step_len)
    cut_points = jnp.where(slot_index < left_count, left_cut, right_cut)
    position = jnp.arange(S)
    passed = (position[None, :, None] >= cut_points[:, None, :]).astype(jnp.int32)
    return jnp.sum(passed, axis=2).astype(jnp.int32)


def draw_slot_doc(key, part):
    block_len = K_SLOTS // DOCS
    slot_index = jnp.arange(1, DOCS)[None, :]
    cut_points = slot_index * block_len + jax.random.randint(key, (ROWS, DOCS - 1), 0, block_len)
    position = jnp.arange(K_SLOTS)
    passed = (position[None, :, None] >= cut_points[:, None, :]).astype(jnp.int32)
    return jnp.sum(passed, axis=2).astype(jnp.int32)


def block_levels(rng, extent, shards, least, largest):
    gain = 1.0
    for dim, shards_of in shards:
        heights = jax.random.uniform(jax.random.fold_in(jax.random.fold_in(rng, 6), dim), (shards_of,), jnp.float32, least / len(shards), largest / len(shards))
        gain = gain * jnp.repeat(jnp.exp(heights), extent[dim] // shards_of).reshape((-1,) + (1,) * (len(extent) - 1 - dim))
    return gain


def noise(own_key, shape, deviation, reach, cuts=(), dtype=jnp.bfloat16):
    level = block_levels(own_key, shape, cuts, -0.22, 0.18) if cuts else 1.0
    values = jax.random.normal(own_key, shape, jnp.float32) * deviation * level
    return jnp.minimum(jnp.maximum(values, -reach), reach).astype(dtype)


def setup_inputs(seed: int = 0) -> dict:
    splits = jax.random.split(jax.random.key(seed), 14)
    tokens = noise(splits[0], (ROWS, S, D), 1.0, 6.0, ((0, 8), (1, 4)))
    seg_ids = draw_seg_ids(jax.random.fold_in(splits[13], 71), 0)
    slot_doc = draw_slot_doc(jax.random.fold_in(splits[13], 71), 0)
    proj_e = noise(splits[3], (S, K_SLOTS), S ** -0.5, 0.25, ((0, 4),))
    g_attn = jnp.clip(1.0 + 0.1 * jax.random.normal(splits[4], (D,), jnp.float32), 0.5, 1.5).astype(jnp.bfloat16)
    w_query = noise(splits[5], (D, D), D ** -0.5, 0.21875)
    w_key = noise(splits[6], (D, D), D ** -0.5, 0.21875)
    w_value = noise(splits[7], (D, D), D ** -0.5, 0.21875)
    w_out = noise(splits[8], (D, D), (D // 16) ** -0.5, 0.875)
    g_ffn = jnp.clip(1.0 + 0.1 * jax.random.normal(splits[9], (D,), jnp.float32), 0.5, 1.5).astype(jnp.bfloat16)
    w_in = noise(splits[10], (D, FF), D ** -0.5, 0.21875)
    w_back = noise(splits[11], (FF, D), FF ** -0.5, 0.109375)
    cotangent = noise(splits[12], (ROWS, S, D), 1.0, 6.0, ((0, 8), (1, 4)))
    return dict(tokens=tokens, seg_ids=seg_ids, slot_doc=slot_doc, proj_e=proj_e, g_attn=g_attn, w_query=w_query, w_key=w_key, w_value=w_value, w_out=w_out, g_ffn=g_ffn, w_in=w_in, w_back=w_back, cotangent=cotangent)


@jax.custom_vjp
def low(v):
    return lax.optimization_barrier(v.astype(jnp.bfloat16)).astype(jnp.float32)

@jax.custom_vjp
def low_back(v):
    return v

def low_keep(v):
    return (low(v), None)

def low_pass(kept, grad):
    return (grad,)

def back_keep(v):
    return (v, None)

def back_low(kept, grad):
    return (low(grad),)
low.defvjp(low_keep, low_pass)
low_back.defvjp(back_keep, back_low)
exact_mode = lax.Precision.HIGHEST

def layer_norm(inputs, gain_vec):
    centre = inputs - lax.optimization_barrier(jnp.mean(inputs, axis=-1, keepdims=True))
    spread = lax.optimization_barrier(jnp.mean(centre * centre, axis=-1, keepdims=True))
    return centre * lax.rsqrt(spread + 1e-05) * gain_vec

def matmul(left_mat, right_mat):
    return jnp.einsum('rtd,de->rte', left_mat, right_mat, precision=exact_mode)

def forward(x_rows, params, seg_rows, slot_rows):
    g_attn, w_query, w_key, w_value, w_out, g_ffn, w_in, w_back, proj_e = params
    row_count = x_rows.shape[0]
    local_len = S // N_SEQ
    normed = low(layer_norm(x_rows, g_attn))
    query_proj = low_back(low(matmul(normed, w_query)))
    key_proj = low_back(low(matmul(normed, w_key)))
    value_proj = low_back(low(matmul(normed, w_value)))
    select = seg_rows[:, :, None] == slot_rows[:, None, :]
    masked_e = jnp.where(select, proj_e[None, :, :], 0.0)
    e_parts = masked_e.reshape(row_count, N_SEQ, local_len, K_SLOTS)
    part_k = low(jnp.einsum('rptj,rptd->rpjd', e_parts, key_proj.reshape(row_count, N_SEQ, local_len, D), precision=exact_mode))
    part_v = low(jnp.einsum('rptj,rptd->rpjd', e_parts, value_proj.reshape(row_count, N_SEQ, local_len, D), precision=exact_mode))
    summ_k = low_back(low(lax.optimization_barrier(jnp.sum(part_k, axis=1)))).reshape(row_count, K_SLOTS, HEADS, HEAD_DIM)
    summ_v = low_back(low(lax.optimization_barrier(jnp.sum(part_v, axis=1)))).reshape(row_count, K_SLOTS, HEADS, HEAD_DIM)
    raw_scores = jnp.einsum('rthe,rjhe->rhtj', query_proj.reshape(row_count, S, HEADS, HEAD_DIM), summ_k, precision=exact_mode)
    scores = jnp.where(select[:, None, :, :], low_back(raw_scores) * HEAD_DIM ** (-0.5), -1e+30)
    row_max = lax.optimization_barrier(jnp.max(scores, axis=-1, keepdims=True))
    exp_scores = jnp.exp(scores - row_max)
    attn_probs = exp_scores / lax.optimization_barrier(jnp.sum(exp_scores, axis=-1, keepdims=True))
    context = jnp.einsum('rhtj,rjhe->rthe', low(attn_probs), summ_v, precision=exact_mode)
    attended = low_back(low(context.reshape(row_count, S, D)))
    mid_rows = x_rows + low_back(matmul(attended, w_out))
    normed_two = low(layer_norm(mid_rows, g_ffn))
    hidden = low_back(matmul(normed_two, w_in))
    activated = low(jax.nn.gelu(hidden))
    return mid_rows + low_back(matmul(activated, w_back))

def reference(tokens, seg_ids, slot_doc, proj_e, g_attn, w_query, w_key, w_value, w_out, g_ffn, w_in, w_back, cotangent):
    weights = tuple((item.astype(jnp.float32) for item in (g_attn, w_query, w_key, w_value, w_out, g_ffn, w_in, w_back, proj_e)))
    groups = ROWS // 8
    x_groups = tokens.astype(jnp.float32).reshape(groups, 8, S, D)
    seg_groups = seg_ids.reshape(groups, 8, S)
    slot_groups = slot_doc.reshape(groups, 8, K_SLOTS)
    cot_groups = cotangent.astype(jnp.float32).reshape(groups, 8, S, D)

    def one_group(totals, group_data):
        x_rows, seg_rows, slot_rows, cot_rows = group_data

        def run(x_in, *params):
            return forward(x_in, params, seg_rows, slot_rows)
        layer_result, pullback = jax.vjp(run, x_rows, *weights)
        gradients = pullback(cot_rows)
        new_totals = tuple((total_old + grad_new for total_old, grad_new in zip(totals, gradients[1:])))
        return (new_totals, (layer_result.astype(jnp.bfloat16), gradients[0]))
    zero_sums = tuple((jnp.zeros_like(item) for item in weights))
    totals, (layer_out, x_grad) = lax.scan(one_group, zero_sums, (x_groups, seg_groups, slot_groups, cot_groups))
    layer_out = layer_out.reshape(ROWS, S, D)
    x_grad = x_grad.reshape(ROWS, S, D)
    return (layer_out, x_grad, totals[0], totals[1], totals[2], totals[3], totals[4], totals[5], totals[6], totals[7], totals[8])
```

```python
import functools
from types import SimpleNamespace

import jax
import jax.numpy as jnp
import numpy as np
from jax import lax
from jax.experimental import pallas as pl
from jax.experimental.pallas import tpu as pltpu
from jax.sharding import PartitionSpec as P

HEAD_DIM = 64
DP, SEQ = "dp", "seq"
BF = jnp.bfloat16
F32 = jnp.float32
MESH = pl.DeviceIdType.MESH
GELU_C = 0.7978845608028654
GELU_K = 0.044715


def nn(a, b):
    return lax.dot_general(a, b, (((1,), (0,)), ((), ())), preferred_element_type=F32)


def nt(a, b):
    return lax.dot_general(a, b, (((1,), (1,)), ((), ())), preferred_element_type=F32)


def selections(d_model, ff):
    unit = d_model // 16
    sel_a = np.zeros((2, d_model // 2, d_model), np.float32)
    sel_b = np.zeros((2, d_model // 2, d_model), np.float32)
    for x in range(2):
        for b in range(8):
            b2, b1, b0 = b // 4, (b // 2) % 2, b % 2
            for mat, j in ((sel_a, 4 * b0 + 2 * b1 + b2), (sel_b, 4 * b0 + 2 * b2 + b1)):
                for o in range(unit):
                    mat[x, b * unit + o, (2 * j + x) * unit + o] = 1
    q = ff // 32
    sel_c = np.zeros((2, 2, 2 * q, ff // 4), np.float32)
    for x in range(2):
        for c in range(2):
            for y in range(2):
                for o in range(q):
                    sel_c[x, c, y * q + o, (y * 4 + x * 2 + c) * q + o] = 1
    return sel_a, sel_b, sel_c


def layer_body(fused, r, sl):
    d, s = lax.axis_index(DP), lax.axis_index(SEQ)
    x, c = s // 2, s % 2
    y, lo, hi = d % 2, (d // 2) % 2, d // 4
    to_core = (d, s + 1 - 2 * c)
    to_x = (d, s + 2 - 4 * x)
    to_y = (d + 1 - 2 * y, s)
    to_lo = (d + 2 - 4 * lo, s)
    to_hi = (d + 4 - 8 * hi, s)
    lsem, ssem, rsem = r.lsem, r.ssem, r.rsem
    D = r.h1.shape[1]
    T = r.h1.shape[0]
    H = T // 2
    J = r.sk.shape[0]
    FC = D
    NF = r.w_in.shape[1] // FC
    HC = D // 2
    U = D // 16
    Q = r.wb.shape[2]
    scale = HEAD_DIM ** (-0.5)

    loads = []

    def load(src, dst):
        cp = pltpu.make_async_copy(src, dst, lsem.at[len(loads)])
        loads.append(cp)
        cp.start()
        return cp

    def rc(i, src, dst, dev):
        return pltpu.make_async_remote_copy(
            src_ref=src, dst_ref=dst, send_sem=ssem.at[i], recv_sem=rsem.at[i], device_id=dev, device_id_type=MESH
        )

    l_x = load(r.x_in, r.xb.at[pl.ds(0, H)])
    l_e = load(r.e_in, r.eb.at[pl.ds(0, H)])
    l_wq = load(r.wq_in, r.wq)
    l_wk = load(r.wk_in, r.wk)
    l_wv = load(r.wv_in, r.wv)
    l_dy = load(r.dy_in, r.dyb.at[pl.ds(0, H)])
    l_sa = load(r.sa_in.at[x], r.sa)
    l_sb = load(r.sb_in.at[x], r.sb)
    l_wo = load(r.wo_in, r.wo)
    l_sc0 = load(r.sc_in.at[x, c], r.sc.at[0])
    l_sc1 = load(r.sc_in.at[x, 1 - c], r.sc.at[1])
    l_w_in = load(r.w_in_in, r.w_in)
    l_w_back = load(r.w_back_in, r.w_back)

    partners = [to_core, to_x] + ([to_y, to_lo, to_hi] if fused else [])
    barrier = pltpu.get_barrier_semaphore()
    for dev in partners:
        pl.semaphore_signal(barrier, inc=1, device_id=dev, device_id_type=MESH)
    r.segf[0] = jnp.broadcast_to(r.seg_in[...].astype(F32), (8, H))
    pl.semaphore_wait(barrier, len(partners))

    x_seg = rc(sl.x_seg, r.segf.at[0], r.segf.at[1], to_x)
    x_e = rc(sl.x_e, r.e_in, r.eb.at[pl.ds(H, H)], to_x)
    x_x = rc(sl.x_x, r.x_in, r.xb.at[pl.ds(H, H)], to_x)
    x_dy = rc(sl.x_dy, r.dy_in, r.dyb.at[pl.ds(H, H)], to_x)
    x_x.start()
    x_seg.start()
    x_e.start()

    rows_i = lax.broadcasted_iota(jnp.int32, (T, T), 0)
    cols_i = lax.broadcasted_iota(jnp.int32, (T, T), 1)
    r.eye[...] = jnp.where(rows_i == cols_i, 1.0, 0.0).astype(BF)
    ga = r.ga[...].astype(F32)
    gf = r.gf[...].astype(F32)
    inv_d = 1.0 / D

    def norm_rows(v):
        cen = v - jnp.sum(v, axis=1, keepdims=True) * inv_d
        rstd = lax.rsqrt(jnp.sum(cen * cen, axis=1, keepdims=True) * inv_d + 1e-5)
        return cen * rstd, rstd

    NR = 64

    def norm_one(i):
        rows = pl.ds(pl.multiple_of(i * NR, NR), NR)
        xh, rstd = norm_rows(r.xb[rows, :].astype(F32))
        r.xh1[rows, :] = xh
        r.rs1[rows, :] = jnp.broadcast_to(rstd, (NR, 128))
        r.h1[rows, :] = (xh * ga).astype(BF)

    l_x.wait()

    @pl.loop(0, 2)
    def _(p):
        @pl.when(p == 1)
        def _():
            x_x.wait()
            x_dy.start()

        @pl.loop(0, H // NR)
        def _(i):
            norm_one(p * (H // NR) + i)

        @pl.when(p == 0)
        def _():
            l_wq.wait()
            l_wk.wait()
            l_wv.wait()

        rows = pl.ds(pl.multiple_of(p * H, H), H)
        h = r.h1[rows, :]
        r.q[rows, :] = nn(h, r.wq[...]).astype(BF)
        r.k[rows, :] = nn(h, r.wk[...]).astype(BF)
        r.v[rows, :] = nn(h, r.wv[...]).astype(BF)

    x_seg.wait()
    x_e.wait()
    l_e.wait()
    seg_row = jnp.concatenate([r.segf[0, 0:1, :], r.segf[1, 0:1, :]], axis=1)
    slot_row = r.slot_in[...].astype(F32)
    eye = r.eye[...]
    zero = jnp.zeros((), BF)
    seg_col = nt(eye, jnp.broadcast_to(seg_row, (J, T)).astype(BF))
    slot_col = nt(eye, jnp.broadcast_to(slot_row, (T, J)).astype(BF))
    r.sel_t[...] = jnp.where(slot_col == seg_row, 1.0, 0.0)
    r.me[...] = jnp.where(seg_col == slot_row, r.eb[...].astype(F32), 0.0).astype(BF)
    r.met[...] = nt(eye, r.me[...]).astype(BF)

    r.pk[0] = nn(r.met[...], r.k[...]).astype(BF)
    c_pk = rc(sl.c_pk, r.pk.at[0], r.pkr.at[0], to_core)
    c_pk.start()
    r.pk[1] = nn(r.met[...], r.v[...]).astype(BF)
    c_pv = rc(sl.c_pv, r.pk.at[1], r.pkr.at[1], to_core)
    c_pv.start()
    l_sa.wait()
    l_sb.wait()
    r.h1t[0] = nt(r.sb[...], r.h1[...]).astype(BF)
    c_h1t = rc(sl.c_h1t, r.h1t.at[0], r.h1t.at[1], to_core)
    c_h1t.start()
    c_pk.wait()
    r.sk[...] = (r.pk[0].astype(F32) + r.pkr[0].astype(F32)).astype(BF)
    c_pv.wait()
    r.sv[...] = (r.pk[1].astype(F32) + r.pkr[1].astype(F32)).astype(BF)

    lane = lax.broadcasted_iota(jnp.int32, (T, 128), 1)
    head_mask = [jnp.where(lane < 64, 1.0, 0.0).astype(BF), jnp.where(lane < 64, 0.0, 1.0).astype(BF)]

    @pl.loop(0, D // 128)
    def _(i):
        cols = pl.ds(pl.multiple_of(i * 128, 128), 128)
        q2, sk2, sv2 = r.q[:, cols], r.sk[:, cols], r.sv[:, cols]
        r.skt[cols, :] = nt(r.eye[0:128, 0:128], sk2).astype(BF)
        r.svt[...] = nt(r.eye[0:128, 0:128], sv2).astype(BF)
        for h in range(2):
            raw = nt(sk2, q2 * head_mask[h])
            sc = jnp.where(r.sel_t[...] > 0.5, raw * scale, -1e30)
            e = jnp.exp(sc - jnp.max(sc, axis=0, keepdims=True))
            pt = (e * (1.0 / jnp.sum(e, axis=0, keepdims=True))).astype(BF)
            r.pt[i, :, h * T : (h + 1) * T] = pt
            r.ctxt[pl.ds(pl.multiple_of(i * 128 + h * 64, 64), 64), :] = nn(
                r.svt[h * 64 : (h + 1) * 64, :], pt
            ).astype(BF)
        r.ctx[:, cols] = nt(r.eye[...], r.ctxt[cols, :]).astype(BF)

    l_wo.wait()

    @pl.loop(0, 2)
    def _(p):
        rows = pl.ds(pl.multiple_of(p * H, H), H)
        r.mid[rows, :] = r.xb[rows, :].astype(F32) + nn(r.ctx[rows, :], r.wo[...])

    @pl.loop(0, T // NR)
    def _(i):
        rows = pl.ds(pl.multiple_of(i * NR, NR), NR)
        xh, rstd = norm_rows(r.mid[rows, :])
        r.xh2[rows, :] = xh
        r.rs2[rows, :] = jnp.broadcast_to(rstd, (NR, 128))
        r.h2[rows, :] = (xh * gf).astype(BF)

    r.h2t[0] = nt(r.sa[...], r.h2[...]).astype(BF)
    c_h2t = rc(sl.c_h2t, r.h2t.at[0], r.h2t.at[1], to_core)
    c_h2t.start()
    x_dy.wait()
    l_dy.wait()
    c_dy = rc(sl.c_dy, r.dyb, r.dyo, to_core)
    c_dy.start()
    r.ctt[0] = nn(r.sb[...], r.ctxt[...]).astype(BF)
    c_ctt = rc(sl.c_ctt, r.ctt.at[0], r.ctt.at[1], to_core)
    c_ctt.start()
    l_w_in.wait()
    l_w_back.wait()
    l_sc0.wait()
    l_sc1.wait()

    def c_at(f):
        return rc(sl.c_at + f, r.at.at[f, 1], r.atr.at[f], to_core)

    def c_du(f):
        return rc(sl.c_du + f, r.du.at[f, 1 - c], r.dur.at[f], to_core)

    def y_wb(f):
        return rc(sl.y_wb + f, r.wb.at[f, 1 - y], r.wb1.at[f], to_y)

    def y_wi(f):
        return rc(sl.y_wi + f, r.wi.at[f, pl.ds(pl.multiple_of((1 - y) * 4 * U, 16), 4 * U)], r.wi1.at[f], to_y)

    SB = 256

    @pl.loop(0, NF + 1)
    def _(f):
        @pl.when(f < NF)
        def _():
            for b in range(FC // SB):
                off = pl.multiple_of(f * FC + b * SB, SB)
                u = nn(r.h2[...], r.w_in[:, pl.ds(off, SB)])
                g = nt(r.dyb[...], r.w_back[pl.ds(off, SB), :])
                u2 = u * u
                th = jnp.tanh(GELU_C * (u + GELU_K * (u2 * u)))
                half = 0.5 * (1.0 + th)
                r.a[:, b * SB : (b + 1) * SB] = (u * half).astype(BF)
                slope = half + 0.5 * u * (1.0 - th * th) * (GELU_C * (1.0 + 3.0 * GELU_K * u2))
                r.duf[:, b * SB : (b + 1) * SB] = (slope * g).astype(BF)
            r.du[f, 0] = r.duf[:, 0:HC]
            r.du[f, 1] = r.duf[:, HC : 2 * HC]
            c_du(f).start()
            r.at[f, 0] = nt(r.sc[0], r.a[...]).astype(BF)
            r.at[f, 1] = nt(r.sc[1], r.a[...]).astype(BF)
            c_at(f).start()
            rows = pl.ds(pl.multiple_of(f * FC, FC), FC)
            part_o = nn(r.a[0:H, :], r.w_back[rows, :])
            part_d = nt(r.duf[...], r.w_in[:, rows])

            @pl.when(f == 0)
            def _():
                c_dy.wait()
                c_h2t.wait()
                r.oacc[...] = part_o
                r.dacc[...] = part_d

            @pl.when(f > 0)
            def _():
                r.oacc[...] += part_o
                r.dacc[...] += part_d

        @pl.when(f > 0)
        def _():
            g = f - 1
            c_at(g).wait()
            wb = nn(r.at[g, 0], r.dyb[...]) + nn(r.atr[g], r.dyo[...])
            r.wb[g, 0] = wb[0:Q, :].astype(BF)
            r.wb[g, 1] = wb[Q : 2 * Q, :].astype(BF)
            if fused:
                y_wb(g).start()
            c_du(g).wait()
            wi = nn(r.h2t[0], r.du[g, c]) + nn(r.h2t[1], r.dur[g])
            r.wi[g] = wi.astype(BF)
            if fused:
                y_wi(g).start()

    def add_into(dst, idx, src):
        dst[idx] = (dst[idx].astype(F32) + src.astype(F32)).astype(BF)

    def lo_wb(p):
        return rc(sl.lo_wb + p, r.wb.at[2 * p + 1 - lo, y], r.wb2.at[p], to_lo)

    def hi_wb():
        return rc(sl.hi_wb, r.wb.at[2 * (1 - hi) + lo, y], r.wb3, to_hi)

    def wi_rows(start, count):
        return pl.ds(pl.multiple_of(start, 16), count)

    def lo_wi(f):
        return rc(sl.lo_wi + f, r.wi.at[f, wi_rows(y * 4 * U + (1 - lo) * 2 * U, 2 * U)], r.wi2.at[f], to_lo)

    def hi_wi(f):
        return rc(
            sl.hi_wi + f, r.wi.at[f, wi_rows(y * 4 * U + lo * 2 * U + (1 - hi) * U, U)], r.wi3.at[f], to_hi
        )

    def pump_wb1(p):
        for e in range(2):
            f = 2 * p + e
            y_wb(f).wait()
            add_into(r.wb, (f, y), r.wb1[f])
        lo_wb(p).start()

    def pump_wi1(f):
        y_wi(f).wait()
        add_into(r.wi, (f, wi_rows(y * 4 * U, 4 * U), slice(None)), r.wi1[f])
        lo_wi(f).start()

    def pump_wb2():
        for p in range(2):
            lo_wb(p).wait()
            add_into(r.wb, (2 * p + lo, y), r.wb2[p])
        hi_wb().start()

    def pump_wi2(f):
        lo_wi(f).wait()
        add_into(r.wi, (f, wi_rows(y * 4 * U + lo * 2 * U, 2 * U), slice(None)), r.wi2[f])
        hi_wi(f).start()

    GN = r.gq.shape[1]
    EB = J // 8

    def st_rows(unit, stage):
        base = [0, lo * 4 * unit, lo * 4 * unit + y * 2 * unit][stage]
        n = [4, 2, 1][stage] * unit
        bit = [lo, y, hi][stage]
        return base + bit * n, base + (1 - bit) * n, n

    if fused:
        chain_o = (r.go, (r.go1, r.go2, r.go3), sl.go, U)
        chain_q = (r.gq, (r.gq1, r.gq2, r.gq3), sl.gq, U)
        chain_e = (r.ge, (r.ge1, r.ge2, r.ge3), sl.ge, EB)

    def st_copy(chain, stage):
        buf, got, slot, unit = chain
        _, sent, n = st_rows(unit, stage)
        dev = [to_lo, to_y, to_hi][stage]
        return rc(slot + stage, buf.at[pl.ds(pl.multiple_of(sent, 16), n)], got[stage], dev)

    def st_add(chain, stage):
        buf, got, _, unit = chain
        st_copy(chain, stage).wait()
        kept, _, n = st_rows(unit, stage)
        add_into(buf, (pl.ds(pl.multiple_of(kept, 16), n), slice(None)), got[stage][...])

    def st_last(chain):
        buf, got, _, unit = chain
        st_copy(chain, 2).wait()
        kept, _, n = st_rows(unit, 2)
        return buf[pl.ds(pl.multiple_of(kept, 16), n), :].astype(F32) + got[2][...].astype(F32)

    @pl.loop(0, T // NR)
    def _(i):
        rows = pl.ds(pl.multiple_of(i * NR, NR), NR)
        dn, xh = r.dacc[rows, :], r.xh2[rows, :]
        part = jnp.sum(dn * xh, axis=0, keepdims=True)

        @pl.when(i == 0)
        def _():
            r.gv[1:2, :] = part

        @pl.when(i > 0)
        def _():
            r.gv[1:2, :] += part

        dg = dn * gf
        m1 = jnp.sum(dg, axis=1, keepdims=True) * inv_d
        m2 = jnp.sum(dg * xh, axis=1, keepdims=True) * inv_d
        dmid = r.dyb[rows, :].astype(F32) + r.rs2[rows, 0:1] * (dg - m1 - xh * m2)
        r.dmid[rows, :] = dmid
        b = dmid.astype(BF)
        r.dmb[0, rows, :] = b[:, 0:HC]
        r.dmb[1, rows, :] = b[:, HC : 2 * HC]

    r.o_layer[...] = (r.mid[0:H, :] + r.oacc[...]).astype(BF)
    c_dm = rc(sl.c_dm, r.dmb.at[1 - c], r.dmr, to_core)
    c_dm.start()
    r.dctx[...] = (nt(r.dmb[0], r.wo[:, 0:HC]) + nt(r.dmb[1], r.wo[:, HC : 2 * HC])).astype(BF)
    c_ctt.wait()
    c_dm.wait()
    r.go[...] = (nn(r.ctt[0], r.dmb[c]) + nn(r.ctt[1], r.dmr[...])).astype(BF)
    if fused:
        st_copy(chain_o, 0).start()

    def c_ds(i):
        return rc(sl.c_ds + i, r.pd.at[i], r.pdr.at[i], to_core)

    @pl.loop(0, D // 128)
    def _(i):
        cols = pl.ds(pl.multiple_of(i * 128, 128), 128)
        q2, dc2, sv2 = r.q[:, cols], r.dctx[:, cols], r.sv[:, cols]
        dsv = None
        dsk = None
        for h in range(2):
            dch = dc2 * head_mask[h]
            ptb = r.pt[i, :, h * T : (h + 1) * T]
            dp = nt(sv2, dch)
            pf = ptb.astype(F32)
            ds = pf * (dp - jnp.sum(pf * dp, axis=0, keepdims=True))
            draw = (ds * scale).astype(BF)
            av = nn(ptb, dch)
            ak = nn(draw, q2 * head_mask[h])
            dsv = av if dsv is None else dsv + av
            dsk = ak if dsk is None else dsk + ak
            r.dqt[h * 64 : (h + 1) * 64, :] = nn(
                r.skt[pl.ds(pl.multiple_of(i * 128 + h * 64, 64), 64), :], draw
            ).astype(BF)
        r.pd[i, 0] = dsk.astype(BF)
        r.pd[i, 1] = dsv.astype(BF)
        c_ds(i).start()
        r.dq[:, cols] = nt(r.eye[...], r.dqt[...]).astype(BF)
        if fused:
            for f in range(2):
                @pl.when(i == 1 + 2 * f)
                def _():
                    pump_wi1(f)
            @pl.when(i == 4)
            def _():
                pump_wb1(0)

    @pl.loop(0, D // 128)
    def _(i):
        cols = pl.ds(pl.multiple_of(i * 128, 128), 128)
        c_ds(i).wait()
        r.dsk[:, cols] = (r.pd[i, 0].astype(F32) + r.pdr[i, 0].astype(F32)).astype(BF)
        r.dsv[:, cols] = (r.pd[i, 1].astype(F32) + r.pdr[i, 1].astype(F32)).astype(BF)

    def c_g(i):
        return rc(sl.c_g + i, r.dqkv.at[i, 1 - c], r.dqr.at[i], to_core)

    r.dqkv[0, 0] = r.dq[:, 0:HC]
    r.dqkv[0, 1] = r.dq[:, HC : 2 * HC]
    c_g(0).start()
    dk = nn(r.me[...], r.dsk[...]).astype(BF)
    r.dqkv[1, 0] = dk[:, 0:HC]
    r.dqkv[1, 1] = dk[:, HC : 2 * HC]
    c_g(1).start()
    dv = nn(r.me[...], r.dsv[...]).astype(BF)
    r.dqkv[2, 0] = dv[:, 0:HC]
    r.dqkv[2, 1] = dv[:, HC : 2 * HC]
    c_g(2).start()

    de = nt(r.dsk[...], r.k[0:H, :]) + nt(r.dsv[...], r.v[0:H, :])
    de = jnp.where(r.sel_t[:, 0:H] > 0.5, de, 0.0).astype(BF)
    for b in range(8):
        b2, b1, b0 = b // 4, (b // 2) % 2, b % 2
        j = 4 * b0 + 2 * b2 + b1
        r.ge[b * EB : (b + 1) * EB, :] = de[j * EB : (j + 1) * EB, :]

    for i, w in enumerate((r.wq, r.wk, r.wv)):
        for hf in range(2):
            part = nt(r.dqkv[i, hf], w[:, hf * HC : (hf + 1) * HC])
            if i == 0 and hf == 0:
                r.dacc[...] = part
            else:
                r.dacc[...] += part

    @pl.loop(0, T // NR)
    def _(i):
        rows = pl.ds(pl.multiple_of(i * NR, NR), NR)
        dn, xh = r.dacc[rows, :], r.xh1[rows, :]
        part = jnp.sum(dn * xh, axis=0, keepdims=True)

        @pl.when(i == 0)
        def _():
            r.gv[0:1, :] = part

        @pl.when(i > 0)
        def _():
            r.gv[0:1, :] += part

        @pl.when(i < H // NR)
        def _():
            dg = dn * ga
            m1 = jnp.sum(dg, axis=1, keepdims=True) * inv_d
            m2 = jnp.sum(dg * xh, axis=1, keepdims=True) * inv_d
            r.o_x[rows, :] = r.dmid[rows, :] + r.rs1[rows, 0:1] * (dg - m1 - xh * m2)

    gv = jnp.concatenate([r.gv[0:2, :], jnp.zeros((126, D), F32)], axis=0).astype(BF)
    r.gq[:, 3 * HC : GN] = nt(r.sb[...], gv).astype(BF)

    c_h1t.wait()
    for i in range(3):
        c_g(i).wait()
        r.gq[:, i * HC : (i + 1) * HC] = (
            nn(r.h1t[0], r.dqkv[i, c]) + nn(r.h1t[1], r.dqr[i])
        ).astype(BF)

    if not fused:
        return

    st_copy(chain_q, 0).start()
    st_copy(chain_e, 0).start()

    st_add(chain_o, 0)
    st_copy(chain_o, 1).start()
    pump_wi1(2)
    pump_wb1(1)
    pump_wi1(3)
    st_add(chain_q, 0)
    st_copy(chain_q, 1).start()
    st_add(chain_e, 0)
    st_copy(chain_e, 1).start()
    for f in range(NF):
        pump_wi2(f)
    pump_wb2()
    st_add(chain_o, 1)
    st_copy(chain_o, 2).start()
    st_add(chain_q, 1)
    st_copy(chain_q, 2).start()
    st_add(chain_e, 1)
    st_copy(chain_e, 2).start()

    fin = r.fin
    for f in range(NF):
        hi_wi(f).wait()
        own = r.wi[f, wi_rows(y * 4 * U + lo * 2 * U + hi * U, U), :]
        fin[:, f * HC : (f + 1) * HC] = own.astype(F32) + r.wi3[f].astype(F32)
    at = NF * HC
    fin[:, at : at + HC] = st_last(chain_o)
    fin[:, at + HC : at + HC + GN] = st_last(chain_q)
    at += HC + GN
    half = U // 2
    c_fin = rc(sl.c_fin, fin.at[pl.ds(pl.multiple_of((1 - c) * half, 8), half)], r.finr, to_core)
    c_fin.start()
    hi_wb().wait()
    r.o_back[...] = r.wb[2 * hi + lo, y].astype(F32) + r.wb3[...].astype(F32)
    r.o_e[...] = st_last(chain_e)
    c_fin.wait()
    mine = pl.ds(pl.multiple_of(c * half, 8), half)

    def put(dst, base, src_col):
        dst[:, pl.ds(pl.multiple_of(base + c * HC, 128), HC)] = fin[mine, src_col : src_col + HC]
        dst[:, pl.ds(pl.multiple_of(base + (1 - c) * HC, 128), HC)] = r.finr[:, src_col : src_col + HC]

    for f in range(NF):
        put(r.o_in, f * FC, f * HC)
    for i, dst in enumerate((r.o_out, r.o_q, r.o_k, r.o_v)):
        put(dst, 0, (NF + i) * HC)
    r.o_g[...] = fin[mine, at - 128 : at] + r.finr[:, at - 128 : at]


def run_layer(mesh_shape, tokens, seg_ids, slot_doc, proj_e, g_attn, w_query, w_key, w_value, w_out, g_ffn, w_in,
              w_back, cotangent):
    n_dp, n_seq = mesh_shape
    rows, H, D = tokens.shape
    J = proj_e.shape[1]
    FF = w_in.shape[1]
    fused = n_dp == 8
    T = 2 * H
    HC, U, NF, Q = D // 2, D // 16, FF // D, FF // 32
    EB = J // 8
    GN = 3 * HC + 128
    sel_a, sel_b, sel_c = (jnp.asarray(m, BF) for m in selections(D, FF))

    inputs = dict(
        x_in=(tokens.reshape(H, D), False),
        seg_in=(seg_ids.reshape(1, H), True),
        slot_in=(slot_doc.reshape(1, J), True),
        e_in=(proj_e, False),
        ga=(g_attn.reshape(1, D), True),
        wq_in=(w_query, False),
        wk_in=(w_key, False),
        wv_in=(w_value, False),
        wo_in=(w_out, False),
        gf=(g_ffn.reshape(1, D), True),
        w_in_in=(w_in, False),
        w_back_in=(w_back, False),
        dy_in=(cotangent.reshape(H, D), False),
        sa_in=(sel_a, False),
        sb_in=(sel_b, False),
        sc_in=(sel_c, False),
    )
    parts = dict(
        wb=((NF, 2, Q, D), BF),
        wi=((NF, D // 2, HC), BF),
        go=((D // 2, HC), BF),
        gq=((D // 2, GN), BF),
        ge=((J, H), BF),
    )
    outs = dict(o_layer=((H, D), BF), o_x=((H, D), F32))
    if fused:
        outs.update(
            o_g=((U // 2, 128), F32),
            o_q=((U // 2, D), F32),
            o_k=((U // 2, D), F32),
            o_v=((U // 2, D), F32),
            o_out=((U // 2, D), F32),
            o_in=((U // 2, FF), F32),
            o_back=((Q, D), F32),
            o_e=((EB, H), F32),
        )
    else:
        outs.update(parts)
    scratch = dict(
        xb=((T, D), BF), eb=((T, J), BF), segf=((2, 8, H), F32),
        wq=((D, D), BF), wk=((D, D), BF), wv=((D, D), BF), wo=((D, D), BF),
        w_in=((D, FF), BF), w_back=((FF, D), BF),
        dyb=((T, D), BF), dyo=((T, D), BF),
        sa=((D // 2, D), BF), sb=((D // 2, D), BF), sc=((2, 2 * Q, FF // 4), BF),
        eye=((T, T), BF),
        h1=((T, D), BF), xh1=((T, D), F32), rs1=((T, 128), F32),
        q=((T, D), BF), k=((T, D), BF), v=((T, D), BF),
        sel_t=((J, T), F32), me=((T, J), BF), met=((J, T), BF),
        pk=((2, J, D), BF), pkr=((2, J, D), BF), sk=((J, D), BF), sv=((J, D), BF),
        skt=((D, J), BF), svt=((128, J), BF),
        pt=((D // 128, J, 2 * T), BF), ctxt=((D, T), BF), ctx=((T, D), BF),
        mid=((T, D), F32), xh2=((T, D), F32), rs2=((T, 128), F32), h2=((T, D), BF),
        h1t=((2, D // 2, T), BF), h2t=((2, D // 2, T), BF), ctt=((2, D // 2, T), BF),
        a=((T, D), BF), duf=((T, D), BF), du=((NF, 2, T, HC), BF), dur=((NF, T, HC), BF),
        at=((NF, 2, 2 * Q, T), BF), atr=((NF, 2 * Q, T), BF),
        oacc=((H, D), F32), dacc=((T, D), F32), dmid=((T, D), F32), gv=((8, D), F32),
        dmb=((2, T, HC), BF), dmr=((T, HC), BF), dctx=((T, D), BF),
        dqt=((128, T), BF), dq=((T, D), BF),
        pd=((D // 128, 2, J, 128), BF), pdr=((D // 128, 2, J, 128), BF),
        dsk=((J, D), BF), dsv=((J, D), BF),
        dqkv=((3, 2, T, HC), BF), dqr=((3, T, HC), BF),
    )
    if fused:
        scratch.update(
            parts,
            wb1=((NF, Q, D), BF), wb2=((2, Q, D), BF), wb3=((Q, D), BF),
            wi1=((NF, 4 * U, HC), BF), wi2=((NF, 2 * U, HC), BF), wi3=((NF, U, HC), BF),
            go1=((4 * U, HC), BF), go2=((2 * U, HC), BF), go3=((U, HC), BF),
            gq1=((4 * U, GN), BF), gq2=((2 * U, GN), BF), gq3=((U, GN), BF),
            ge1=((4 * EB, H), BF), ge2=((2 * EB, H), BF), ge3=((EB, H), BF),
            fin=((U, NF * HC + HC + GN), F32), finr=((U // 2, NF * HC + HC + GN), F32),
        )
    counts = dict(
        x_seg=1, x_e=1, x_x=1, x_dy=1, c_pk=1, c_pv=1, c_h1t=1, c_h2t=1, c_dy=1, c_ctt=1, c_at=NF, c_du=NF, c_dm=1,
        c_ds=D // 128, c_g=3, y_wb=NF, y_wi=NF, lo_wb=2, lo_wi=NF, hi_wb=1, hi_wi=NF, go=3, gq=3, ge=3, c_fin=1,
    )
    sl, count = SimpleNamespace(), 0
    for name, n in counts.items():
        setattr(sl, name, count)
        count += n
    names = [*inputs, *outs, *scratch]

    def body(*refs):
        r = SimpleNamespace(**dict(zip(names, refs)))
        r.lsem, r.ssem, r.rsem = refs[len(names) :]
        layer_body(fused, r, sl)

    res = pl.pallas_call(
        body,
        out_shape=[jax.ShapeDtypeStruct(sh, dt) for sh, dt in outs.values()],
        in_specs=[pl.BlockSpec(memory_space=pltpu.VMEM if v else pl.ANY) for _, v in inputs.values()],
        out_specs=[pl.BlockSpec(memory_space=pltpu.VMEM) for _ in outs],
        scratch_shapes=[pltpu.VMEM(sh, dt) for sh, dt in scratch.values()]
        + [pltpu.SemaphoreType.DMA((13,)), pltpu.SemaphoreType.DMA((count,)), pltpu.SemaphoreType.DMA((count,))],
        compiler_params=pltpu.CompilerParams(
            collective_id=0, has_side_effects=True, vmem_limit_bytes=60 * 1024 * 1024
        ),
        cost_estimate=pl.CostEstimate(flops=12 * 10**9, bytes_accessed=24 * 10**6, transcendentals=2 * 10**6),
    )(*[v for v, _ in inputs.values()])
    o = SimpleNamespace(**dict(zip(outs, res)))
    layer = o.o_layer.reshape(rows, H, D)
    x_grad = o.o_x.reshape(rows, H, D)
    if fused:
        return (
            layer, x_grad, o.o_g[:, 0], o.o_q, o.o_k, o.o_v, o.o_out, o.o_g[:, 1], o.o_in, o.o_back, o.o_e.T,
        )

    s = lax.axis_index(SEQ)
    x, c = s // 2, s % 2
    both = (DP, SEQ)

    def scatter(v):
        return lax.psum_scatter(v, both, scatter_dimension=0, tiled=True)

    def rows_back(v, y_first):
        v = v.astype(F32).reshape(2, 2, 2, U, v.shape[-1])
        v = v.transpose(2, 1, 0, 3, 4) if y_first else v.transpose(2, 0, 1, 3, 4)
        return v.reshape(8, U, v.shape[-1])

    def whole(v, y_first):
        v = rows_back(v, y_first)
        full = jnp.zeros((8, 2, U, 2, HC), F32)
        full = lax.dynamic_update_slice(full, v[:, None, :, None, :], (0, x, 0, c, 0))
        return full.reshape(D, 2 * HC)

    wi = jnp.stack([whole(o.wi[f], True) for f in range(NF)], axis=1).reshape(D, FF)
    wo = whole(o.go, False)
    wqkv = [whole(o.gq[:, i * HC : (i + 1) * HC], False) for i in range(3)]
    gains = rows_back(o.gq[:, 3 * HC :], False)
    gfull = lax.dynamic_update_slice(jnp.zeros((8, 2, U, 128), F32), gains[:, None], (0, x, 0, 0)).reshape(D, 128)
    wb = o.wb.astype(F32).reshape(NF * 2, 1, Q, D)
    wb = lax.dynamic_update_slice(jnp.zeros((NF * 2, 4, Q, D), F32), wb, (0, s, 0, 0)).reshape(FF, D)
    ge = o.ge.astype(F32).reshape(2, 2, 2, EB, H).transpose(2, 0, 1, 3, 4).reshape(J, H).T
    return (
        layer, x_grad, scatter(gfull[:, 0]), scatter(wqkv[0]), scatter(wqkv[1]), scatter(wqkv[2]), scatter(wo),
        scatter(gfull[:, 1]), scatter(wi), scatter(wb), lax.psum_scatter(ge, DP, scatter_dimension=1, tiled=True),
    )


def solution(mesh):
    shape = (mesh.shape[DP], mesh.shape[SEQ])
    both = (DP, SEQ)
    in_specs = (
        P(DP, SEQ, None), P(DP, SEQ), P(DP, None), P(SEQ, None),
        P(), P(), P(), P(), P(), P(), P(), P(), P(DP, SEQ, None),
    )
    out_specs = (
        P(DP, SEQ, None), P(DP, SEQ, None), P(both), P(both, None), P(both, None), P(both, None),
        P(both, None), P(both), P(both, None), P(both, None), P(SEQ, DP),
    )
    return jax.shard_map(
        functools.partial(run_layer, shape), mesh=mesh, in_specs=in_specs, out_specs=out_specs, check_vma=False
    )
```

```python
import functools
from types import SimpleNamespace

import jax
import jax.numpy as jnp
import numpy as np
from jax import lax
from jax.experimental import pallas as pl
from jax.experimental.pallas import tpu as pltpu
from jax.sharding import PartitionSpec as P

HEAD_DIM = 64
DP, SEQ = "dp", "seq"
YLH, LYH = "ylh", "lyh"
BF = jnp.bfloat16
F32 = jnp.float32
MESH = pl.DeviceIdType.MESH
GELU_C = 0.7978845608028654
GELU_K = 0.044715


def nn(a, b):
    return lax.dot_general(a, b, (((1,), (0,)), ((), ())), preferred_element_type=F32)


def tn(a, b):
    return lax.dot_general(a, b, (((0,), (0,)), ((), ())), preferred_element_type=F32)


def nt(a, b):
    return lax.dot_general(a, b, (((1,), (1,)), ((), ())), preferred_element_type=F32)


def selections(d_model, ff):
    unit = d_model // 16
    sel_a = np.zeros((2, d_model // 2, d_model), np.float32)
    for x in range(2):
        for b in range(8):
            j = 4 * (b % 2) + 2 * ((b // 2) % 2) + b // 4
            for o in range(unit):
                sel_a[x, b * unit + o, (2 * j + x) * unit + o] = 1
    q = ff // 32
    sel_c = np.zeros((2, 2, 2 * q, ff // 4), np.float32)
    for x in range(2):
        for c in range(2):
            for y in range(2):
                for o in range(q):
                    sel_c[x, c, y * q + o, (y * 4 + x * 2 + c) * q + o] = 1
    return sel_a, sel_c


def layer_body(fused, r, sl):
    d, s = lax.axis_index(DP), lax.axis_index(SEQ)
    x, c = s // 2, s % 2
    y, lo, hi = d % 2, (d // 2) % 2, d // 4
    to_core = (d, s + 1 - 2 * c)
    to_x = (d, s + 2 - 4 * x)
    to_y = (d + 1 - 2 * y, s)
    to_lo = (d + 2 - 4 * lo, s)
    to_hi = (d + 4 - 8 * hi, s)
    lsem, ssem, rsem = r.lsem, r.ssem, r.rsem
    D = r.h1.shape[1]
    T = r.h1.shape[0]
    H = T // 2
    J = r.sk.shape[0]
    FC = D
    NF = r.w_in.shape[1] // FC
    HC = D // 2
    U = D // 16
    Q = r.wb.shape[2]
    scale = HEAD_DIM ** (-0.5)

    loads = []

    def load(src, dst):
        cp = pltpu.make_async_copy(src, dst, lsem.at[len(loads)])
        loads.append(cp)
        cp.start()
        return cp

    def rc(i, src, dst, dev):
        return pltpu.make_async_remote_copy(
            src_ref=src, dst_ref=dst, send_sem=ssem.at[i], recv_sem=rsem.at[i], device_id=dev, device_id_type=MESH
        )

    l_x = load(r.x_in, r.xb.at[pl.ds(0, H)])
    l_e = load(r.e_in, r.eb.at[pl.ds(0, H)])
    l_wq = load(r.wq_in, r.wq)
    l_wk = load(r.wk_in, r.wk)
    l_wv = load(r.wv_in, r.wv)
    l_dy = load(r.dy_in, r.dyb.at[pl.ds(0, H)])
    l_sa = load(r.sa_in.at[x], r.sa)
    l_wo = load(r.wo_in, r.wo)
    l_sc0 = load(r.sc_in.at[x, c], r.sc.at[pl.ds(0, 2 * Q)])
    l_sc1 = load(r.sc_in.at[x, 1 - c], r.sc.at[pl.ds(2 * Q, 2 * Q)])
    l_w_in = load(r.w_in_in, r.w_in)
    l_w_back = load(r.w_back_in, r.w_back)

    partners = [to_core, to_x] + ([to_y, to_lo, to_hi] if fused else [])
    barrier = pltpu.get_barrier_semaphore()
    for dev in partners:
        pl.semaphore_signal(barrier, inc=1, device_id=dev, device_id_type=MESH)
    r.segf[0] = jnp.broadcast_to(r.seg_in[...].astype(F32), (8, H))
    pl.semaphore_wait(barrier, len(partners))

    x_seg = rc(sl.x_seg, r.segf.at[0], r.segf.at[1], to_x)
    x_e = rc(sl.x_e, r.e_in, r.eb.at[pl.ds(H, H)], to_x)
    x_x = rc(sl.x_x, r.x_in, r.xb.at[pl.ds(H, H)], to_x)
    x_dy = rc(sl.x_dy, r.dy_in, r.dyb.at[pl.ds(H, H)], to_x)
    x_x.start()

    rows_i = lax.broadcasted_iota(jnp.int32, (T, T), 0)
    cols_i = lax.broadcasted_iota(jnp.int32, (T, T), 1)
    eye = jnp.where(rows_i == cols_i, 1.0, 0.0).astype(BF)
    r.eye[...] = eye
    ga = r.ga[...].astype(F32).reshape(1, D)
    gf = r.gf[...].astype(F32).reshape(1, D)
    inv_d = 1.0 / D
    NR = 64

    def norm_rows(v):
        cen = v - jnp.sum(v, axis=1, keepdims=True) * inv_d
        rstd = lax.rsqrt(jnp.sum(cen * cen, axis=1, keepdims=True) * inv_d + 1e-5)
        return cen * rstd, rstd

    def norm_into(src, gain, xh_ref, rs_ref, h_ref, start, count):
        for i in range(start // NR, (start + count) // NR):
            rows = slice(i * NR, (i + 1) * NR)
            xh, rstd = norm_rows(src[rows, :].astype(F32))
            xh_ref[rows, :] = xh
            rs_ref[rows, :] = jnp.broadcast_to(rstd, (NR, 128))
            h_ref[rows, :] = (xh * gain).astype(BF)

    l_x.wait()
    norm_into(r.xb, ga, r.xh1, r.rs1, r.h1, 0, H)
    x_seg.start()
    x_e.start()
    slot_row = r.slot_in[...].astype(F32)
    slot_col = nt(eye, jnp.broadcast_to(slot_row, (T, J)).astype(BF))
    l_wq.wait()
    l_wk.wait()
    l_wv.wait()
    own, far = slice(0, H), slice(H, T)
    r.k[own, :] = nn(r.h1[own, :], r.wk[...]).astype(BF)
    r.v[own, :] = nn(r.h1[own, :], r.wv[...]).astype(BF)
    r.q[own, :] = nn(r.h1[own, :], r.wq[...]).astype(BF)
    l_e.wait()
    l_sa.wait()
    x_x.wait()
    x_dy.start()
    norm_into(r.xb, ga, r.xh1, r.rs1, r.h1, H, H)
    r.k[far, :] = nn(r.h1[far, :], r.wk[...]).astype(BF)

    x_seg.wait()
    x_e.wait()
    seg_row = jnp.concatenate([r.segf[0, 0:1, :], r.segf[1, 0:1, :]], axis=1)
    seg_col = nt(eye, jnp.broadcast_to(seg_row, (J, T)).astype(BF))
    r.sel_t[...] = jnp.where(slot_col == seg_row, 1.0, 0.0)
    r.me[...] = jnp.where(seg_col == slot_row, r.eb[...].astype(F32), 0.0).astype(BF)
    r.met[...] = nt(eye, r.me[...]).astype(BF)

    c_pk = rc(sl.c_pk, r.pk.at[0], r.pkr.at[0], to_core)
    c_pv = rc(sl.c_pv, r.pk.at[1], r.pkr.at[1], to_core)
    r.pk[0] = nn(r.met[...], r.k[...]).astype(BF)
    c_pk.start()
    r.v[far, :] = nn(r.h1[far, :], r.wv[...]).astype(BF)
    r.pk[1] = nn(r.met[...], r.v[...]).astype(BF)
    c_pv.start()
    r.q[far, :] = nn(r.h1[far, :], r.wq[...]).astype(BF)
    r.h1t[0] = nt(r.sa[...], r.h1[...]).astype(BF)
    c_h1t = rc(sl.c_h1t, r.h1t.at[0], r.h1t.at[1], to_core)
    c_pk.wait()
    r.sk[...] = (r.pk[0].astype(F32) + r.pkr[0].astype(F32)).astype(BF)
    c_pv.wait()
    r.sv[...] = (r.pk[1].astype(F32) + r.pkr[1].astype(F32)).astype(BF)
    c_h1t.start()

    lane = lax.broadcasted_iota(jnp.int32, (T, 128), 1)
    head_mask = [jnp.where(lane < 64, 1.0, 0.0).astype(BF), jnp.where(lane < 64, 0.0, 1.0).astype(BF)]

    NP = D // 128

    def fwd_raw(i):
        cols = slice(i * 128, (i + 1) * 128)
        q2 = r.q[:, cols]
        return nt(r.sk[:, cols], jnp.concatenate([q2 * head_mask[0], q2 * head_mask[1]], axis=0))

    def fwd_soft(i, raw):
        for m in range(2 * T // 128):
            h, tc = m * 128 // T, slice(m * 128 % T, m * 128 % T + 128)
            sc = jnp.where(r.sel_t[:, tc] > 0.5, raw[:, m * 128 : (m + 1) * 128] * scale, -1e30)
            e = jnp.exp(sc - jnp.max(sc, axis=0, keepdims=True))
            r.pt[i, h * J : (h + 1) * J, tc] = (e * (1.0 / jnp.sum(e, axis=0, keepdims=True))).astype(BF)

    def fwd_ctx(i):
        cols = slice(i * 128, (i + 1) * 128)
        sv2 = r.sv[:, cols]
        stack = jnp.concatenate([sv2 * head_mask[0], sv2 * head_mask[1]], axis=0)
        r.ctx[:, cols] = tn(r.pt[i], stack).astype(BF)

    raw = fwd_raw(0)
    for i in range(NP):
        nxt = fwd_raw(i + 1) if i + 1 < NP else None
        fwd_soft(i, raw)
        if i > 0:
            fwd_ctx(i - 1)
        raw = nxt
    fwd_ctx(NP - 1)

    l_wo.wait()
    r.mid[...] = r.xb[...].astype(F32) + nn(r.ctx[...], r.wo[...])
    norm_into(r.mid, gf, r.xh2, r.rs2, r.h2, 0, T)
    x_dy.wait()
    l_dy.wait()
    c_dy = rc(sl.c_dy, r.dyb, r.dyo, to_core)
    c_dy.start()
    l_w_in.wait()
    l_w_back.wait()
    l_sc0.wait()
    l_sc1.wait()
    c_h2t = rc(sl.c_h2t, r.h2t.at[0], r.h2t.at[1], to_core)
    c_ctt = rc(sl.c_ctt, r.ctt.at[0], r.ctt.at[1], to_core)

    def c_at(f):
        return rc(sl.c_at + f, r.at.at[f, pl.ds(2 * Q, 2 * Q)], r.atr.at[f], to_core)

    def c_du(f):
        return rc(sl.c_du + f, r.du.at[f, 1 - c], r.dur.at[f], to_core)

    def y_wb(k):
        return rc(sl.y_wb + k, r.wb.at[k, 1 - y], r.wb1.at[k], to_y)

    bits = dict(y=(y, to_y), l=(lo, to_lo), h=(hi, to_hi))

    def span(order, unit, stage):
        start, n = 0, 4 * unit
        for i in range(stage + 1):
            bit = bits[order[i]][0]
            kept, sent = start + bit * n, start + (1 - bit) * n
            if i < stage:
                start, n = kept, n // 2
        return kept, sent, n

    def rows16(start, n):
        return pl.ds(pl.multiple_of(start, 16), n)

    GN = HC + 128
    EB = J // 8
    if fused:
        chain_w = [
            (LYH if k % 2 == 0 else YLH, r.wi.at[k], (r.wi1.at[k], r.wi2.at[k], r.wi3.at[k]), sl.wi + 3 * k, U)
            for k in range(NF)
        ]
        chain_o = (YLH, r.go, (r.go1, r.go2, r.go3), sl.go, U)
        chain_q = (LYH, r.gq, (r.gq1, r.gq2, r.gq3), sl.gq, U)
        chain_k = (YLH, r.gk, (r.gk1, r.gk2, r.gk3), sl.gk, U)
        chain_v = (YLH, r.gv, (r.gv1, r.gv2, r.gv3), sl.gv, U)
        chain_e = (LYH, r.ge, (r.ge1, r.ge2, r.ge3), sl.ge, EB)

    def add_into(dst, idx, src):
        dst[idx] = (dst[idx].astype(F32) + src.astype(F32)).astype(BF)

    def lo_wb(p):
        return rc(sl.lo_wb + p, r.wb.at[2 * p + 1 - lo, y], r.wb2.at[p], to_lo)

    def hi_wb():
        return rc(sl.hi_wb, r.wb.at[2 * (1 - hi) + lo, y], r.wb3, to_hi)

    def pump_wb(k):
        if k < 4:
            y_wb(k).wait()
            add_into(r.wb, (k, y), r.wb1[k])

            @pl.when(lo == 1 - k % 2)
            def _():
                lo_wb(k // 2).start()
        else:
            p = k - 4
            lo_wb(p).wait()
            add_into(r.wb, (2 * p + lo, y), r.wb2[p])

            @pl.when(hi == 1 - p)
            def _():
                hi_wb().start()

    def pump(steps):
        for step in steps:
            if step[0] is None:
                pump_wb(step[1])
            else:
                st_next(step[0], step[1])

    def st_copy(chain, stage):
        order, buf, got, slot, unit = chain
        _, sent, n = span(order, unit, stage)
        return rc(slot + stage, buf.at[rows16(sent, n)], got[stage], bits[order[stage]][1])

    def st_next(chain, stage):
        order, buf, got, _, unit = chain
        st_copy(chain, stage).wait()
        kept, _, n = span(order, unit, stage)
        add_into(buf, (rows16(kept, n), slice(None)), got[stage][...])
        st_copy(chain, stage + 1).start()

    def st_last(chain):
        order, buf, got, _, unit = chain
        st_copy(chain, 2).wait()
        kept, _, n = span(order, unit, 2)
        return buf[rows16(kept, n), :].astype(F32) + got[2][...].astype(F32)

    def swap_rows(buf, cols, val, unit):
        q = 2 * unit
        for b in range(4):
            to = (b % 2) * 2 + b // 2
            buf[to * q : (to + 1) * q, cols] = val[b * q : (b + 1) * q, :].astype(BF)

    SB = 256
    GR = 32

    if fused:
        b0, b1, b2, b3, b4, b5 = [(None, k) for k in range(6)]
        w0, w1, w2, w3 = chain_w
        FFN_PUMPS = [[], [], [b0], [(w0, 0)]]
        MID_PUMPS = [[b1], [(w1, 0)]]
        ATT_PUMPS = [[], [b2, b4], [(w0, 1)], [(w2, 0)], [], [b3]]
        END_PUMPS = [(w1, 1), (w2, 1), (w3, 0), b5, (chain_q, 0), (chain_e, 0), (w3, 1), (chain_o, 0), (chain_q, 1),
                     (chain_e, 1), (chain_o, 1), (chain_k, 0), (chain_v, 0), (chain_k, 1), (chain_v, 1)]

    def swapped(buf, val, order, unit):
        if order == YLH:
            buf[...] = val.astype(BF)
        else:
            swap_rows(buf, slice(0, val.shape[1]), val, unit)

    def grad_wi(k):
        c_du(k).wait()
        val = nn(r.h2t[0], r.du[k, c]) + nn(r.h2t[1], r.dur[k])
        if not fused:
            r.wi[k] = val.astype(BF)
            return
        swapped(chain_w[k][1], val, chain_w[k][0], U)
        st_copy(chain_w[k], 0).start()

    for k in range(NF):
        for b in range(FC // SB):
            off = k * FC + b * SB
            u = nn(r.h2[...], r.w_in[:, off : off + SB])
            g = nt(r.dyb[...], r.w_back[off : off + SB, :])
            for m in range(T // GR):
                rr = slice(m * GR, (m + 1) * GR)
                um = u[rr, :]
                u2 = um * um
                th = jnp.tanh(um * (GELU_C + (GELU_C * GELU_K) * u2))
                half = 0.5 + 0.5 * th
                r.a[rr, b * SB : (b + 1) * SB] = (um * half).astype(BF)
                slope = half + (um * half) * ((1.0 - th) * (GELU_C + (3.0 * GELU_C * GELU_K) * u2))
                r.duf[rr, b * SB : (b + 1) * SB] = (slope * g[rr, :]).astype(BF)
        r.at[k] = nt(r.sc[...], r.a[...]).astype(BF)
        c_at(k).start()
        r.du[k, 0] = r.duf[:, 0:HC]
        r.du[k, 1] = r.duf[:, HC : 2 * HC]
        c_du(k).start()
        if k == 0:
            r.h2t[0] = nt(r.sa[...], r.h2[...]).astype(BF)
            c_h2t.start()
            c_dy.wait()
        if k == 1:
            c_h2t.wait()
        if k > 0:
            grad_wi(k - 1)
        else:
            r.ctt[0] = nt(r.sa[...], r.ctx[...]).astype(BF)
            c_ctt.start()
        c_at(k).wait()
        wb = nn(r.at[k, 0 : 2 * Q, :], r.dyb[...]) + nn(r.atr[k], r.dyo[...])
        r.wb[k, 0] = wb[0:Q, :].astype(BF)
        r.wb[k, 1] = wb[Q : 2 * Q, :].astype(BF)
        if fused:
            y_wb(k).start()
        rows = slice(k * FC, (k + 1) * FC)
        part_d = nt(r.duf[...], r.w_in[:, rows])
        part_o = nn(r.a[0:H, :], r.w_back[rows, :])
        if k == 0:
            r.oacc[...] = part_o
            r.dacc[...] = part_d
        else:
            r.oacc[...] += part_o
            r.dacc[...] += part_d
        if fused:
            pump(FFN_PUMPS[k])
    grad_wi(NF - 1)

    if fused:
        pump(MID_PUMPS[0])
    gsum = None
    for i in range(T // NR):
        rows = slice(i * NR, (i + 1) * NR)
        dn, xh = r.dacc[rows, :], r.xh2[rows, :]
        part = jnp.sum(dn * xh, axis=0, keepdims=True)
        gsum = part if gsum is None else gsum + part
        dg = dn * gf
        m1 = jnp.sum(dg, axis=1, keepdims=True) * inv_d
        m2 = jnp.sum(dg * xh, axis=1, keepdims=True) * inv_d
        dmid = r.dyb[rows, :].astype(F32) + r.rs2[rows, 0:1] * (dg - m1 - xh * m2)
        r.dmid[rows, :] = dmid
        b = dmid.astype(BF)
        r.dmb[0, rows, :] = b[:, 0:HC]
        r.dmb[1, rows, :] = b[:, HC : 2 * HC]
    r.gvec[1:2, :] = gsum
    c_dm = rc(sl.c_dm, r.dmb.at[1 - c], r.dmr, to_core)
    c_dm.start()
    r.dctx[...] = (nt(r.dmb[0], r.wo[:, 0:HC]) + nt(r.dmb[1], r.wo[:, HC : 2 * HC])).astype(BF)
    r.o_layer[...] = (r.mid[0:H, :] + r.oacc[...]).astype(BF)
    if fused:
        pump(MID_PUMPS[1])

    def c_ds(i):
        return rc(sl.c_ds + i, r.pd.at[i], r.pdr.at[i], to_core)

    def bwd_dp(i):
        cols = slice(i * 128, (i + 1) * 128)
        dc2 = r.dctx[:, cols]
        return nt(r.sv[:, cols], jnp.concatenate([dc2 * head_mask[0], dc2 * head_mask[1]], axis=0))

    def bwd_soft(i, dpf):
        for m in range(2 * T // 128):
            h, tc = m * 128 // T, slice(m * 128 % T, m * 128 % T + 128)
            pf = r.pt[i, h * J : (h + 1) * J, tc].astype(F32)
            dp = dpf[:, m * 128 : (m + 1) * 128]
            ds = pf * (dp - jnp.sum(pf * dp, axis=0, keepdims=True))
            r.draw[i % 2, h * J : (h + 1) * J, tc] = (ds * scale).astype(BF)

    def bwd_out(i):
        cols = slice(i * 128, (i + 1) * 128)
        q2, dc2, sk2 = r.q[:, cols], r.dctx[:, cols], r.sk[:, cols]
        draw = r.draw[i % 2]
        dsv = nn(r.pt[i, 0:J], dc2 * head_mask[0]) + nn(r.pt[i, J : 2 * J], dc2 * head_mask[1])
        dsk = nn(draw[0:J], q2 * head_mask[0]) + nn(draw[J : 2 * J], q2 * head_mask[1])
        r.pd[i, 0] = dsk.astype(BF)
        r.pd[i, 1] = dsv.astype(BF)
        c_ds(i).start()
        stack = jnp.concatenate([sk2 * head_mask[0], sk2 * head_mask[1]], axis=0)
        r.dqkv[0, i // 3, :, (i % 3) * 128 : (i % 3 + 1) * 128] = tn(draw, stack).astype(BF)

    dpf = bwd_dp(0)
    for i in range(NP):
        nxt = bwd_dp(i + 1) if i + 1 < NP else None
        bwd_soft(i, dpf)
        if i > 0:
            bwd_out(i - 1)
        dpf = nxt
        if i == 0:
            c_ctt.wait()
            c_dm.wait()
            r.go[...] = (nn(r.ctt[0], r.dmb[c]) + nn(r.ctt[1], r.dmr[...])).astype(BF)
            if fused:
                st_copy(chain_o, 0).start()
        if fused:
            pump(ATT_PUMPS[i])
    bwd_out(NP - 1)

    def c_g(i):
        return rc(sl.c_g + i, r.dqkv.at[i, 1 - c], r.dqr.at[i], to_core)

    c_g(0).start()
    for i in range(D // 128):
        cols = slice(i * 128, (i + 1) * 128)
        c_ds(i).wait()
        r.dsk[:, cols] = (r.pd[i, 0].astype(F32) + r.pdr[i, 0].astype(F32)).astype(BF)
        r.dsv[:, cols] = (r.pd[i, 1].astype(F32) + r.pdr[i, 1].astype(F32)).astype(BF)

    dk = nn(r.me[...], r.dsk[...]).astype(BF)
    r.dqkv[1, 0] = dk[:, 0:HC]
    r.dqkv[1, 1] = dk[:, HC : 2 * HC]
    c_g(1).start()
    dv = nn(r.me[...], r.dsv[...]).astype(BF)
    r.dqkv[2, 0] = dv[:, 0:HC]
    r.dqkv[2, 1] = dv[:, HC : 2 * HC]
    c_g(2).start()

    def wgrad(i):
        c_g(i).wait()
        return nn(r.h1t[0], r.dqkv[i, c]) + nn(r.h1t[1], r.dqr[i])

    c_h1t.wait()
    swap_rows(r.gq, slice(0, HC), wgrad(0), U)
    if fused:
        st_copy(chain_q, 0).start()
    r.gk[...] = wgrad(1).astype(BF)
    if fused:
        st_copy(chain_k, 0).start()
    r.gv[:, 0:HC] = wgrad(2).astype(BF)

    acc = None
    for i, w in enumerate((r.wq, r.wk, r.wv)):
        for hf in range(2):
            part = nt(r.dqkv[i, hf], w[:, hf * HC : (hf + 1) * HC])
            acc = part if acc is None else acc + part
    r.dacc[...] = acc

    gsum = None
    for i in range(T // NR):
        rows = slice(i * NR, (i + 1) * NR)
        dn, xh = r.dacc[rows, :], r.xh1[rows, :]
        part = jnp.sum(dn * xh, axis=0, keepdims=True)
        gsum = part if gsum is None else gsum + part
        if i < H // NR:
            dg = dn * ga
            m1 = jnp.sum(dg, axis=1, keepdims=True) * inv_d
            m2 = jnp.sum(dg * xh, axis=1, keepdims=True) * inv_d
            r.o_x[rows, :] = r.dmid[rows, :] + r.rs1[rows, 0:1] * (dg - m1 - xh * m2)
    r.gvec[0:1, :] = gsum
    gains = jnp.concatenate([r.gvec[0:2, :], jnp.zeros((126, D), F32)], axis=0).astype(BF)
    r.gv[:, HC:GN] = nt(r.sa[...], gains).astype(BF)
    if fused:
        st_copy(chain_v, 0).start()

    de = nt(r.dsk[...], r.k[0:H, :]) + nt(r.dsv[...], r.v[0:H, :])
    de = jnp.where(r.sel_t[:, 0:H] > 0.5, de, 0.0).astype(BF)
    for b in range(8):
        b2, b1, b0 = b // 4, (b // 2) % 2, b % 2
        j = 4 * b0 + 2 * b2 + b1
        r.ge[b * EB : (b + 1) * EB, :] = de[j * EB : (j + 1) * EB, :]

    if not fused:
        return

    st_copy(chain_e, 0).start()
    pump(END_PUMPS)

    fin = r.fin
    for k in range(NF):
        fin[:, k * HC : (k + 1) * HC] = st_last(chain_w[k])
    at = NF * HC
    for chain in (chain_o, chain_q, chain_v, chain_k):
        width = chain[1].shape[1]
        fin[:, at : at + width] = st_last(chain)
        at += width
    half = U // 2
    c_fin = rc(sl.c_fin, fin.at[pl.ds(pl.multiple_of((1 - c) * half, 8), half)], r.finr, to_core)
    c_fin.start()
    hi_wb().wait()
    r.o_back[...] = r.wb[2 * hi + lo, y].astype(F32) + r.wb3[...].astype(F32)
    r.o_e[...] = st_last(chain_e)
    c_fin.wait()
    mine = pl.ds(pl.multiple_of(c * half, 8), half)

    def put(dst, base, src_col):
        dst[:, pl.ds(pl.multiple_of(base + c * HC, 128), HC)] = fin[mine, src_col : src_col + HC]
        dst[:, pl.ds(pl.multiple_of(base + (1 - c) * HC, 128), HC)] = r.finr[:, src_col : src_col + HC]

    for k in range(NF):
        put(r.o_in, k * FC, k * HC)
    for dst, at in ((r.o_out, NF * HC), (r.o_q, (NF + 1) * HC), (r.o_v, (NF + 2) * HC), (r.o_k, (NF + 2) * HC + GN)):
        put(dst, 0, at)
    at = (NF + 3) * HC
    r.o_g[...] = fin[mine, at : at + 128] + r.finr[:, at : at + 128]


def hand_over(r, names):
    copies = []
    for i, (src, dst) in enumerate(names):
        cp = pltpu.make_async_copy(src, dst, r.sem.at[i])
        cp.start()
        copies.append(cp)
    g = jnp.concatenate([r.s_g[...], jnp.zeros((128 - r.s_g.shape[0], 128), F32)], axis=0).T
    n = r.s_g.shape[0]
    r.d_ga[...] = g[0, 0:n]
    r.d_gf[...] = g[1, 0:n]
    for cp in copies:
        cp.wait()


def run_layer(mesh_shape, tokens, seg_ids, slot_doc, proj_e, g_attn, w_query, w_key, w_value, w_out, g_ffn, w_in,
              w_back, cotangent):
    n_dp, n_seq = mesh_shape
    rows, H, D = tokens.shape
    J = proj_e.shape[1]
    FF = w_in.shape[1]
    fused = n_dp == 8
    T = 2 * H
    HC, U, NF, Q = D // 2, D // 16, FF // D, FF // 32
    EB = J // 8
    GN = HC + 128
    sel_a, sel_c = (jnp.asarray(m, BF) for m in selections(D, FF))

    inputs = dict(
        x_in=(tokens.reshape(H, D), False),
        seg_in=(seg_ids.reshape(1, H), True),
        slot_in=(slot_doc.reshape(1, J), True),
        e_in=(proj_e, False),
        ga=(g_attn, True),
        wq_in=(w_query, False),
        wk_in=(w_key, False),
        wv_in=(w_value, False),
        wo_in=(w_out, False),
        gf=(g_ffn, True),
        w_in_in=(w_in, False),
        w_back_in=(w_back, False),
        dy_in=(cotangent.reshape(H, D), False),
        sa_in=(sel_a, False),
        sc_in=(sel_c, False),
    )
    parts = dict(
        wb=((NF, 2, Q, D), BF),
        wi=((NF, D // 2, HC), BF),
        go=((D // 2, HC), BF),
        gq=((D // 2, HC), BF),
        gk=((D // 2, HC), BF),
        gv=((D // 2, GN), BF),
        ge=((J, H), BF),
    )
    outs = dict(o_layer=((H, D), BF), o_x=((H, D), F32))
    if fused:
        outs.update(
            o_g=((U // 2, 128), F32),
            o_q=((U // 2, D), F32),
            o_k=((U // 2, D), F32),
            o_v=((U // 2, D), F32),
            o_out=((U // 2, D), F32),
            o_in=((U // 2, FF), F32),
            o_back=((Q, D), F32),
            o_e=((EB, H), F32),
        )
    else:
        outs.update(parts)
    scratch = dict(
        xb=((T, D), BF), eb=((T, J), BF), segf=((2, 8, H), F32),
        wq=((D, D), BF), wk=((D, D), BF), wv=((D, D), BF), wo=((D, D), BF),
        w_in=((D, FF), BF), w_back=((FF, D), BF),
        dyb=((T, D), BF), dyo=((T, D), BF),
        sa=((D // 2, D), BF), sc=((4 * Q, FF // 4), BF),
        eye=((T, T), BF),
        h1=((T, D), BF), xh1=((T, D), F32), rs1=((T, 128), F32),
        q=((T, D), BF), k=((T, D), BF), v=((T, D), BF),
        sel_t=((J, T), F32), me=((T, J), BF), met=((J, T), BF),
        pk=((2, J, D), BF), pkr=((2, J, D), BF), sk=((J, D), BF), sv=((J, D), BF),

        pt=((D // 128, 2 * J, T), BF), ctx=((T, D), BF),
        mid=((T, D), F32), xh2=((T, D), F32), rs2=((T, 128), F32), h2=((T, D), BF),
        h1t=((2, D // 2, T), BF), h2t=((2, D // 2, T), BF), ctt=((2, D // 2, T), BF),
        a=((T, D), BF), duf=((T, D), BF), du=((NF, 2, T, HC), BF), dur=((NF, T, HC), BF),
        at=((NF, 4 * Q, T), BF), atr=((NF, 2 * Q, T), BF),
        oacc=((H, D), F32), dacc=((T, D), F32), dmid=((T, D), F32), gvec=((8, D), F32),
        dmb=((2, T, HC), BF), dmr=((T, HC), BF), dctx=((T, D), BF), draw=((2, 2 * J, T), BF),
        pd=((D // 128, 2, J, 128), BF), pdr=((D // 128, 2, J, 128), BF),
        dsk=((J, D), BF), dsv=((J, D), BF),
        dqkv=((3, 2, T, HC), BF), dqr=((3, T, HC), BF),
    )
    if fused:
        scratch.update(
            parts,
            wb1=((NF, Q, D), BF), wb2=((2, Q, D), BF), wb3=((Q, D), BF),
            wi1=((NF, 4 * U, HC), BF), wi2=((NF, 2 * U, HC), BF), wi3=((NF, U, HC), BF),
            go1=((4 * U, HC), BF), go2=((2 * U, HC), BF), go3=((U, HC), BF),
            gq1=((4 * U, HC), BF), gq2=((2 * U, HC), BF), gq3=((U, HC), BF),
            gk1=((4 * U, HC), BF), gk2=((2 * U, HC), BF), gk3=((U, HC), BF),
            gv1=((4 * U, GN), BF), gv2=((2 * U, GN), BF), gv3=((U, GN), BF),
            ge1=((4 * EB, H), BF), ge2=((2 * EB, H), BF), ge3=((EB, H), BF),
            fin=((U, NF * HC + 3 * HC + GN), F32), finr=((U // 2, NF * HC + 3 * HC + GN), F32),
        )
    counts = dict(
        x_seg=1, x_e=1, x_x=1, x_dy=1, c_pk=1, c_pv=1, c_h1t=1, c_h2t=1, c_dy=1, c_ctt=1, c_at=NF, c_du=NF, c_dm=1,
        c_ds=D // 128, c_g=3, y_wb=NF, wi=3 * NF, lo_wb=2, hi_wb=1, go=3, gq=3, gk=3, gv=3, ge=3, c_fin=1,
    )
    sl, count = SimpleNamespace(), 0
    for name, n in counts.items():
        setattr(sl, name, count)
        count += n
    names = [*inputs, *outs, *scratch]

    def body(*refs):
        r = SimpleNamespace(**dict(zip(names, refs)))
        r.lsem, r.ssem, r.rsem = refs[len(names) :]
        layer_body(fused, r, sl)

    res = pl.pallas_call(
        body,
        out_shape=[jax.ShapeDtypeStruct(sh, dt) for sh, dt in outs.values()],
        in_specs=[pl.BlockSpec(memory_space=pltpu.VMEM if v else pl.ANY) for _, v in inputs.values()],
        out_specs=[pl.BlockSpec(memory_space=pltpu.VMEM) for _ in outs],
        scratch_shapes=[pltpu.VMEM(sh, dt) for sh, dt in scratch.values()]
        + [pltpu.SemaphoreType.DMA((12,)), pltpu.SemaphoreType.DMA((count,)), pltpu.SemaphoreType.DMA((count,))],
        compiler_params=pltpu.CompilerParams(
            collective_id=0, has_side_effects=True, vmem_limit_bytes=60 * 1024 * 1024
        ),
        cost_estimate=pl.CostEstimate(flops=12 * 10**9, bytes_accessed=24 * 10**6, transcendentals=2 * 10**6),
    )(*[v for v, _ in inputs.values()])
    o = SimpleNamespace(**dict(zip(outs, res)))
    if fused:
        src = dict(s_layer=o.o_layer, s_x=o.o_x, s_q=o.o_q, s_k=o.o_k, s_v=o.o_v, s_out=o.o_out, s_in=o.o_in,
                   s_back=o.o_back, s_e=o.o_e, s_g=o.o_g)
        n_copy = len(src) - 1
        dst = dict(
            d_layer=((rows, H, D), BF), d_x=((rows, H, D), F32), d_q=((U // 2, D), F32), d_k=((U // 2, D), F32),
            d_v=((U // 2, D), F32), d_out=((U // 2, D), F32), d_in=((U // 2, FF), F32), d_back=((Q, D), F32),
            d_e=((EB, H), F32), d_ga=((U // 2,), F32), d_gf=((U // 2,), F32),
        )

        def tail(*refs):
            r = SimpleNamespace(**dict(zip([*src, *dst], refs)))
            r.sem = refs[-1]
            r.d_layer, r.d_x = r.d_layer.at[0], r.d_x.at[0]
            pairs = list(zip(vars(r).values(), list(vars(r).values())[len(src) :]))[:n_copy]
            hand_over(r, pairs)

        res = pl.pallas_call(
            tail,
            out_shape=[jax.ShapeDtypeStruct(sh, dt) for sh, dt in dst.values()],
            in_specs=[pl.BlockSpec(memory_space=pl.ANY)] * n_copy + [pl.BlockSpec(memory_space=pltpu.VMEM)],
            out_specs=[pl.BlockSpec(memory_space=pltpu.VMEM)] * len(dst),
            scratch_shapes=[pltpu.SemaphoreType.DMA((n_copy,))],
        )(*src.values())
        o = SimpleNamespace(**dict(zip(dst, res)))
        return o.d_layer, o.d_x, o.d_ga, o.d_q, o.d_k, o.d_v, o.d_out, o.d_gf, o.d_in, o.d_back, o.d_e.T

    layer = o.o_layer.reshape(rows, H, D)
    x_grad = o.o_x.reshape(rows, H, D)

    s = lax.axis_index(SEQ)
    x, c = s // 2, s % 2
    both = (DP, SEQ)

    def scatter(v):
        return lax.psum_scatter(v, both, scatter_dimension=0, tiled=True)

    def rows_back(v, y_first):
        v = v.astype(F32).reshape(2, 2, 2, U, v.shape[-1])
        v = v.transpose(2, 1, 0, 3, 4) if y_first else v.transpose(2, 0, 1, 3, 4)
        return v.reshape(8, U, v.shape[-1])

    def whole(v, y_first):
        v = rows_back(v, y_first)
        full = jnp.zeros((8, 2, U, 2, HC), F32)
        full = lax.dynamic_update_slice(full, v[:, None, :, None, :], (0, x, 0, c, 0))
        return full.reshape(D, 2 * HC)

    wi = jnp.stack([whole(o.wi[f], True) for f in range(NF)], axis=1).reshape(D, FF)
    wo = whole(o.go, True)
    wqkv = [whole(o.gq, False), whole(o.gk, True), whole(o.gv[:, :HC], True)]
    gains = rows_back(o.gv[:, HC:], True)
    gfull = lax.dynamic_update_slice(jnp.zeros((8, 2, U, 128), F32), gains[:, None], (0, x, 0, 0)).reshape(D, 128)
    wb = o.wb.astype(F32).reshape(NF * 2, 1, Q, D)
    wb = lax.dynamic_update_slice(jnp.zeros((NF * 2, 4, Q, D), F32), wb, (0, s, 0, 0)).reshape(FF, D)
    ge = o.ge.astype(F32).reshape(2, 2, 2, EB, H).transpose(2, 0, 1, 3, 4).reshape(J, H).T
    return (
        layer, x_grad, scatter(gfull[:, 0]), scatter(wqkv[0]), scatter(wqkv[1]), scatter(wqkv[2]), scatter(wo),
        scatter(gfull[:, 1]), scatter(wi), scatter(wb), lax.psum_scatter(ge, DP, scatter_dimension=1, tiled=True),
    )


def solution(mesh):
    shape = (mesh.shape[DP], mesh.shape[SEQ])
    both = (DP, SEQ)
    in_specs = (
        P(DP, SEQ, None), P(DP, SEQ), P(DP, None), P(SEQ, None),
        P(), P(), P(), P(), P(), P(), P(), P(), P(DP, SEQ, None),
    )
    out_specs = (
        P(DP, SEQ, None), P(DP, SEQ, None), P(both), P(both, None), P(both, None), P(both, None),
        P(both, None), P(both), P(both, None), P(both, None), P(SEQ, DP),
    )
    return jax.shard_map(
        functools.partial(run_layer, shape), mesh=mesh, in_specs=in_specs, out_specs=out_specs, check_vma=False
    )
```

```python
import functools
from types import SimpleNamespace

import jax
import jax.numpy as jnp
import numpy as np
from jax import lax
from jax.experimental import pallas as pl
from jax.experimental.pallas import tpu as pltpu
from jax.sharding import PartitionSpec as P

HEAD_DIM = 64
DP, SEQ = "dp", "seq"
YLH, LYH = "ylh", "lyh"
BF = jnp.bfloat16
F32 = jnp.float32
MESH = pl.DeviceIdType.MESH
GELU_C = 0.7978845608028654
GELU_K = 0.044715


def nn(a, b):
    return lax.dot_general(a, b, (((1,), (0,)), ((), ())), preferred_element_type=F32)


def tn(a, b):
    return lax.dot_general(a, b, (((0,), (0,)), ((), ())), preferred_element_type=F32)


def nt(a, b):
    return lax.dot_general(a, b, (((1,), (1,)), ((), ())), preferred_element_type=F32)


def selections(d_model, ff):
    unit = d_model // 16
    sel_a = np.zeros((2, d_model // 2, d_model), np.float32)
    for x in range(2):
        for b in range(8):
            j = 4 * (b % 2) + 2 * ((b // 2) % 2) + b // 4
            for o in range(unit):
                sel_a[x, b * unit + o, (2 * j + x) * unit + o] = 1
    q = ff // 32
    sel_c = np.zeros((2, 2, 2 * q, ff // 4), np.float32)
    for x in range(2):
        for c in range(2):
            for y in range(2):
                for o in range(q):
                    sel_c[x, c, y * q + o, (y * 4 + x * 2 + c) * q + o] = 1
    return sel_a, sel_c


def layer_body(fused, r, sl):
    d, s = lax.axis_index(DP), lax.axis_index(SEQ)
    x, c = s // 2, s % 2
    y, lo, hi = d % 2, (d // 2) % 2, d // 4
    to_core = (d, s + 1 - 2 * c)
    to_x = (d, s + 2 - 4 * x)
    to_y = (d + 1 - 2 * y, s)
    to_lo = (d + 2 - 4 * lo, s)
    to_hi = (d + 4 - 8 * hi, s)
    lsem, ssem, rsem = r.lsem, r.ssem, r.rsem
    D = r.h1.shape[1]
    T = r.h1.shape[0]
    H = T // 2
    J = r.sk.shape[0]
    FC = D
    NF = r.w_in.shape[1] // FC
    HC = D // 2
    U = D // 16
    Q = r.wb.shape[2]
    scale = HEAD_DIM ** (-0.5)

    loads = []

    def load(src, dst):
        cp = pltpu.make_async_copy(src, dst, lsem.at[len(loads)])
        loads.append(cp)
        cp.start()
        return cp

    def rc(i, src, dst, dev):
        return pltpu.make_async_remote_copy(
            src_ref=src, dst_ref=dst, send_sem=ssem.at[i], recv_sem=rsem.at[i], device_id=dev, device_id_type=MESH
        )

    partners = [to_core, to_x] + ([to_y, to_lo, to_hi] if fused else [])
    barrier = pltpu.get_barrier_semaphore()
    for dev in partners:
        pl.semaphore_signal(barrier, inc=1, device_id=dev, device_id_type=MESH)
    l_x = load(r.x_in, r.xb.at[pl.ds(0, H)])
    l_seg = load(r.seg_in, r.segs.at[0])
    l_slot = load(r.slot_in, r.slot)
    l_e = load(r.e_in, r.eb.at[pl.ds(0, H)])
    l_wq = load(r.wq_in, r.wq)
    l_wk = load(r.wk_in, r.wk)
    l_wv = load(r.wv_in, r.wv)
    l_dy = load(r.dy_in, r.dyb.at[pl.ds(0, H)])
    l_sa = load(r.sa_in.at[x], r.sa)
    l_wo = load(r.wo_in, r.wo)
    l_sc0 = load(r.sc_in.at[x, c], r.sc.at[pl.ds(0, 2 * Q)])
    l_sc1 = load(r.sc_in.at[x, 1 - c], r.sc.at[pl.ds(2 * Q, 2 * Q)])
    l_w_in = load(r.w_in_in, r.w_in)
    l_w_back = load(r.w_back_in, r.w_back)

    pl.semaphore_wait(barrier, len(partners))

    x_seg = rc(sl.x_seg, r.seg_in, r.segs.at[1], to_x)
    x_e = rc(sl.x_e, r.e_in, r.eb.at[pl.ds(H, H)], to_x)
    x_x = rc(sl.x_x, r.x_in, r.xb.at[pl.ds(H, H)], to_x)
    x_dy = rc(sl.x_dy, r.dy_in, r.dyb.at[pl.ds(H, H)], to_x)
    x_x.start()

    rows_i = lax.broadcasted_iota(jnp.int32, (T, T), 0)
    cols_i = lax.broadcasted_iota(jnp.int32, (T, T), 1)
    eye = jnp.where(rows_i == cols_i, 1.0, 0.0).astype(BF)
    r.eye[...] = eye
    ga = r.ga[...].astype(F32).reshape(1, D)
    gf = r.gf[...].astype(F32).reshape(1, D)
    inv_d = 1.0 / D
    NR = 64

    def norm_rows(v):
        cen = v - jnp.sum(v, axis=1, keepdims=True) * inv_d
        rstd = lax.rsqrt(jnp.sum(cen * cen, axis=1, keepdims=True) * inv_d + 1e-5)
        return cen * rstd, rstd

    def norm_into(src, gain, xh_ref, rs_ref, h_ref, start, count):
        for i in range(start // NR, (start + count) // NR):
            rows = slice(i * NR, (i + 1) * NR)
            xh, rstd = norm_rows(src[rows, :].astype(F32))
            xh_ref[rows, :] = xh
            rs_ref[rows, :] = jnp.broadcast_to(rstd, (NR, 128))
            h_ref[rows, :] = (xh * gain).astype(BF)

    l_x.wait()
    norm_into(r.xb, ga, r.xh1, r.rs1, r.h1, 0, H)
    x_seg.start()
    x_e.start()
    l_slot.wait()
    slot_row = r.slot[...].astype(F32)
    slot_col = nt(eye, jnp.broadcast_to(slot_row, (T, J)).astype(BF))
    l_wq.wait()
    l_wk.wait()
    l_wv.wait()
    own, far = slice(0, H), slice(H, T)
    r.k[own, :] = nn(r.h1[own, :], r.wk[...]).astype(BF)
    r.v[own, :] = nn(r.h1[own, :], r.wv[...]).astype(BF)
    r.q[own, :] = nn(r.h1[own, :], r.wq[...]).astype(BF)
    l_e.wait()
    l_sa.wait()
    x_x.wait()
    x_dy.start()
    norm_into(r.xb, ga, r.xh1, r.rs1, r.h1, H, H)
    r.k[far, :] = nn(r.h1[far, :], r.wk[...]).astype(BF)

    x_seg.wait()
    x_e.wait()
    l_seg.wait()
    seg_row = jnp.concatenate([r.segs[0], r.segs[1]], axis=1).astype(F32)
    seg_col = nt(eye, jnp.broadcast_to(seg_row, (J, T)).astype(BF))
    r.sel_t[...] = jnp.where(slot_col == seg_row, 1.0, 0.0)
    r.me[...] = jnp.where(seg_col == slot_row, r.eb[...].astype(F32), 0.0).astype(BF)
    r.met[...] = nt(eye, r.me[...]).astype(BF)

    c_pk = rc(sl.c_pk, r.pk.at[0], r.pkr.at[0], to_core)
    c_pv = rc(sl.c_pv, r.pk.at[1], r.pkr.at[1], to_core)
    r.pk[0] = nn(r.met[...], r.k[...]).astype(BF)
    c_pk.start()
    r.v[far, :] = nn(r.h1[far, :], r.wv[...]).astype(BF)
    r.pk[1] = nn(r.met[...], r.v[...]).astype(BF)
    c_pv.start()
    r.q[far, :] = nn(r.h1[far, :], r.wq[...]).astype(BF)
    c_h1t = rc(sl.c_h1t, r.h1t.at[0], r.h1t.at[1], to_core)

    lane = lax.broadcasted_iota(jnp.int32, (T, 128), 1)
    head_mask = [jnp.where(lane < 64, 1.0, 0.0).astype(BF), jnp.where(lane < 64, 0.0, 1.0).astype(BF)]

    NP = D // 128

    def fwd_raw(i):
        cols = slice(i * 128, (i + 1) * 128)
        q2 = r.q[:, cols]
        return nt(r.sk[:, cols], jnp.concatenate([q2 * head_mask[0], q2 * head_mask[1]], axis=0))

    def fwd_soft(i, raw):
        for m in range(2 * T // 128):
            h, tc = m * 128 // T, slice(m * 128 % T, m * 128 % T + 128)
            sc = jnp.where(r.sel_t[:, tc] > 0.5, raw[:, m * 128 : (m + 1) * 128] * scale, -1e30)
            e = jnp.exp(sc - jnp.max(sc, axis=0, keepdims=True))
            r.pt[i, h * J : (h + 1) * J, tc] = (e * (1.0 / jnp.sum(e, axis=0, keepdims=True))).astype(BF)

    def fwd_ctx(i):
        cols = slice(i * 128, (i + 1) * 128)
        sv2 = r.sv[:, cols]
        stack = jnp.concatenate([sv2 * head_mask[0], sv2 * head_mask[1]], axis=0)
        r.ctx[:, cols] = tn(r.pt[i], stack).astype(BF)

    c_pk.wait()
    r.sk[...] = (r.pk[0].astype(F32) + r.pkr[0].astype(F32)).astype(BF)
    raw = fwd_raw(0)
    for i in range(NP):
        nxt = fwd_raw(i + 1) if i + 1 < NP else None
        fwd_soft(i, raw)
        if i == 0:
            c_pv.wait()
            r.sv[...] = (r.pk[1].astype(F32) + r.pkr[1].astype(F32)).astype(BF)
        if i > 0:
            fwd_ctx(i - 1)
        raw = nxt
    fwd_ctx(NP - 1)

    l_wo.wait()
    r.mid[...] = r.xb[...].astype(F32) + nn(r.ctx[...], r.wo[...])
    norm_into(r.mid, gf, r.xh2, r.rs2, r.h2, 0, T)
    x_dy.wait()
    l_dy.wait()
    c_dy = rc(sl.c_dy, r.dyb, r.dyo, to_core)
    c_dy.start()
    l_w_in.wait()
    l_w_back.wait()
    l_sc0.wait()
    l_sc1.wait()
    c_h2t = rc(sl.c_h2t, r.h2t.at[0], r.h2t.at[1], to_core)
    c_ctt = rc(sl.c_ctt, r.ctt.at[0], r.ctt.at[1], to_core)

    def c_at(f):
        return rc(sl.c_at + f, r.at.at[f, pl.ds(2 * Q, 2 * Q)], r.atr.at[f], to_core)

    def c_du(f):
        return rc(sl.c_du + f, r.du.at[f, 1 - c], r.dur.at[f], to_core)

    def y_wb(k):
        return rc(sl.y_wb + k, r.wb.at[k, 1 - y], r.wb1.at[k], to_y)

    bits = dict(y=(y, to_y), l=(lo, to_lo), h=(hi, to_hi))

    def span(order, unit, stage):
        start, n = 0, 4 * unit
        for i in range(stage + 1):
            bit = bits[order[i]][0]
            kept, sent = start + bit * n, start + (1 - bit) * n
            if i < stage:
                start, n = kept, n // 2
        return kept, sent, n

    def rows16(start, n):
        return pl.ds(pl.multiple_of(start, 16), n)

    GN = HC + 128
    VW = GN // 2
    EB = J // 8
    if fused:
        chain_w = [
            (LYH, r.wi.at[k], (r.wi1.at[k], r.wi2.at[k], r.wi3.at[k]), sl.wi + 3 * k, U)
            for k in range(NF)
        ]
        chain_o = (YLH, r.go, (r.go1, r.go2, r.go3), sl.go, U)
        chain_q = (YLH, r.gq, (r.gq1, r.gq2, r.gq3), sl.gq, U)
        chain_k = (YLH, r.gk, (r.gk1, r.gk2, r.gk3), sl.gk, U)
        chain_va = (YLH, r.gva, (r.gva1, r.gva2, r.gva3), sl.gva, U)
        chain_vb = (YLH, r.gvb, (r.gvb1, r.gvb2, r.gvb3), sl.gvb, U)
        chain_e = (LYH, r.ge, (r.ge1, r.ge2, r.ge3), sl.ge, EB)

    def add_into(dst, idx, src):
        dst[idx] = (dst[idx].astype(F32) + src.astype(F32)).astype(BF)

    def lo_wb(p):
        return rc(sl.lo_wb + p, r.wb.at[2 * p + 1 - lo, y], r.wb2.at[p], to_lo)

    def hi_wb():
        return rc(sl.hi_wb, r.wb.at[2 * (1 - hi) + lo, y], r.wb3, to_hi)

    def pump_wb(k):
        if k < 4:
            y_wb(k).wait()
            add_into(r.wb, (k, y), r.wb1[k])

            @pl.when(lo == 1 - k % 2)
            def _():
                lo_wb(k // 2).start()
        else:
            p = k - 4
            lo_wb(p).wait()
            add_into(r.wb, (2 * p + lo, y), r.wb2[p])

            @pl.when(hi == 1 - p)
            def _():
                hi_wb().start()

    def pump(steps):
        for step in steps:
            if step[0] is None:
                pump_wb(step[1])
            else:
                st_next(step[0], step[1])

    def st_copy(chain, stage):
        order, buf, got, slot, unit = chain
        _, sent, n = span(order, unit, stage)
        return rc(slot + stage, buf.at[rows16(sent, n)], got[stage], bits[order[stage]][1])

    def st_next(chain, stage):
        order, buf, got, _, unit = chain
        st_copy(chain, stage).wait()
        kept, _, n = span(order, unit, stage)
        add_into(buf, (rows16(kept, n), slice(None)), got[stage][...])
        st_copy(chain, stage + 1).start()

    def st_last(chain):
        order, buf, got, _, unit = chain
        st_copy(chain, 2).wait()
        kept, _, n = span(order, unit, 2)
        return buf[rows16(kept, n), :].astype(F32) + got[2][...].astype(F32)

    def swap_rows(buf, cols, val, unit):
        q = 2 * unit
        for b in range(4):
            to = (b % 2) * 2 + b // 2
            buf[to * q : (to + 1) * q, cols] = val[b * q : (b + 1) * q, :].astype(BF)

    SB = 256
    GR = 32

    if fused:
        b0, b1, b2, b3, b4, b5 = [(None, k) for k in range(6)]
        w0, w1, w2, w3 = chain_w
        FFN_PUMPS = [[], [], [b0, (w0, 0)], [b1, (w1, 0)]]
        MID_PUMPS = [[(w0, 1)], [(w2, 0)]]
        ATT_PUMPS = [[], [b2], [], [(w1, 1), b4], [], []]
        KV_PUMPS = [[], [b3], [(w3, 0), (w2, 1)]]
        END_PUMPS = [(chain_o, 0), b5, (chain_e, 0), (chain_o, 1), (chain_q, 0), (chain_k, 0), (chain_va, 0),
                     (chain_q, 1), (w3, 1), (chain_k, 1), (chain_va, 1), (chain_vb, 0), (chain_e, 1), (chain_vb, 1)]

    def swapped(buf, val, order, unit):
        if order == YLH:
            buf[...] = val.astype(BF)
        else:
            swap_rows(buf, slice(0, val.shape[1]), val, unit)

    def grad_wi(k):
        c_du(k).wait()
        val = nn(r.h2t[0], r.du[k, c]) + nn(r.h2t[1], r.dur[k])
        if not fused:
            r.wi[k] = val.astype(BF)
            return
        swapped(chain_w[k][1], val, chain_w[k][0], U)
        st_copy(chain_w[k], 0).start()

    for k in range(NF):
        for b in range(FC // SB):
            off = k * FC + b * SB
            u = nn(r.h2[...], r.w_in[:, off : off + SB])
            g = nt(r.dyb[...], r.w_back[off : off + SB, :])
            for m in range(T // GR):
                rr = slice(m * GR, (m + 1) * GR)
                um = u[rr, :]
                u2 = um * um
                th = jnp.tanh(um * (GELU_C + (GELU_C * GELU_K) * u2))
                half = 0.5 + 0.5 * th
                r.a[rr, b * SB : (b + 1) * SB] = (um * half).astype(BF)
                slope = half + (um * half) * ((1.0 - th) * (GELU_C + (3.0 * GELU_C * GELU_K) * u2))
                r.duf[rr, b * SB : (b + 1) * SB] = (slope * g[rr, :]).astype(BF)
        r.at[k] = nt(r.sc[...], r.a[...]).astype(BF)
        c_at(k).start()
        r.du[k, 0] = r.duf[:, 0:HC]
        r.du[k, 1] = r.duf[:, HC : 2 * HC]
        c_du(k).start()
        if k == 0:
            r.h2t[0] = nt(r.sa[...], r.h2[...]).astype(BF)
            c_h2t.start()
            c_dy.wait()
        if fused:
            pump(FFN_PUMPS[k])
        rows = slice(k * FC, (k + 1) * FC)
        part_d = nt(r.duf[...], r.w_in[:, rows])
        part_o = nn(r.a[0:H, :], r.w_back[rows, :])
        if k == 0:
            r.oacc[...] = part_o
            r.dacc[...] = part_d
        else:
            r.oacc[...] += part_o
            r.dacc[...] += part_d
        c_at(k).wait()
        wb = nn(r.at[k, 0 : 2 * Q, :], r.dyb[...]) + nn(r.atr[k], r.dyo[...])
        r.wb[k, 0] = wb[0:Q, :].astype(BF)
        r.wb[k, 1] = wb[Q : 2 * Q, :].astype(BF)
        if fused:
            y_wb(k).start()
        if k == 0:
            c_h2t.wait()
        grad_wi(k)
        if k == 0:
            r.ctt[0] = nt(r.sa[...], r.ctx[...]).astype(BF)
            c_ctt.start()
            r.h1t[0] = nt(r.sa[...], r.h1[...]).astype(BF)
            c_h1t.start()

    if fused:
        pump(MID_PUMPS[0])
    gsum = None
    for i in range(T // NR):
        rows = slice(i * NR, (i + 1) * NR)
        dn, xh = r.dacc[rows, :], r.xh2[rows, :]
        part = jnp.sum(dn * xh, axis=0, keepdims=True)
        gsum = part if gsum is None else gsum + part
        dg = dn * gf
        m1 = jnp.sum(dg, axis=1, keepdims=True) * inv_d
        m2 = jnp.sum(dg * xh, axis=1, keepdims=True) * inv_d
        dmid = r.dyb[rows, :].astype(F32) + r.rs2[rows, 0:1] * (dg - m1 - xh * m2)
        r.dmid[rows, :] = dmid
        b = dmid.astype(BF)
        r.dmb[0, rows, :] = b[:, 0:HC]
        r.dmb[1, rows, :] = b[:, HC : 2 * HC]
    r.gvec[1:2, :] = gsum
    c_dm = rc(sl.c_dm, r.dmb.at[1 - c], r.dmr, to_core)
    c_dm.start()
    r.dctx[...] = (nt(r.dmb[0], r.wo[:, 0:HC]) + nt(r.dmb[1], r.wo[:, HC : 2 * HC])).astype(BF)
    r.s_layer[...] = (r.mid[0:H, :] + r.oacc[...]).astype(BF)
    outs = [pltpu.make_async_copy(r.s_layer, r.o_layer, r.osem.at[0]), pltpu.make_async_copy(r.s_x, r.o_x, r.osem.at[1])]
    outs[0].start()
    if fused:
        pump(MID_PUMPS[1])

    def c_ds(i):
        return rc(sl.c_ds + i, r.pd.at[i], r.pdr.at[i], to_core)

    def bwd_dp(i):
        cols = slice(i * 128, (i + 1) * 128)
        dc2 = r.dctx[:, cols]
        return nt(r.sv[:, cols], jnp.concatenate([dc2 * head_mask[0], dc2 * head_mask[1]], axis=0))

    def bwd_soft(i, dpf):
        for m in range(2 * T // 128):
            h, tc = m * 128 // T, slice(m * 128 % T, m * 128 % T + 128)
            pf = r.pt[i, h * J : (h + 1) * J, tc].astype(F32)
            dp = dpf[:, m * 128 : (m + 1) * 128]
            ds = pf * (dp - jnp.sum(pf * dp, axis=0, keepdims=True))
            r.draw[i % 2, h * J : (h + 1) * J, tc] = (ds * scale).astype(BF)

    def bwd_out(i):
        cols = slice(i * 128, (i + 1) * 128)
        q2, dc2, sk2 = r.q[:, cols], r.dctx[:, cols], r.sk[:, cols]
        draw = r.draw[i % 2]
        dsv = nn(r.pt[i, 0:J], dc2 * head_mask[0]) + nn(r.pt[i, J : 2 * J], dc2 * head_mask[1])
        dsk = nn(draw[0:J], q2 * head_mask[0]) + nn(draw[J : 2 * J], q2 * head_mask[1])
        r.pd[i, 0] = dsk.astype(BF)
        r.pd[i, 1] = dsv.astype(BF)
        c_ds(i).start()
        stack = jnp.concatenate([sk2 * head_mask[0], sk2 * head_mask[1]], axis=0)
        r.dqkv[0, i // 3, :, (i % 3) * 128 : (i % 3 + 1) * 128] = tn(draw, stack).astype(BF)

    dpf = bwd_dp(0)
    for i in range(NP):
        nxt = bwd_dp(i + 1) if i + 1 < NP else None
        bwd_soft(i, dpf)
        if i > 0:
            bwd_out(i - 1)
        dpf = nxt
        if i == 0:
            c_ctt.wait()
            c_dm.wait()
            r.go[...] = (nn(r.ctt[0], r.dmb[c]) + nn(r.ctt[1], r.dmr[...])).astype(BF)
            if fused:
                st_copy(chain_o, 0).start()
        if fused:
            pump(ATT_PUMPS[i])
    bwd_out(NP - 1)

    def c_g(i):
        return rc(sl.c_g + i, r.dqkv.at[i, 1 - c], r.dqr.at[i], to_core)

    c_g(0).start()
    for i in range(D // 128):
        cols = slice(i * 128, (i + 1) * 128)
        c_ds(i).wait()
        r.dsk[:, cols] = (r.pd[i, 0].astype(F32) + r.pdr[i, 0].astype(F32)).astype(BF)
        r.dsv[:, cols] = (r.pd[i, 1].astype(F32) + r.pdr[i, 1].astype(F32)).astype(BF)

    dk = nn(r.me[...], r.dsk[...]).astype(BF)
    r.dqkv[1, 0] = dk[:, 0:HC]
    r.dqkv[1, 1] = dk[:, HC : 2 * HC]
    c_g(1).start()
    dv = nn(r.me[...], r.dsv[...]).astype(BF)
    r.dqkv[2, 0] = dv[:, 0:HC]
    r.dqkv[2, 1] = dv[:, HC : 2 * HC]
    c_g(2).start()

    if fused:
        pump(KV_PUMPS[0])

    def wgrad(i):
        c_g(i).wait()
        return nn(r.h1t[0], r.dqkv[i, c]) + nn(r.h1t[1], r.dqr[i])

    c_h1t.wait()
    r.gq[...] = wgrad(0).astype(BF)
    if fused:
        st_copy(chain_q, 0).start()
    r.gk[...] = wgrad(1).astype(BF)
    if fused:
        st_copy(chain_k, 0).start()
        pump(KV_PUMPS[1])
    gv = wgrad(2).astype(BF)
    r.gva[...] = gv[:, 0:VW]
    r.gvb[:, 0 : HC - VW] = gv[:, VW:HC]
    if fused:
        st_copy(chain_va, 0).start()

    acc = None
    for i, w in enumerate((r.wq, r.wk, r.wv)):
        for hf in range(2):
            part = nt(r.dqkv[i, hf], w[:, hf * HC : (hf + 1) * HC])
            acc = part if acc is None else acc + part
    r.dacc[...] = acc

    gsum = None
    for i in range(T // NR):
        rows = slice(i * NR, (i + 1) * NR)
        dn, xh = r.dacc[rows, :], r.xh1[rows, :]
        part = jnp.sum(dn * xh, axis=0, keepdims=True)
        gsum = part if gsum is None else gsum + part
        if i < H // NR:
            dg = dn * ga
            m1 = jnp.sum(dg, axis=1, keepdims=True) * inv_d
            m2 = jnp.sum(dg * xh, axis=1, keepdims=True) * inv_d
            r.s_x[rows, :] = r.dmid[rows, :] + r.rs1[rows, 0:1] * (dg - m1 - xh * m2)
    outs[1].start()
    r.gvec[0:1, :] = gsum
    if fused:
        pump(KV_PUMPS[2])
    gains = jnp.concatenate([r.gvec[0:2, :], jnp.zeros((126, D), F32)], axis=0).astype(BF)
    r.gvb[:, HC - VW : VW] = nt(r.sa[...], gains).astype(BF)
    if fused:
        st_copy(chain_vb, 0).start()

    de = nt(r.dsk[...], r.k[0:H, :]) + nt(r.dsv[...], r.v[0:H, :])
    de = jnp.where(r.sel_t[:, 0:H] > 0.5, de, 0.0).astype(BF)
    for b in range(8):
        b2, b1, b0 = b // 4, (b // 2) % 2, b % 2
        j = 4 * b0 + 2 * b2 + b1
        r.ge[b * EB : (b + 1) * EB, :] = de[j * EB : (j + 1) * EB, :]

    if not fused:
        for cp in outs:
            cp.wait()
        return

    st_copy(chain_e, 0).start()
    pump(END_PUMPS)

    fin = r.fin
    half = U // 2
    mine = pl.ds(pl.multiple_of(c * half, 8), half)
    first = (w0, w1, w2, w3, chain_o, chain_q, chain_k)
    homes = [(r.s_in, k * FC) for k in range(NF)] + [(r.s_out, 0), (r.s_q, 0), (r.s_k, 0), (r.s_v, 0)]
    n1 = len(first) * HC

    def send_out(src, dst):
        cp = pltpu.make_async_copy(src, dst, r.osem.at[len(outs)])
        cp.start()
        outs.append(cp)

    def c_fin(i):
        cols = pl.ds(0, n1) if i == 0 else pl.ds(n1, GN)
        rows = pl.ds(pl.multiple_of((1 - c) * half, 8), half)
        return rc(sl.c_fin + i, fin.at[rows, cols], r.finr.at[:, cols], to_core)

    def put(i):
        dst, base = homes[i]
        at = i * HC
        dst[:, pl.ds(pl.multiple_of(base + c * HC, 128), HC)] = fin[mine, at : at + HC]
        dst[:, pl.ds(pl.multiple_of(base + (1 - c) * HC, 128), HC)] = r.finr[:, at : at + HC]

    def take(i):
        fin[:, i * HC : (i + 1) * HC] = st_last(first[i])

    for i in (0, 1, 2):
        take(i)
    hi_wb().wait()
    r.s_back[...] = r.wb[2 * hi + lo, y].astype(F32) + r.wb3[...].astype(F32)
    send_out(r.s_back, r.o_back)
    for i in (4, 5, 3, 6):
        take(i)
    c_fin(0).start()
    fin[:, n1 : n1 + VW] = st_last(chain_va)
    r.s_e[...] = st_last(chain_e)
    send_out(r.s_e, r.o_e)
    c_fin(0).wait()
    for i in range(len(first)):
        put(i)
    for src, dst in ((r.s_in, r.o_in), (r.s_out, r.o_out), (r.s_q, r.o_q), (r.s_k, r.o_k)):
        send_out(src, dst)
    fin[:, n1 + VW : n1 + GN] = st_last(chain_vb)
    c_fin(1).start()
    c_fin(1).wait()
    put(len(first))
    at = n1 + HC
    r.s_g[...] = fin[mine, at : at + 128] + r.finr[:, at : at + 128]
    send_out(r.s_v, r.o_v)
    send_out(r.s_g, r.o_g)
    for cp in outs:
        cp.wait()


def staged(name):
    return f"s{name[1:]}"


def hand_over(r, names):
    copies = []
    for i, (src, dst) in enumerate(names):
        cp = pltpu.make_async_copy(src, dst, r.sem.at[i])
        cp.start()
        copies.append(cp)
    g = jnp.concatenate([r.s_g[...], jnp.zeros((128 - r.s_g.shape[0], 128), F32)], axis=0).T
    n = r.s_g.shape[0]
    r.d_ga[...] = g[0, 0:n]
    r.d_gf[...] = g[1, 0:n]
    for cp in copies:
        cp.wait()


def run_layer(mesh_shape, tokens, seg_ids, slot_doc, proj_e, g_attn, w_query, w_key, w_value, w_out, g_ffn, w_in,
              w_back, cotangent):
    n_dp, n_seq = mesh_shape
    rows, H, D = tokens.shape
    J = proj_e.shape[1]
    FF = w_in.shape[1]
    fused = n_dp == 8
    T = 2 * H
    HC, U, NF, Q = D // 2, D // 16, FF // D, FF // 32
    EB = J // 8
    GN = HC + 128
    sel_a, sel_c = (jnp.asarray(m, BF) for m in selections(D, FF))

    inputs = dict(
        x_in=(tokens.reshape(H, D), False),
        seg_in=(seg_ids.reshape(1, H), False),
        slot_in=(slot_doc.reshape(1, J), False),
        e_in=(proj_e, False),
        ga=(g_attn, True),
        wq_in=(w_query, False),
        wk_in=(w_key, False),
        wv_in=(w_value, False),
        wo_in=(w_out, False),
        gf=(g_ffn, True),
        w_in_in=(w_in, False),
        w_back_in=(w_back, False),
        dy_in=(cotangent.reshape(H, D), False),
        sa_in=(sel_a, False),
        sc_in=(sel_c, False),
    )
    parts = dict(
        wb=((NF, 2, Q, D), BF),
        wi=((NF, D // 2, HC), BF),
        go=((D // 2, HC), BF),
        gq=((D // 2, HC), BF),
        gk=((D // 2, HC), BF),
        gva=((D // 2, GN // 2), BF),
        gvb=((D // 2, GN // 2), BF),
        ge=((J, H), BF),
    )
    outs = dict(o_layer=((H, D), BF), o_x=((H, D), F32))
    if fused:
        outs.update(
            o_g=((U // 2, 128), F32),
            o_q=((U // 2, D), F32),
            o_k=((U // 2, D), F32),
            o_v=((U // 2, D), F32),
            o_out=((U // 2, D), F32),
            o_in=((U // 2, FF), F32),
            o_back=((Q, D), F32),
            o_e=((EB, H), F32),
        )
    else:
        outs.update(parts)
    scratch = dict(
        xb=((T, D), BF), eb=((T, J), BF), segs=((2, 1, H), jnp.int32), slot=((1, J), jnp.int32),
        wq=((D, D), BF), wk=((D, D), BF), wv=((D, D), BF), wo=((D, D), BF),
        w_in=((D, FF), BF), w_back=((FF, D), BF),
        dyb=((T, D), BF), dyo=((T, D), BF),
        sa=((D // 2, D), BF), sc=((4 * Q, FF // 4), BF),
        eye=((T, T), BF),
        h1=((T, D), BF), xh1=((T, D), F32), rs1=((T, 128), F32),
        q=((T, D), BF), k=((T, D), BF), v=((T, D), BF),
        sel_t=((J, T), F32), me=((T, J), BF), met=((J, T), BF),
        pk=((2, J, D), BF), pkr=((2, J, D), BF), sk=((J, D), BF), sv=((J, D), BF),

        pt=((D // 128, 2 * J, T), BF), ctx=((T, D), BF),
        mid=((T, D), F32), xh2=((T, D), F32), rs2=((T, 128), F32), h2=((T, D), BF),
        h1t=((2, D // 2, T), BF), h2t=((2, D // 2, T), BF), ctt=((2, D // 2, T), BF),
        a=((T, D), BF), duf=((T, D), BF), du=((NF, 2, T, HC), BF), dur=((NF, T, HC), BF),
        at=((NF, 4 * Q, T), BF), atr=((NF, 2 * Q, T), BF),
        oacc=((H, D), F32), dacc=((T, D), F32), dmid=((T, D), F32), gvec=((8, D), F32),
        dmb=((2, T, HC), BF), dmr=((T, HC), BF), dctx=((T, D), BF), draw=((2, 2 * J, T), BF),
        pd=((D // 128, 2, J, 128), BF), pdr=((D // 128, 2, J, 128), BF),
        dsk=((J, D), BF), dsv=((J, D), BF),
        dqkv=((3, 2, T, HC), BF), dqr=((3, T, HC), BF),
    )
    if fused:
        scratch.update(
            parts,
            wb1=((NF, Q, D), BF), wb2=((2, Q, D), BF), wb3=((Q, D), BF),
            wi1=((NF, 4 * U, HC), BF), wi2=((NF, 2 * U, HC), BF), wi3=((NF, U, HC), BF),
            go1=((4 * U, HC), BF), go2=((2 * U, HC), BF), go3=((U, HC), BF),
            gq1=((4 * U, HC), BF), gq2=((2 * U, HC), BF), gq3=((U, HC), BF),
            gk1=((4 * U, HC), BF), gk2=((2 * U, HC), BF), gk3=((U, HC), BF),
            gva1=((4 * U, GN // 2), BF), gva2=((2 * U, GN // 2), BF), gva3=((U, GN // 2), BF),
            gvb1=((4 * U, GN // 2), BF), gvb2=((2 * U, GN // 2), BF), gvb3=((U, GN // 2), BF),
            ge1=((4 * EB, H), BF), ge2=((2 * EB, H), BF), ge3=((EB, H), BF),
            fin=((U, NF * HC + 3 * HC + GN), F32), finr=((U // 2, NF * HC + 3 * HC + GN), F32),
        )
    counts = dict(
        x_seg=1, x_e=1, x_x=1, x_dy=1, c_pk=1, c_pv=1, c_h1t=1, c_h2t=1, c_dy=1, c_ctt=1, c_at=NF, c_du=NF, c_dm=1,
        c_ds=D // 128, c_g=3, y_wb=NF, wi=3 * NF, lo_wb=2, hi_wb=1, go=3, gq=3, gk=3, gva=3, gvb=3, ge=3, c_fin=2,
    )
    sl, count = SimpleNamespace(), 0
    for name, n in counts.items():
        setattr(sl, name, count)
        count += n
    scratch.update((staged(n), v) for n, v in outs.items() if n[0] == "o")
    names = [*inputs, *outs, *scratch]

    def body(*refs):
        r = SimpleNamespace(**dict(zip(names, refs)))
        r.osem, r.lsem, r.ssem, r.rsem = refs[len(names) :]
        layer_body(fused, r, sl)

    res = pl.pallas_call(
        body,
        out_shape=[jax.ShapeDtypeStruct(sh, dt) for sh, dt in outs.values()],
        in_specs=[pl.BlockSpec(memory_space=pltpu.VMEM if v else pl.ANY) for _, v in inputs.values()],
        out_specs=[pl.BlockSpec(memory_space=pl.ANY if n[0] == "o" else pltpu.VMEM) for n in outs],
        scratch_shapes=[pltpu.VMEM(sh, dt) for sh, dt in scratch.values()]
        + [pltpu.SemaphoreType.DMA((10,))]
        + [pltpu.SemaphoreType.DMA((14,)), pltpu.SemaphoreType.DMA((count,)), pltpu.SemaphoreType.DMA((count,))],
        compiler_params=pltpu.CompilerParams(
            collective_id=0, has_side_effects=True, vmem_limit_bytes=60 * 1024 * 1024
        ),
        cost_estimate=pl.CostEstimate(flops=12 * 10**9, bytes_accessed=24 * 10**6, transcendentals=2 * 10**6),
    )(*[v for v, _ in inputs.values()])
    o = SimpleNamespace(**dict(zip(outs, res)))
    if fused:
        src = dict(s_layer=o.o_layer, s_x=o.o_x, s_q=o.o_q, s_k=o.o_k, s_v=o.o_v, s_out=o.o_out, s_in=o.o_in,
                   s_back=o.o_back, s_e=o.o_e, s_g=o.o_g)
        n_copy = len(src) - 1
        dst = dict(
            d_layer=((rows, H, D), BF), d_x=((rows, H, D), F32), d_q=((U // 2, D), F32), d_k=((U // 2, D), F32),
            d_v=((U // 2, D), F32), d_out=((U // 2, D), F32), d_in=((U // 2, FF), F32), d_back=((Q, D), F32),
            d_e=((EB, H), F32), d_ga=((U // 2,), F32), d_gf=((U // 2,), F32),
        )

        def tail(*refs):
            r = SimpleNamespace(**dict(zip([*src, *dst], refs)))
            r.sem = refs[-1]
            r.d_layer, r.d_x = r.d_layer.at[0], r.d_x.at[0]
            pairs = list(zip(vars(r).values(), list(vars(r).values())[len(src) :]))[:n_copy]
            hand_over(r, pairs)

        res = pl.pallas_call(
            tail,
            out_shape=[jax.ShapeDtypeStruct(sh, dt) for sh, dt in dst.values()],
            in_specs=[pl.BlockSpec(memory_space=pl.ANY)] * n_copy + [pl.BlockSpec(memory_space=pltpu.VMEM)],
            out_specs=[pl.BlockSpec(memory_space=pltpu.VMEM)] * len(dst),
            scratch_shapes=[pltpu.SemaphoreType.DMA((n_copy,))],
        )(*src.values())
        o = SimpleNamespace(**dict(zip(dst, res)))
        return o.d_layer, o.d_x, o.d_ga, o.d_q, o.d_k, o.d_v, o.d_out, o.d_gf, o.d_in, o.d_back, o.d_e.T

    layer = o.o_layer.reshape(rows, H, D)
    x_grad = o.o_x.reshape(rows, H, D)

    s = lax.axis_index(SEQ)
    x, c = s // 2, s % 2
    both = (DP, SEQ)

    def scatter(v):
        return lax.psum_scatter(v, both, scatter_dimension=0, tiled=True)

    def rows_back(v, y_first):
        v = v.astype(F32).reshape(2, 2, 2, U, v.shape[-1])
        v = v.transpose(2, 1, 0, 3, 4) if y_first else v.transpose(2, 0, 1, 3, 4)
        return v.reshape(8, U, v.shape[-1])

    def whole(v, y_first):
        v = rows_back(v, y_first)
        full = jnp.zeros((8, 2, U, 2, HC), F32)
        full = lax.dynamic_update_slice(full, v[:, None, :, None, :], (0, x, 0, c, 0))
        return full.reshape(D, 2 * HC)

    wi = jnp.stack([whole(o.wi[f], True) for f in range(NF)], axis=1).reshape(D, FF)
    wo = whole(o.go, True)
    gv = jnp.concatenate([o.gva, o.gvb], axis=1)
    wqkv = [whole(o.gq, True), whole(o.gk, True), whole(gv[:, :HC], True)]
    gains = rows_back(gv[:, HC:], True)
    gfull = lax.dynamic_update_slice(jnp.zeros((8, 2, U, 128), F32), gains[:, None], (0, x, 0, 0)).reshape(D, 128)
    wb = o.wb.astype(F32).reshape(NF * 2, 1, Q, D)
    wb = lax.dynamic_update_slice(jnp.zeros((NF * 2, 4, Q, D), F32), wb, (0, s, 0, 0)).reshape(FF, D)
    ge = o.ge.astype(F32).reshape(2, 2, 2, EB, H).transpose(2, 0, 1, 3, 4).reshape(J, H).T
    return (
        layer, x_grad, scatter(gfull[:, 0]), scatter(wqkv[0]), scatter(wqkv[1]), scatter(wqkv[2]), scatter(wo),
        scatter(gfull[:, 1]), scatter(wi), scatter(wb), lax.psum_scatter(ge, DP, scatter_dimension=1, tiled=True),
    )


def solution(mesh):
    shape = (mesh.shape[DP], mesh.shape[SEQ])
    both = (DP, SEQ)
    in_specs = (
        P(DP, SEQ, None), P(DP, SEQ), P(DP, None), P(SEQ, None),
        P(), P(), P(), P(), P(), P(), P(), P(), P(DP, SEQ, None),
    )
    out_specs = (
        P(DP, SEQ, None), P(DP, SEQ, None), P(both), P(both, None), P(both, None), P(both, None),
        P(both, None), P(both), P(both, None), P(both, None), P(SEQ, DP),
    )
    return jax.shard_map(
        functools.partial(run_layer, shape), mesh=mesh, in_specs=in_specs, out_specs=out_specs, check_vma=False
    )
```

```python
import functools
from types import SimpleNamespace

import jax
import jax.numpy as jnp
import numpy as np
from jax import lax
from jax.experimental import pallas as pl
from jax.experimental.pallas import tpu as pltpu
from jax.sharding import PartitionSpec as P

HEAD_DIM = 64
DP, SEQ = "dp", "seq"
YLH, LYH = "ylh", "lyh"
BF = jnp.bfloat16
F32 = jnp.float32
MESH = pl.DeviceIdType.MESH
GELU_C = 0.7978845608028654
GELU_K = 0.044715


def nn(a, b):
    return lax.dot_general(a, b, (((1,), (0,)), ((), ())), preferred_element_type=F32)


def tn(a, b):
    return lax.dot_general(a, b, (((0,), (0,)), ((), ())), preferred_element_type=F32)


def nt(a, b):
    return lax.dot_general(a, b, (((1,), (1,)), ((), ())), preferred_element_type=F32)


def selections(d_model, ff):
    unit = d_model // 16
    sel_a = np.zeros((2, d_model // 2, d_model), np.float32)
    for x in range(2):
        for b in range(8):
            j = 4 * (b % 2) + 2 * ((b // 2) % 2) + b // 4
            for o in range(unit):
                sel_a[x, b * unit + o, (2 * j + x) * unit + o] = 1
    q = ff // 32
    sel_c = np.zeros((2, 4 * q, ff // 4), np.float32)
    for x in range(2):
        for b in range(4):
            for o in range(q):
                sel_c[x, b * q + o, (b // 2 * 4 + x * 2 + b % 2) * q + o] = 1
    return sel_a, sel_c


def layer_body(fused, r, sl):
    d, s = lax.axis_index(DP), lax.axis_index(SEQ)
    x, c = s // 2, s % 2
    y, lo, hi = d % 2, (d // 2) % 2, d // 4
    to_core = (d, s + 1 - 2 * c)
    to_x = (d, s + 2 - 4 * x)
    to_y = (d + 1 - 2 * y, s)
    to_lo = (d + 2 - 4 * lo, s)
    to_hi = (d + 4 - 8 * hi, s)
    lsem, ssem, rsem = r.lsem, r.ssem, r.rsem
    D = r.h1.shape[1]
    T = r.h1.shape[0]
    H = T // 2
    J = r.sk.shape[0]
    FC = D
    NF = r.w_in.shape[1] // FC
    HC = D // 2
    U = D // 16
    Q = r.wb.shape[1] // 4
    scale = HEAD_DIM ** (-0.5)

    loads = []

    def load(src, dst):
        cp = pltpu.make_async_copy(src, dst, lsem.at[len(loads)])
        loads.append(cp)
        cp.start()
        return cp

    def rc(i, src, dst, dev):
        return pltpu.make_async_remote_copy(
            src_ref=src, dst_ref=dst, send_sem=ssem.at[i], recv_sem=rsem.at[i], device_id=dev, device_id_type=MESH
        )

    partners = [to_core, to_x] + ([to_y, to_lo, to_hi] if fused else [])
    barrier = pltpu.get_barrier_semaphore()
    for dev in partners:
        pl.semaphore_signal(barrier, inc=1, device_id=dev, device_id_type=MESH)
    l_x = load(r.x_in, r.xb.at[pl.ds(0, H)])
    l_seg = load(r.seg_in, r.segs.at[0])
    l_slot = load(r.slot_in, r.slot)
    l_e = load(r.e_in, r.eb.at[pl.ds(0, H)])
    l_wq = load(r.wq_in, r.wq)
    l_wk = load(r.wk_in, r.wk)
    l_wv = load(r.wv_in, r.wv)
    l_dy = load(r.dy_in, r.dyb.at[pl.ds(0, H)])
    l_sa = load(r.sa_in.at[x], r.sa)
    l_wo = load(r.wo_in, r.wo)
    l_sc = load(r.sc_in.at[x], r.sc)
    l_w_in = load(r.w_in_in, r.w_in)
    l_w_back = load(r.w_back_in, r.w_back)

    pl.semaphore_wait(barrier, len(partners))

    x_seg = rc(sl.x_seg, r.seg_in, r.segs.at[1], to_x)
    x_e = rc(sl.x_e, r.e_in, r.eb.at[pl.ds(H, H)], to_x)
    x_x = rc(sl.x_x, r.x_in, r.xb.at[pl.ds(H, H)], to_x)
    x_dy = rc(sl.x_dy, r.dy_in, r.dyb.at[pl.ds(H, H)], to_x)
    x_x.start()
    if fused:
        own_rows, far_rows = pl.ds(0, H), pl.ds(H, H)
        l_dyf = rc(sl.l_dy, r.dy_in, r.dyf.at[own_rows], to_lo)
        x_dyf = rc(sl.x_dyf, r.dyf.at[own_rows], r.dyf.at[far_rows], to_x)
        l_dyf.start()

    rows_i = lax.broadcasted_iota(jnp.int32, (T, T), 0)
    cols_i = lax.broadcasted_iota(jnp.int32, (T, T), 1)
    eye = jnp.where(rows_i == cols_i, 1.0, 0.0).astype(BF)
    r.eye[...] = eye
    ga = r.ga[...].astype(F32).reshape(1, D)
    gf = r.gf[...].astype(F32).reshape(1, D)
    inv_d = 1.0 / D
    NR = 64

    def norm_rows(v):
        cen = v - jnp.sum(v, axis=1, keepdims=True) * inv_d
        rstd = lax.rsqrt(jnp.sum(cen * cen, axis=1, keepdims=True) * inv_d + 1e-5)
        return cen * rstd, rstd

    def norm_into(src, gain, xh_ref, rs_ref, h_ref, start, count):
        for i in range(start // NR, (start + count) // NR):
            rows = slice(i * NR, (i + 1) * NR)
            xh, rstd = norm_rows(src[rows, :].astype(F32))
            xh_ref[rows, :] = xh
            rs_ref[rows, :] = jnp.broadcast_to(rstd, (NR, 128))
            h_ref[rows, :] = (xh * gain).astype(BF)

    l_x.wait()
    norm_into(r.xb, ga, r.xh1, r.rs1, r.h1, 0, H)
    x_seg.start()
    x_e.start()
    l_slot.wait()
    slot_row = r.slot[...].astype(F32)
    slot_col = nt(eye, jnp.broadcast_to(slot_row, (T, J)).astype(BF))
    l_wq.wait()
    l_wk.wait()
    l_wv.wait()
    own, far = slice(0, H), slice(H, T)
    r.k[own, :] = nn(r.h1[own, :], r.wk[...]).astype(BF)
    r.v[own, :] = nn(r.h1[own, :], r.wv[...]).astype(BF)
    r.q[own, :] = nn(r.h1[own, :], r.wq[...]).astype(BF)
    l_e.wait()
    l_sa.wait()
    x_x.wait()
    x_dy.start()
    norm_into(r.xb, ga, r.xh1, r.rs1, r.h1, H, H)
    r.k[far, :] = nn(r.h1[far, :], r.wk[...]).astype(BF)

    x_seg.wait()
    x_e.wait()
    l_seg.wait()
    seg_row = jnp.concatenate([r.segs[0], r.segs[1]], axis=1).astype(F32)
    seg_col = nt(eye, jnp.broadcast_to(seg_row, (J, T)).astype(BF))
    r.sel_t[...] = jnp.where(slot_col == seg_row, 1.0, 0.0)
    r.me[...] = jnp.where(seg_col == slot_row, r.eb[...].astype(F32), 0.0).astype(BF)
    r.met[...] = nt(eye, r.me[...]).astype(BF)

    c_pk = rc(sl.c_pk, r.pk.at[0], r.pkr.at[0], to_core)
    c_pv = rc(sl.c_pv, r.pk.at[1], r.pkr.at[1], to_core)
    r.pk[0] = nn(r.met[...], r.k[...]).astype(BF)
    c_pk.start()
    r.v[far, :] = nn(r.h1[far, :], r.wv[...]).astype(BF)
    r.pk[1] = nn(r.met[...], r.v[...]).astype(BF)
    c_pv.start()
    r.q[far, :] = nn(r.h1[far, :], r.wq[...]).astype(BF)
    c_h1t = rc(sl.c_h1t, r.h1t.at[0], r.h1t.at[1], to_core)

    lane = lax.broadcasted_iota(jnp.int32, (T, 128), 1)
    head_mask = [jnp.where(lane < 64, 1.0, 0.0).astype(BF), jnp.where(lane < 64, 0.0, 1.0).astype(BF)]

    NP = D // 128

    def fwd_raw(i):
        cols = slice(i * 128, (i + 1) * 128)
        q2 = r.q[:, cols]
        return nt(r.sk[:, cols], jnp.concatenate([q2 * head_mask[0], q2 * head_mask[1]], axis=0))

    def fwd_soft(i, raw):
        for m in range(2 * T // 128):
            h, tc = m * 128 // T, slice(m * 128 % T, m * 128 % T + 128)
            sc = jnp.where(r.sel_t[:, tc] > 0.5, raw[:, m * 128 : (m + 1) * 128] * scale, -1e30)
            e = jnp.exp(sc - jnp.max(sc, axis=0, keepdims=True))
            r.pt[i, h * J : (h + 1) * J, tc] = (e * (1.0 / jnp.sum(e, axis=0, keepdims=True))).astype(BF)

    def fwd_ctx(i):
        cols = slice(i * 128, (i + 1) * 128)
        sv2 = r.sv[:, cols]
        stack = jnp.concatenate([sv2 * head_mask[0], sv2 * head_mask[1]], axis=0)
        r.ctx[:, cols] = tn(r.pt[i], stack).astype(BF)

    c_pk.wait()
    r.sk[...] = (r.pk[0].astype(F32) + r.pkr[0].astype(F32)).astype(BF)
    raw = fwd_raw(0)
    for i in range(NP):
        nxt = fwd_raw(i + 1) if i + 1 < NP else None
        fwd_soft(i, raw)
        if i == 0:
            c_pv.wait()
            r.sv[...] = (r.pk[1].astype(F32) + r.pkr[1].astype(F32)).astype(BF)
        if i > 0:
            fwd_ctx(i - 1)
        raw = nxt
    fwd_ctx(NP - 1)

    if fused:
        l_dyf.wait()
        x_dyf.start()

    def l_h2(p):
        rows = pl.ds(p * NR, NR)
        return rc(sl.l_h2 + p, r.h2.at[rows], r.h2f.at[rows], to_lo)

    def x_h2(p):
        return rc(sl.x_h2 + p, r.h2f.at[pl.ds(p * NR, NR)], r.h2f.at[pl.ds(H + p * NR, NR)], to_x)

    l_wo.wait()
    for rows in (own, far):
        r.mid[rows, :] = r.xb[rows, :].astype(F32) + nn(r.ctx[rows, :], r.wo[...])
    norm_into(r.mid, gf, r.xh2, r.rs2, r.h2, 0, H)
    if fused:
        for p in range(H // NR):
            l_h2(p).start()
    norm_into(r.mid, gf, r.xh2, r.rs2, r.h2, H, H)
    x_dy.wait()
    l_dy.wait()
    c_dy = rc(sl.c_dy, r.dyh.at[1 - c], r.dyr, to_core)
    l_w_in.wait()
    l_w_back.wait()
    l_sc.wait()
    c_h2t = rc(sl.c_h2t, r.h2t.at[0], r.h2t.at[1], to_core)
    c_ctt = rc(sl.c_ctt, r.ctt.at[0], r.ctt.at[1], to_core)

    def c_at(k):
        return rc(sl.c_at + k, r.at.at[k], r.atr.at[k], to_core)

    def c_du(f):
        return rc(sl.c_du + f, r.du.at[f, 1 - c], r.dur.at[f], to_core)

    def y_wb(k):
        return rc(sl.y_wb + k, r.wb.at[k, rows16((1 - y) * 2 * Q, 2 * Q)], r.wb1.at[k], to_y)

    bits = dict(y=(y, to_y), l=(lo, to_lo), h=(hi, to_hi))

    def span(order, unit, stage):
        start, n = 0, 4 * unit
        for i in range(stage + 1):
            bit = bits[order[i]][0]
            kept, sent = start + bit * n, start + (1 - bit) * n
            if i < stage:
                start, n = kept, n // 2
        return kept, sent, n

    def rows16(start, n):
        return pl.ds(pl.multiple_of(start, 16), n)

    GN = 128
    VW = 256
    EB = J // 8
    if fused:
        chain_w = [
            (LYH if k % 2 else YLH, r.wi.at[k], (r.wi1.at[k], r.wi2.at[k], r.wi3.at[k]), sl.wi + 3 * k, U)
            for k in range(NF)
        ]
        chain_o = (LYH, r.go, (r.go1, r.go2, r.go3), sl.go, U)
        chain_q = (LYH, r.gq, (r.gq1, r.gq2, r.gq3), sl.gq, U)
        chain_k = (YLH, r.gk, (r.gk1, r.gk2, r.gk3), sl.gk, U)
        chain_va = (YLH, r.gva, (r.gva1, r.gva2, r.gva3), sl.gva, U)
        chain_vb = (YLH, r.gvb, (r.gvb1, r.gvb2, r.gvb3), sl.gvb, U)
        chain_g = (YLH, r.gg, (r.gg1, r.gg2, r.gg3), sl.gg, U)
        chain_e = (LYH, r.ge, (r.ge1, r.ge2, r.ge3), sl.ge, EB)

    def add_into(dst, idx, src):
        dst[idx] = (dst[idx].astype(F32) + src.astype(F32)).astype(BF)

    def hi_wb():
        return rc(sl.hi_wb, r.wb.at[1 - hi, rows16(y * 2 * Q, 2 * Q)], r.wb2, to_hi)

    def pump_wb(k):
        if k < 2:
            y_wb(k).wait()
            add_into(r.wb, (k, rows16(y * 2 * Q, 2 * Q), slice(None)), r.wb1[k])

            @pl.when(hi == 1 - k)
            def _():
                hi_wb().start()
        else:
            l_h2(k - 2).wait()
            x_h2(k - 2).start()

    def pump(steps):
        for step in steps:
            if step[0] is None:
                pump_wb(step[1])
            else:
                st_next(step[0], step[1])

    def st_copy(chain, stage):
        order, buf, got, slot, unit = chain
        _, sent, n = span(order, unit, stage)
        return rc(slot + stage, buf.at[rows16(sent, n)], got[stage], bits[order[stage]][1])

    def st_next(chain, stage):
        order, buf, got, _, unit = chain
        st_copy(chain, stage).wait()
        kept, _, n = span(order, unit, stage)
        add_into(buf, (rows16(kept, n), slice(None)), got[stage][...])
        st_copy(chain, stage + 1).start()

    def st_last(chain):
        order, buf, got, _, unit = chain
        st_copy(chain, 2).wait()
        kept, _, n = span(order, unit, 2)
        return buf[rows16(kept, n), :].astype(F32) + got[2][...].astype(F32)

    def swap_rows(buf, cols, val, unit):
        q = 2 * unit
        for b in range(4):
            to = (b % 2) * 2 + b // 2
            buf[to * q : (to + 1) * q, cols] = val[b * q : (b + 1) * q, :].astype(BF)

    SB = 256
    GR = 32

    if fused:
        b0, b1, h0, h1 = [(None, k) for k in range(4)]
        w0, w1, w2, w3 = chain_w
        FFN_PUMPS = [[], [], [h0], [h1]]
        MID_PUMPS = [[(w0, 0)], [(w1, 0)]]
        ATT_PUMPS = [[(w2, 0)], [(w0, 1), (w3, 0)], [], [], [(w1, 1)], []]
        KV_PUMPS = [[(chain_o, 0)], [], [(w2, 1), b0]]
        END_PUMPS = [(w3, 1), b1, (chain_q, 0), (chain_e, 0), (chain_o, 1), (chain_k, 0), (chain_va, 0), (chain_vb, 0),
                     (chain_g, 0), (chain_k, 1), (chain_va, 1), (chain_q, 1), (chain_vb, 1), (chain_e, 1),
                     (chain_g, 1)]

    def swapped(buf, val, order, unit):
        if order == YLH:
            buf[...] = val.astype(BF)
        else:
            swap_rows(buf, slice(0, val.shape[1]), val, unit)

    def dense(k):
        wi = nn(r.h2t[0], r.du[k, c]) + nn(r.h2t[1], r.dur[k])
        if fused:
            swapped(chain_w[k][1], wi, chain_w[k][0], U)
        else:
            r.wi[k] = wi.astype(BF)

    def send_dense(k):
        if fused:
            st_copy(chain_w[k], 0).start()

    NW = r.wb.shape[0]

    def act_rows():
        for h in range(2):
            r.dyh[h, 0:T, :] = r.dyb[:, h * HC : (h + 1) * HC]
        if fused:
            x_dyf.wait()
            for h in range(2):
                r.dyh[h, T : 2 * T, :] = r.dyf[:, h * HC : (h + 1) * HC]
        c_dy.start()
        if fused:
            for p in range(H // NR):
                x_h2(p).wait()
            for k in range(NW):
                for b in range(NB):
                    cols = slice(b * SB, (b + 1) * SB)
                    u = nn(r.h2f[...], r.w_in[:, pl.ds(pl.multiple_of((lo + 2 * k) * FC + b * SB, SB), SB)])
                    for m in range(T // GR):
                        rr = slice(m * GR, (m + 1) * GR)
                        um = u[rr, :]
                        th = jnp.tanh(um * (GELU_C + (GELU_C * GELU_K) * (um * um)))
                        r.af[k, rr, cols] = (um * (0.5 + 0.5 * th)).astype(BF)
        for k in range(NW):
            r.at[k, :, 0:T] = nt(r.sc[...], r.a[lo + 2 * k if fused else k]).astype(BF)
            if fused:
                r.at[k, :, T : 2 * T] = nt(r.sc[...], r.af[k]).astype(BF)
            c_at(k).start()

    def grad_wb():
        c_dy.wait()
        for k in range(NW):
            c_at(k).wait()
        for k in range(NW):
            r.wb[k] = (nn(r.at[k], r.dyh[c]) + nn(r.atr[k], r.dyr[...])).astype(BF)
        if fused:
            for k in range(NW):
                y_wb(k).start()

    def back(k):
        rows = slice(k * FC, (k + 1) * FC)
        part_d = nt(r.duf[k % 2], r.w_in[:, rows])
        part_o = nn(r.a[k, 0:H, :], r.w_back[rows, :])
        if k == 0:
            r.oacc[...] = part_o
            r.dacc[...] = part_d
        else:
            r.oacc[...] += part_o
            r.dacc[...] += part_d

    NB = FC // SB

    def hidden(k, b):
        off = k * FC + b * SB
        cols = slice(b * SB, (b + 1) * SB)
        r.u[k % 2, :, cols] = nn(r.h2[...], r.w_in[:, off : off + SB])
        r.g[k % 2, :, cols] = nt(r.dyb[...], r.w_back[off : off + SB, :])

    def gelu(k, b):
        cols = slice(b * SB, (b + 1) * SB)
        for m in range(T // GR):
            rr = slice(m * GR, (m + 1) * GR)
            um = r.u[k % 2, rr, cols]
            u2 = um * um
            th = jnp.tanh(um * (GELU_C + (GELU_C * GELU_K) * u2))
            half = 0.5 + 0.5 * th
            act = um * half
            r.a[k, rr, cols] = act.astype(BF)
            slope = half + act * ((1.0 - th) * (GELU_C + (3.0 * GELU_C * GELU_K) * u2))
            r.duf[k % 2, rr, cols] = (slope * r.g[k % 2, rr, cols]).astype(BF)

    for b in range(NB):
        hidden(0, b)
    for k in range(NF):
        for b in range(NB):
            if k + 1 < NF:
                hidden(k + 1, b)
            gelu(k, b)
        if k > 0:
            back(k - 1)
            if fused:
                pump(FFN_PUMPS[k])
            if k == 1:
                c_h2t.wait()
            c_du(k - 1).wait()
            dense(k - 1)
        else:
            r.h2t[0] = nt(r.sa[...], r.h2[...]).astype(BF)
        r.du[k, 0] = r.duf[k % 2, :, 0:HC]
        r.du[k, 1] = r.duf[k % 2, :, HC : 2 * HC]
        c_du(k).start()
        if k > 0:
            send_dense(k - 1)
        else:
            c_h2t.start()
    back(NF - 1)
    r.ctt[0] = nt(r.sa[...], r.ctx[...]).astype(BF)
    r.h1t[0] = nt(r.sa[...], r.h1[...]).astype(BF)
    c_ctt.start()
    c_h1t.start()

    c_du(NF - 1).wait()
    dense(NF - 1)
    if fused:
        pump(MID_PUMPS[0])
    gsum = None
    for i in range(T // NR):
        rows = slice(i * NR, (i + 1) * NR)
        dn, xh = r.dacc[rows, :], r.xh2[rows, :]
        part = jnp.sum(dn * xh, axis=0, keepdims=True)
        gsum = part if gsum is None else gsum + part
        dg = dn * gf
        m1 = jnp.sum(dg, axis=1, keepdims=True) * inv_d
        m2 = jnp.sum(dg * xh, axis=1, keepdims=True) * inv_d
        dmid = r.dyb[rows, :].astype(F32) + r.rs2[rows, 0:1] * (dg - m1 - xh * m2)
        r.dmid[rows, :] = dmid
        b = dmid.astype(BF)
        r.dmb[0, rows, :] = b[:, 0:HC]
        r.dmb[1, rows, :] = b[:, HC : 2 * HC]
    r.gvec[1:2, :] = gsum
    c_dm = rc(sl.c_dm, r.dmb.at[1 - c], r.dmr, to_core)
    c_dm.start()
    send_dense(NF - 1)
    r.dctx[...] = (nt(r.dmb[0], r.wo[:, 0:HC]) + nt(r.dmb[1], r.wo[:, HC : 2 * HC])).astype(BF)
    r.s_layer[...] = (r.mid[0:H, :] + r.oacc[...]).astype(BF)
    outs = [pltpu.make_async_copy(r.s_layer, r.o_layer, r.osem.at[0]), pltpu.make_async_copy(r.s_x, r.o_x, r.osem.at[1])]
    outs[0].start()
    if fused:
        pump(MID_PUMPS[1])

    act_rows()

    def c_ds(g):
        pair = pl.ds(2 * g, 2)
        return rc(sl.c_ds + g, r.pd.at[pair], r.pdr.at[pair], to_core)

    def bwd_dp(i):
        cols = slice(i * 128, (i + 1) * 128)
        dc2 = r.dctx[:, cols]
        return nt(r.sv[:, cols], jnp.concatenate([dc2 * head_mask[0], dc2 * head_mask[1]], axis=0))

    def bwd_soft(i, dpf):
        for m in range(2 * T // 128):
            h, tc = m * 128 // T, slice(m * 128 % T, m * 128 % T + 128)
            pf = r.pt[i, h * J : (h + 1) * J, tc].astype(F32)
            dp = dpf[:, m * 128 : (m + 1) * 128]
            ds = pf * (dp - jnp.sum(pf * dp, axis=0, keepdims=True))
            r.draw[i % 2, h * J : (h + 1) * J, tc] = (ds * scale).astype(BF)

    def bwd_out(i):
        cols = slice(i * 128, (i + 1) * 128)
        q2, dc2, sk2 = r.q[:, cols], r.dctx[:, cols], r.sk[:, cols]
        draw = r.draw[i % 2]
        dsv = nn(r.pt[i, 0:J], dc2 * head_mask[0]) + nn(r.pt[i, J : 2 * J], dc2 * head_mask[1])
        dsk = nn(draw[0:J], q2 * head_mask[0]) + nn(draw[J : 2 * J], q2 * head_mask[1])
        r.pd[i, 0] = dsk.astype(BF)
        r.pd[i, 1] = dsv.astype(BF)
        stack = jnp.concatenate([sk2 * head_mask[0], sk2 * head_mask[1]], axis=0)
        r.dqkv[0, i // 3, :, (i % 3) * 128 : (i % 3 + 1) * 128] = tn(draw, stack).astype(BF)
        if i % 2:
            c_ds(i // 2).start()

    dpf = bwd_dp(0)
    for i in range(NP):
        nxt = bwd_dp(i + 1) if i + 1 < NP else None
        bwd_soft(i, dpf)
        if i > 0:
            bwd_out(i - 1)
        dpf = nxt
        if i == 0:
            c_ctt.wait()
            c_dm.wait()
            swapped(r.go, nn(r.ctt[0], r.dmb[c]) + nn(r.ctt[1], r.dmr[...]), LYH if fused else YLH, U)
            if fused:
                st_copy(chain_o, 0).start()
        if i == 1:
            grad_wb()
        if fused:
            pump(ATT_PUMPS[i])
    bwd_out(NP - 1)

    def c_g(i):
        return rc(sl.c_g + i, r.dqkv.at[i, 1 - c], r.dqr.at[i], to_core)

    c_g(0).start()
    for i in range(D // 128):
        cols = slice(i * 128, (i + 1) * 128)
        if i % 2 == 0:
            c_ds(i // 2).wait()
        r.dsk[:, cols] = (r.pd[i, 0].astype(F32) + r.pdr[i, 0].astype(F32)).astype(BF)
        r.dsv[:, cols] = (r.pd[i, 1].astype(F32) + r.pdr[i, 1].astype(F32)).astype(BF)

    dk = nn(r.me[...], r.dsk[...]).astype(BF)
    dv = nn(r.me[...], r.dsv[...]).astype(BF)
    r.dqkv[1, 0] = dk[:, 0:HC]
    r.dqkv[1, 1] = dk[:, HC : 2 * HC]
    r.dqkv[2, 0] = dv[:, 0:HC]
    r.dqkv[2, 1] = dv[:, HC : 2 * HC]
    c_g(1).start()
    c_g(2).start()

    def wgrad(i):
        return (nn(r.h1t[0], r.dqkv[i, c]) + nn(r.h1t[1], r.dqr[i])).astype(BF)

    c_h1t.wait()
    c_g(0).wait()
    swapped(r.gq, wgrad(0), LYH if fused else YLH, U)
    if fused:
        st_copy(chain_q, 0).start()
        pump(KV_PUMPS[0])
    de = nt(r.dsk[...], r.k[0:H, :]) + nt(r.dsv[...], r.v[0:H, :])
    de = jnp.where(r.sel_t[:, 0:H] > 0.5, de, 0.0).astype(BF)
    for b in range(8):
        b2, b1, b0 = b // 4, (b // 2) % 2, b % 2
        j = 4 * b0 + 2 * b2 + b1
        r.ge[b * EB : (b + 1) * EB, :] = de[j * EB : (j + 1) * EB, :]
    acc = None
    for i, w in enumerate((r.wq, r.wk, r.wv)):
        if i == 1:
            r.dacc[...] = acc
            c_g(1).wait()
            c_g(2).wait()
            r.gk[...] = wgrad(1)
            gv = wgrad(2)
            r.gva[...] = gv[:, 0:VW]
            r.gvb[...] = gv[:, VW:HC]
            if fused:
                st_copy(chain_k, 0).start()
                st_copy(chain_va, 0).start()
                st_copy(chain_vb, 0).start()
                st_copy(chain_e, 0).start()
                pump(KV_PUMPS[1])
            acc = r.dacc[...]
        for hf in range(2):
            part = nt(r.dqkv[i, hf], w[:, hf * HC : (hf + 1) * HC])
            acc = part if acc is None else acc + part
    r.dacc[...] = acc

    gsum = None
    for i in range(T // NR):
        rows = slice(i * NR, (i + 1) * NR)
        dn, xh = r.dacc[rows, :], r.xh1[rows, :]
        part = jnp.sum(dn * xh, axis=0, keepdims=True)
        gsum = part if gsum is None else gsum + part
        if i < H // NR:
            dg = dn * ga
            m1 = jnp.sum(dg, axis=1, keepdims=True) * inv_d
            m2 = jnp.sum(dg * xh, axis=1, keepdims=True) * inv_d
            r.s_x[rows, :] = r.dmid[rows, :] + r.rs1[rows, 0:1] * (dg - m1 - xh * m2)
    outs[1].start()
    r.gvec[0:1, :] = gsum
    if fused:
        pump(KV_PUMPS[2])
    gains = jnp.concatenate([r.gvec[0:2, :], jnp.zeros((126, D), F32)], axis=0).astype(BF)
    r.gg[...] = nt(r.sa[...], gains).astype(BF)
    if fused:
        st_copy(chain_g, 0).start()

    if not fused:
        for cp in outs:
            cp.wait()
        return

    pump(END_PUMPS)

    fin = r.fin
    half = U // 2
    mine = pl.ds(pl.multiple_of(c * half, 8), half)
    first = (w0, w1, w2, w3, chain_o, chain_q, chain_k)
    homes = [(r.s_in, k * FC) for k in range(NF)] + [(r.s_out, 0), (r.s_q, 0), (r.s_k, 0), (r.s_v, 0)]
    n1 = len(first) * HC

    def send_out(src, dst):
        cp = pltpu.make_async_copy(src, dst, r.osem.at[len(outs)])
        cp.start()
        outs.append(cp)

    def c_fin(i):
        cols = pl.ds(0, n1) if i == 0 else pl.ds(n1, HC + GN)
        rows = pl.ds(pl.multiple_of((1 - c) * half, 8), half)
        return rc(sl.c_fin + i, fin.at[rows, cols], r.finr.at[:, cols], to_core)

    def put(i):
        dst, base = homes[i]
        at = i * HC
        dst[:, pl.ds(pl.multiple_of(base + c * HC, 128), HC)] = fin[mine, at : at + HC]
        dst[:, pl.ds(pl.multiple_of(base + (1 - c) * HC, 128), HC)] = r.finr[:, at : at + HC]

    def take(i):
        fin[:, i * HC : (i + 1) * HC] = st_last(first[i])

    for i in (0, 1, 2, 3):
        take(i)
    hi_wb().wait()
    r.finb[...] = r.wb[hi, rows16(y * 2 * Q, 2 * Q), :].astype(F32) + r.wb2[...].astype(F32)
    c_finb = rc(sl.c_finb, r.finb.at[pl.ds(pl.multiple_of((1 - c) * Q, 8), Q)], r.finbr, to_core)
    c_finb.start()
    for i in (4, 6):
        take(i)
    fin[:, n1 : n1 + VW] = st_last(chain_va)
    take(5)
    c_fin(0).start()
    fin[:, n1 + VW : n1 + HC] = st_last(chain_vb)
    r.s_e[...] = st_last(chain_e)
    send_out(r.s_e, r.o_e)
    fin[:, n1 + HC : n1 + HC + GN] = st_last(chain_g)
    c_fin(1).start()
    c_finb.wait()
    r.s_back[:, pl.ds(pl.multiple_of(c * HC, 128), HC)] = r.finb[pl.ds(pl.multiple_of(c * Q, 8), Q), :]
    r.s_back[:, pl.ds(pl.multiple_of((1 - c) * HC, 128), HC)] = r.finbr[...]
    send_out(r.s_back, r.o_back)
    c_fin(0).wait()
    for i in range(len(first)):
        put(i)
    for src, dst in ((r.s_in, r.o_in), (r.s_out, r.o_out), (r.s_q, r.o_q), (r.s_k, r.o_k)):
        send_out(src, dst)
    c_fin(1).wait()
    put(len(first))
    at = n1 + HC
    r.s_g[...] = fin[mine, at : at + 128] + r.finr[:, at : at + 128]
    send_out(r.s_v, r.o_v)
    send_out(r.s_g, r.o_g)
    for cp in outs:
        cp.wait()


def staged(name):
    return f"s{name[1:]}"


def hand_over(r, names):
    copies = []
    for i, (src, dst) in enumerate(names):
        cp = pltpu.make_async_copy(src, dst, r.sem.at[i])
        cp.start()
        copies.append(cp)
    g = jnp.concatenate([r.s_g[...], jnp.zeros((128 - r.s_g.shape[0], 128), F32)], axis=0).T
    n = r.s_g.shape[0]
    r.d_ga[...] = g[0, 0:n]
    r.d_gf[...] = g[1, 0:n]
    for cp in copies:
        cp.wait()


def run_layer(mesh_shape, tokens, seg_ids, slot_doc, proj_e, g_attn, w_query, w_key, w_value, w_out, g_ffn, w_in,
              w_back, cotangent):
    n_dp, n_seq = mesh_shape
    rows, H, D = tokens.shape
    J = proj_e.shape[1]
    FF = w_in.shape[1]
    fused = n_dp == 8
    T = 2 * H
    HC, U, NF, Q = D // 2, D // 16, FF // D, FF // 32
    EB = J // 8
    NW, TW = (2, 2 * T) if fused else (NF, T)
    GN, VW = 128, 256
    sel_a, sel_c = (jnp.asarray(m, BF) for m in selections(D, FF))

    inputs = dict(
        x_in=(tokens.reshape(H, D), False),
        seg_in=(seg_ids.reshape(1, H), False),
        slot_in=(slot_doc.reshape(1, J), False),
        e_in=(proj_e, False),
        ga=(g_attn, True),
        wq_in=(w_query, False),
        wk_in=(w_key, False),
        wv_in=(w_value, False),
        wo_in=(w_out, False),
        gf=(g_ffn, True),
        w_in_in=(w_in, False),
        w_back_in=(w_back, False),
        dy_in=(cotangent.reshape(H, D), False),
        sa_in=(sel_a, False),
        sc_in=(sel_c, False),
    )
    parts = dict(
        wb=((NW, 4 * Q, HC), BF),
        wi=((NF, D // 2, HC), BF),
        go=((D // 2, HC), BF),
        gq=((D // 2, HC), BF),
        gk=((D // 2, HC), BF),
        gva=((D // 2, VW), BF),
        gvb=((D // 2, HC - VW), BF),
        gg=((D // 2, GN), BF),
        ge=((J, H), BF),
    )
    outs = dict(o_layer=((H, D), BF), o_x=((H, D), F32))
    if fused:
        outs.update(
            o_g=((U // 2, 128), F32),
            o_q=((U // 2, D), F32),
            o_k=((U // 2, D), F32),
            o_v=((U // 2, D), F32),
            o_out=((U // 2, D), F32),
            o_in=((U // 2, FF), F32),
            o_back=((Q, D), F32),
            o_e=((EB, H), F32),
        )
    else:
        outs.update(parts)
    scratch = dict(
        xb=((T, D), BF), eb=((T, J), BF), segs=((2, 1, H), jnp.int32), slot=((1, J), jnp.int32),
        wq=((D, D), BF), wk=((D, D), BF), wv=((D, D), BF), wo=((D, D), BF),
        w_in=((D, FF), BF), w_back=((FF, D), BF),
        dyb=((T, D), BF), dyh=((2, TW, HC), BF), dyr=((TW, HC), BF),
        sa=((D // 2, D), BF), sc=((4 * Q, FF // 4), BF),
        eye=((T, T), BF),
        h1=((T, D), BF), xh1=((T, D), F32), rs1=((T, 128), F32),
        q=((T, D), BF), k=((T, D), BF), v=((T, D), BF),
        sel_t=((J, T), F32), me=((T, J), BF), met=((J, T), BF),
        pk=((2, J, D), BF), pkr=((2, J, D), BF), sk=((J, D), BF), sv=((J, D), BF),

        pt=((D // 128, 2 * J, T), BF), ctx=((T, D), BF),
        mid=((T, D), F32), xh2=((T, D), F32), rs2=((T, 128), F32), h2=((T, D), BF),
        h1t=((2, D // 2, T), BF), h2t=((2, D // 2, T), BF), ctt=((2, D // 2, T), BF),
        a=((NF, T, D), BF), duf=((2, T, D), BF), u=((2, T, D), F32), g=((2, T, D), F32), du=((NF, 2, T, HC), BF), dur=((NF, T, HC), BF),
        at=((NW, 4 * Q, TW), BF), atr=((NW, 4 * Q, TW), BF),
        oacc=((H, D), F32), dacc=((T, D), F32), dmid=((T, D), F32), gvec=((8, D), F32),
        dmb=((2, T, HC), BF), dmr=((T, HC), BF), dctx=((T, D), BF), draw=((2, 2 * J, T), BF),
        pd=((D // 128, 2, J, 128), BF), pdr=((D // 128, 2, J, 128), BF),
        dsk=((J, D), BF), dsv=((J, D), BF),
        dqkv=((3, 2, T, HC), BF), dqr=((3, T, HC), BF),
    )
    if fused:
        scratch.update(
            parts,
            wb1=((2, 2 * Q, HC), BF), wb2=((2 * Q, HC), BF), finb=((2 * Q, HC), F32), finbr=((Q, HC), F32),
            h2f=((T, D), BF), dyf=((T, D), BF), af=((2, T, D), BF),
            wi1=((NF, 4 * U, HC), BF), wi2=((NF, 2 * U, HC), BF), wi3=((NF, U, HC), BF),
            go1=((4 * U, HC), BF), go2=((2 * U, HC), BF), go3=((U, HC), BF),
            gq1=((4 * U, HC), BF), gq2=((2 * U, HC), BF), gq3=((U, HC), BF),
            gk1=((4 * U, HC), BF), gk2=((2 * U, HC), BF), gk3=((U, HC), BF),
            gva1=((4 * U, VW), BF), gva2=((2 * U, VW), BF), gva3=((U, VW), BF),
            gvb1=((4 * U, HC - VW), BF), gvb2=((2 * U, HC - VW), BF), gvb3=((U, HC - VW), BF),
            gg1=((4 * U, GN), BF), gg2=((2 * U, GN), BF), gg3=((U, GN), BF),
            ge1=((4 * EB, H), BF), ge2=((2 * EB, H), BF), ge3=((EB, H), BF),
            fin=((U, NF * HC + 4 * HC + GN), F32), finr=((U // 2, NF * HC + 4 * HC + GN), F32),
        )
    counts = dict(
        x_seg=1, x_e=1, x_x=1, x_dy=1, c_pk=1, c_pv=1, c_h1t=1, c_h2t=1, c_dy=1, c_ctt=1, c_at=NF, c_du=NF, c_dm=1,
        c_ds=D // 256, c_g=3, y_wb=NF, wi=3 * NF, hi_wb=1, l_dy=1, x_dyf=1, l_h2=2, x_h2=2, c_finb=1, go=3, gq=3, gk=3, gva=3, gvb=3, gg=3, ge=3, c_fin=2,
    )
    sl, count = SimpleNamespace(), 0
    for name, n in counts.items():
        setattr(sl, name, count)
        count += n
    scratch.update((staged(n), v) for n, v in outs.items() if n[0] == "o")
    names = [*inputs, *outs, *scratch]

    def body(*refs):
        r = SimpleNamespace(**dict(zip(names, refs)))
        r.osem, r.lsem, r.ssem, r.rsem = refs[len(names) :]
        layer_body(fused, r, sl)

    res = pl.pallas_call(
        body,
        out_shape=[jax.ShapeDtypeStruct(sh, dt) for sh, dt in outs.values()],
        in_specs=[pl.BlockSpec(memory_space=pltpu.VMEM if v else pl.ANY) for _, v in inputs.values()],
        out_specs=[pl.BlockSpec(memory_space=pl.ANY if n[0] == "o" else pltpu.VMEM) for n in outs],
        scratch_shapes=[pltpu.VMEM(sh, dt) for sh, dt in scratch.values()]
        + [pltpu.SemaphoreType.DMA((10,))]
        + [pltpu.SemaphoreType.DMA((13,)), pltpu.SemaphoreType.DMA((count,)), pltpu.SemaphoreType.DMA((count,))],
        compiler_params=pltpu.CompilerParams(
            collective_id=0, has_side_effects=True, vmem_limit_bytes=60 * 1024 * 1024
        ),
        cost_estimate=pl.CostEstimate(flops=12 * 10**9, bytes_accessed=24 * 10**6, transcendentals=2 * 10**6),
    )(*[v for v, _ in inputs.values()])
    o = SimpleNamespace(**dict(zip(outs, res)))
    if fused:
        src = dict(s_layer=o.o_layer, s_x=o.o_x, s_q=o.o_q, s_k=o.o_k, s_v=o.o_v, s_out=o.o_out, s_in=o.o_in,
                   s_back=o.o_back, s_e=o.o_e, s_g=o.o_g)
        n_copy = len(src) - 1
        dst = dict(
            d_layer=((rows, H, D), BF), d_x=((rows, H, D), F32), d_q=((U // 2, D), F32), d_k=((U // 2, D), F32),
            d_v=((U // 2, D), F32), d_out=((U // 2, D), F32), d_in=((U // 2, FF), F32), d_back=((Q, D), F32),
            d_e=((EB, H), F32), d_ga=((U // 2,), F32), d_gf=((U // 2,), F32),
        )

        def tail(*refs):
            r = SimpleNamespace(**dict(zip([*src, *dst], refs)))
            r.sem = refs[-1]
            r.d_layer, r.d_x = r.d_layer.at[0], r.d_x.at[0]
            pairs = list(zip(vars(r).values(), list(vars(r).values())[len(src) :]))[:n_copy]
            hand_over(r, pairs)

        res = pl.pallas_call(
            tail,
            out_shape=[jax.ShapeDtypeStruct(sh, dt) for sh, dt in dst.values()],
            in_specs=[pl.BlockSpec(memory_space=pl.ANY)] * n_copy + [pl.BlockSpec(memory_space=pltpu.VMEM)],
            out_specs=[pl.BlockSpec(memory_space=pltpu.VMEM)] * len(dst),
            scratch_shapes=[pltpu.SemaphoreType.DMA((n_copy,))],
        )(*src.values())
        o = SimpleNamespace(**dict(zip(dst, res)))
        return o.d_layer, o.d_x, o.d_ga, o.d_q, o.d_k, o.d_v, o.d_out, o.d_gf, o.d_in, o.d_back, o.d_e.T

    layer = o.o_layer.reshape(rows, H, D)
    x_grad = o.o_x.reshape(rows, H, D)

    s = lax.axis_index(SEQ)
    x, c = s // 2, s % 2
    both = (DP, SEQ)

    def scatter(v):
        return lax.psum_scatter(v, both, scatter_dimension=0, tiled=True)

    def rows_back(v, y_first):
        v = v.astype(F32).reshape(2, 2, 2, U, v.shape[-1])
        v = v.transpose(2, 1, 0, 3, 4) if y_first else v.transpose(2, 0, 1, 3, 4)
        return v.reshape(8, U, v.shape[-1])

    def whole(v, y_first):
        v = rows_back(v, y_first)
        full = jnp.zeros((8, 2, U, 2, HC), F32)
        full = lax.dynamic_update_slice(full, v[:, None, :, None, :], (0, x, 0, c, 0))
        return full.reshape(D, 2 * HC)

    wi = jnp.stack([whole(o.wi[f], True) for f in range(NF)], axis=1).reshape(D, FF)
    wo = whole(o.go, True)
    gv = jnp.concatenate([o.gva, o.gvb], axis=1)
    wqkv = [whole(o.gq, True), whole(o.gk, True), whole(gv, True)]
    gains = rows_back(o.gg, True)
    gfull = lax.dynamic_update_slice(jnp.zeros((8, 2, U, 128), F32), gains[:, None], (0, x, 0, 0)).reshape(D, 128)
    wb = o.wb.astype(F32).reshape(NF * 2, 1, 2 * Q, 1, HC)
    wb = lax.dynamic_update_slice(jnp.zeros((NF * 2, 2, 2 * Q, 2, HC), F32), wb, (0, x, 0, c, 0)).reshape(FF, D)
    ge = o.ge.astype(F32).reshape(2, 2, 2, EB, H).transpose(2, 0, 1, 3, 4).reshape(J, H).T
    return (
        layer, x_grad, scatter(gfull[:, 0]), scatter(wqkv[0]), scatter(wqkv[1]), scatter(wqkv[2]), scatter(wo),
        scatter(gfull[:, 1]), scatter(wi), scatter(wb), lax.psum_scatter(ge, DP, scatter_dimension=1, tiled=True),
    )


def solution(mesh):
    shape = (mesh.shape[DP], mesh.shape[SEQ])
    both = (DP, SEQ)
    in_specs = (
        P(DP, SEQ, None), P(DP, SEQ), P(DP, None), P(SEQ, None),
        P(), P(), P(), P(), P(), P(), P(), P(), P(DP, SEQ, None),
    )
    out_specs = (
        P(DP, SEQ, None), P(DP, SEQ, None), P(both), P(both, None), P(both, None), P(both, None),
        P(both, None), P(both), P(both, None), P(both, None), P(SEQ, DP),
    )
    return jax.shard_map(
        functools.partial(run_layer, shape), mesh=mesh, in_specs=in_specs, out_specs=out_specs, check_vma=False
    )
```

```python
import functools
from types import SimpleNamespace

import jax
import jax.numpy as jnp
import numpy as np
from jax import lax
from jax.experimental import pallas as pl
from jax.experimental.pallas import tpu as pltpu
from jax.sharding import PartitionSpec as P

HEAD_DIM = 64
DP, SEQ = "dp", "seq"
YLH, LYH = "ylh", "lyh"
BF = jnp.bfloat16
F32 = jnp.float32
MESH = pl.DeviceIdType.MESH
GELU_C = 0.7978845608028654
GELU_K = 0.044715


def nn(a, b):
    return lax.dot_general(a, b, (((1,), (0,)), ((), ())), preferred_element_type=F32)


def tn(a, b):
    return lax.dot_general(a, b, (((0,), (0,)), ((), ())), preferred_element_type=F32)


def nt(a, b):
    return lax.dot_general(a, b, (((1,), (1,)), ((), ())), preferred_element_type=F32)


def selections(d_model, ff):
    unit = d_model // 16
    sel_a = np.zeros((2, d_model // 2, d_model), np.float32)
    for x in range(2):
        for b in range(8):
            j = 4 * (b % 2) + 2 * ((b // 2) % 2) + b // 4
            for o in range(unit):
                sel_a[x, b * unit + o, (2 * j + x) * unit + o] = 1
    q = ff // 32
    sel_c = np.zeros((2, 4 * q, ff // 4), np.float32)
    for x in range(2):
        for b in range(4):
            for o in range(q):
                sel_c[x, b * q + o, (b // 2 * 4 + x * 2 + b % 2) * q + o] = 1
    return sel_a, sel_c


def layer_body(fused, r, sl):
    d, s = lax.axis_index(DP), lax.axis_index(SEQ)
    x, c = s // 2, s % 2
    y, lo, hi = d % 2, (d // 2) % 2, d // 4
    to_core = (d, s + 1 - 2 * c)
    to_x = (d, s + 2 - 4 * x)
    to_y = (d + 1 - 2 * y, s)
    to_lo = (d + 2 - 4 * lo, s)
    to_hi = (d + 4 - 8 * hi, s)
    lsem, ssem, rsem = r.lsem, r.ssem, r.rsem
    D = r.h1.shape[1]
    T = r.h1.shape[0]
    H = T // 2
    J = r.sk.shape[0]
    FC = D
    NF = r.w_in.shape[1] // FC
    HC = D // 2
    U = D // 16
    Q = r.wb.shape[1] // 4
    scale = HEAD_DIM ** (-0.5)

    loads = []

    def load(src, dst):
        cp = pltpu.make_async_copy(src, dst, lsem.at[len(loads)])
        loads.append(cp)
        cp.start()
        return cp

    def rc(i, src, dst, dev):
        return pltpu.make_async_remote_copy(
            src_ref=src, dst_ref=dst, send_sem=ssem.at[i], recv_sem=rsem.at[i], device_id=dev, device_id_type=MESH
        )

    partners = [to_core, to_x] + ([to_y, to_lo, to_hi] if fused else [])
    barrier = pltpu.get_barrier_semaphore()
    for dev in partners:
        pl.semaphore_signal(barrier, inc=1, device_id=dev, device_id_type=MESH)
    l_x = load(r.x_in, r.xb.at[pl.ds(0, H)])
    l_seg = load(r.seg_in, r.segs.at[0])
    l_slot = load(r.slot_in, r.slot)
    l_e = load(r.e_in, r.eb.at[pl.ds(0, H)])
    l_wq = load(r.wq_in, r.wq)
    l_wk = load(r.wk_in, r.wk)
    l_wv = load(r.wv_in, r.wv)
    l_dy = load(r.dy_in, r.dyb.at[pl.ds(0, H)])
    l_sa = load(r.sa_in.at[x], r.sa)
    l_wo = load(r.wo_in, r.wo)
    l_sc = load(r.sc_in.at[x], r.sc)
    l_w_in = load(r.w_in_in, r.w_in)
    l_w_back = load(r.w_back_in, r.w_back)

    pl.semaphore_wait(barrier, len(partners))

    x_seg = rc(sl.x_seg, r.seg_in, r.segs.at[1], to_x)
    x_e = rc(sl.x_e, r.e_in, r.eb.at[pl.ds(H, H)], to_x)
    x_x = rc(sl.x_x, r.x_in, r.xb.at[pl.ds(H, H)], to_x)
    x_dy = rc(sl.x_dy, r.dy_in, r.dyb.at[pl.ds(H, H)], to_x)
    x_x.start()
    if fused:
        own_rows, far_rows = pl.ds(0, H), pl.ds(H, H)
        l_dyf = rc(sl.l_dy, r.dy_in, r.dyf.at[own_rows], to_lo)
        x_dyf = rc(sl.x_dyf, r.dyf.at[own_rows], r.dyf.at[far_rows], to_x)
        l_dyf.start()

    rows_i = lax.broadcasted_iota(jnp.int32, (T, T), 0)
    cols_i = lax.broadcasted_iota(jnp.int32, (T, T), 1)
    eye = jnp.where(rows_i == cols_i, 1.0, 0.0).astype(BF)
    r.eye[...] = eye
    ga = r.ga[...].astype(F32).reshape(1, D)
    gf = r.gf[...].astype(F32).reshape(1, D)
    inv_d = 1.0 / D
    NR = 64

    def norm_rows(v):
        cen = v - jnp.sum(v, axis=1, keepdims=True) * inv_d
        rstd = lax.rsqrt(jnp.sum(cen * cen, axis=1, keepdims=True) * inv_d + 1e-5)
        return cen * rstd, rstd

    def norm_into(src, gain, xh_ref, rs_ref, h_ref, start, count):
        for i in range(start // NR, (start + count) // NR):
            rows = slice(i * NR, (i + 1) * NR)
            xh, rstd = norm_rows(src[rows, :].astype(F32))
            xh_ref[rows, :] = xh
            rs_ref[rows, :] = jnp.broadcast_to(rstd, (NR, 128))
            h_ref[rows, :] = (xh * gain).astype(BF)

    l_x.wait()
    norm_into(r.xb, ga, r.xh1, r.rs1, r.h1, 0, H)
    x_seg.start()
    x_e.start()
    l_slot.wait()
    slot_row = r.slot[...].astype(F32)
    slot_col = nt(eye, jnp.broadcast_to(slot_row, (T, J)).astype(BF))
    l_wq.wait()
    l_wk.wait()
    l_wv.wait()
    own, far = slice(0, H), slice(H, T)
    r.k[own, :] = nn(r.h1[own, :], r.wk[...]).astype(BF)
    r.v[own, :] = nn(r.h1[own, :], r.wv[...]).astype(BF)
    r.q[own, :] = nn(r.h1[own, :], r.wq[...]).astype(BF)
    l_e.wait()
    l_sa.wait()
    l_seg.wait()

    def masks(part, at):
        row = r.segs[part].astype(F32)
        col = nt(eye[0:H, 0:H], jnp.broadcast_to(row, (J, H)).astype(BF))
        r.sel_t[:, at] = jnp.where(slot_col[:, 0:H] == row, 1.0, 0.0)
        r.me[at, :] = jnp.where(col == slot_row, r.eb[at, :].astype(F32), 0.0).astype(BF)
        r.met[:, at] = nt(eye, r.me[at, :]).astype(BF)

    masks(0, own)
    x_x.wait()
    x_dy.start()
    norm_into(r.xb, ga, r.xh1, r.rs1, r.h1, H, H)
    r.k[far, :] = nn(r.h1[far, :], r.wk[...]).astype(BF)

    x_seg.wait()
    x_e.wait()
    masks(1, far)

    c_pk = rc(sl.c_pk, r.pk.at[0], r.pkr.at[0], to_core)
    c_pv = rc(sl.c_pv, r.pk.at[1], r.pkr.at[1], to_core)
    r.pk[0] = nn(r.met[...], r.k[...]).astype(BF)
    c_pk.start()
    r.v[far, :] = nn(r.h1[far, :], r.wv[...]).astype(BF)
    r.pk[1] = nn(r.met[...], r.v[...]).astype(BF)
    c_pv.start()
    r.q[far, :] = nn(r.h1[far, :], r.wq[...]).astype(BF)
    c_h1t = rc(sl.c_h1t, r.h1t.at[0], r.h1t.at[1], to_core)

    lane = lax.broadcasted_iota(jnp.int32, (T, 128), 1)
    head_mask = [jnp.where(lane < 64, 1.0, 0.0).astype(BF), jnp.where(lane < 64, 0.0, 1.0).astype(BF)]

    NP = D // 128

    def fwd_raw(i):
        cols = slice(i * 128, (i + 1) * 128)
        q2 = r.q[:, cols]
        return nt(r.sk[:, cols], jnp.concatenate([q2 * head_mask[0], q2 * head_mask[1]], axis=0))

    def fwd_soft(i, raw):
        for m in range(2 * T // 128):
            h, tc = m * 128 // T, slice(m * 128 % T, m * 128 % T + 128)
            sc = jnp.where(r.sel_t[:, tc] > 0.5, raw[:, m * 128 : (m + 1) * 128] * scale, -1e30)
            e = jnp.exp(sc - jnp.max(sc, axis=0, keepdims=True))
            r.pt[i, h * J : (h + 1) * J, tc] = (e * (1.0 / jnp.sum(e, axis=0, keepdims=True))).astype(BF)

    def fwd_ctx(i):
        cols = slice(i * 128, (i + 1) * 128)
        sv2 = r.sv[:, cols]
        stack = jnp.concatenate([sv2 * head_mask[0], sv2 * head_mask[1]], axis=0)
        r.ctx[:, cols] = tn(r.pt[i], stack).astype(BF)

    c_pk.wait()
    r.sk[...] = (r.pk[0].astype(F32) + r.pkr[0].astype(F32)).astype(BF)
    raw = fwd_raw(0)
    for i in range(NP):
        nxt = fwd_raw(i + 1) if i + 1 < NP else None
        fwd_soft(i, raw)
        if i == 0:
            c_pv.wait()
            r.sv[...] = (r.pk[1].astype(F32) + r.pkr[1].astype(F32)).astype(BF)
        if i > 0:
            fwd_ctx(i - 1)
        raw = nxt
    fwd_ctx(NP - 1)

    if fused:
        l_dyf.wait()
        x_dyf.start()

    def l_h2(p):
        rows = pl.ds(p * NR, NR)
        return rc(sl.l_h2 + p, r.h2.at[rows], r.h2f.at[rows], to_lo)

    def x_h2(p):
        return rc(sl.x_h2 + p, r.h2f.at[pl.ds(p * NR, NR)], r.h2f.at[pl.ds(H + p * NR, NR)], to_x)

    l_wo.wait()
    for rows in (own, far):
        r.mid[rows, :] = r.xb[rows, :].astype(F32) + nn(r.ctx[rows, :], r.wo[...])
    norm_into(r.mid, gf, r.xh2, r.rs2, r.h2, 0, H)
    if fused:
        for p in range(H // NR):
            l_h2(p).start()
    norm_into(r.mid, gf, r.xh2, r.rs2, r.h2, H, H)
    x_dy.wait()
    l_dy.wait()
    c_dy = rc(sl.c_dy, r.dyh.at[1 - c], r.dyr, to_core)
    l_w_in.wait()
    l_w_back.wait()
    l_sc.wait()
    c_h2t = rc(sl.c_h2t, r.h2t.at[0], r.h2t.at[1], to_core)
    c_ctt = rc(sl.c_ctt, r.ctt.at[0], r.ctt.at[1], to_core)

    def c_at(k):
        return rc(sl.c_at + k, r.at.at[k], r.atr.at[k], to_core)

    def c_du(f):
        return rc(sl.c_du + f, r.du.at[f, 1 - c], r.dur.at[f], to_core)

    def y_wb(k):
        return rc(sl.y_wb + k, r.wb.at[k, rows16((1 - y) * 2 * Q, 2 * Q)], r.wb1.at[k], to_y)

    bits = dict(y=(y, to_y), l=(lo, to_lo), h=(hi, to_hi))

    def span(order, unit, stage):
        start, n = 0, 4 * unit
        for i in range(stage + 1):
            bit = bits[order[i]][0]
            kept, sent = start + bit * n, start + (1 - bit) * n
            if i < stage:
                start, n = kept, n // 2
        return kept, sent, n

    def rows16(start, n):
        return pl.ds(pl.multiple_of(start, 16), n)

    GN = 128
    VW = 256
    EB = J // 8
    if fused:
        chain_w = [
            (LYH if k in (1, 3) else YLH, r.wi.at[k], (r.wi1.at[k], r.wi2.at[k], r.wi3.at[k]), sl.wi + 3 * k, U)
            for k in range(NF)
        ]
        chain_o = (LYH, r.go, (r.go1, r.go2, r.go3), sl.go, U)
        chain_q = (LYH, r.gq, (r.gq1, r.gq2, r.gq3), sl.gq, U)
        chain_k = (YLH, r.gk, (r.gk1, r.gk2, r.gk3), sl.gk, U)
        chain_va = (YLH, r.gva, (r.gva1, r.gva2, r.gva3), sl.gva, U)
        chain_vb = (LYH, r.gvb, (r.gvb1, r.gvb2, r.gvb3), sl.gvb, U)
        chain_g = (YLH, r.gg, (r.gg1, r.gg2, r.gg3), sl.gg, U)
        chain_e = (LYH, r.ge, (r.ge1, r.ge2, r.ge3), sl.ge, EB)

    def add_into(dst, idx, src):
        dst[idx] = (dst[idx].astype(F32) + src.astype(F32)).astype(BF)

    def hi_wb():
        return rc(sl.hi_wb, r.wb.at[1 - hi, rows16(y * 2 * Q, 2 * Q)], r.wb2, to_hi)

    def pump_wb(k):
        if k < 2:
            y_wb(k).wait()
            add_into(r.wb, (k, rows16(y * 2 * Q, 2 * Q), slice(None)), r.wb1[k])

            @pl.when(hi == 1 - k)
            def _():
                hi_wb().start()
        else:
            l_h2(k - 2).wait()
            x_h2(k - 2).start()

    def pump(steps):
        for step in steps:
            if step[0] is None:
                pump_wb(step[1])
            else:
                st_next(step[0], step[1])

    def st_copy(chain, stage):
        order, buf, got, slot, unit = chain
        _, sent, n = span(order, unit, stage)
        return rc(slot + stage, buf.at[rows16(sent, n)], got[stage], bits[order[stage]][1])

    def st_next(chain, stage):
        order, buf, got, _, unit = chain
        st_copy(chain, stage).wait()
        kept, _, n = span(order, unit, stage)
        add_into(buf, (rows16(kept, n), slice(None)), got[stage][...])
        st_copy(chain, stage + 1).start()

    def st_last(chain):
        order, buf, got, _, unit = chain
        st_copy(chain, 2).wait()
        kept, _, n = span(order, unit, 2)
        return buf[rows16(kept, n), :].astype(F32) + got[2][...].astype(F32)

    def swap_rows(buf, cols, val, unit):
        q = 2 * unit
        for b in range(4):
            to = (b % 2) * 2 + b // 2
            buf[to * q : (to + 1) * q, cols] = val[b * q : (b + 1) * q, :].astype(BF)

    SB = 256
    GR = 32

    if fused:
        b0, b1, h0, h1 = [(None, k) for k in range(4)]
        w0, w1, w2, w3 = chain_w
        FFN_PUMPS = [[], [], [h0], [h1]]
        MID_PUMPS = [[(w0, 0)], [(w1, 0)]]
        ATT_PUMPS = [[(w2, 0)], [(w0, 1), (w3, 0)], [], [], [(w1, 1)], []]
        KV_PUMPS = [[(chain_o, 0)], [], [(w2, 1), b0]]
        END_PUMPS = [(w3, 1), b1, (chain_q, 0), (chain_vb, 0), (chain_e, 0), (chain_o, 1), (chain_k, 0), (chain_va, 0), (chain_g, 0), (chain_k, 1), (chain_q, 1), (chain_va, 1), (chain_vb, 1), (chain_e, 1), (chain_g, 1)]

    def swapped(buf, val, order, unit):
        if order == YLH:
            buf[...] = val.astype(BF)
        else:
            swap_rows(buf, slice(0, val.shape[1]), val, unit)

    def dense(k):
        wi = nn(r.h2t[0], r.du[k, c]) + nn(r.h2t[1], r.dur[k])
        if fused:
            swapped(chain_w[k][1], wi, chain_w[k][0], U)
        else:
            r.wi[k] = wi.astype(BF)

    def send_dense(k):
        if fused:
            st_copy(chain_w[k], 0).start()

    NW = r.wb.shape[0]

    def act_rows():
        for h in range(2):
            r.dyh[h, 0:T, :] = r.dyb[:, h * HC : (h + 1) * HC]
        if fused:
            x_dyf.wait()
            for h in range(2):
                r.dyh[h, T : 2 * T, :] = r.dyf[:, h * HC : (h + 1) * HC]
        c_dy.start()
        if fused:
            for p in range(H // NR):
                x_h2(p).wait()
            for k in range(NW):
                for b in range(NB):
                    cols = slice(b * SB, (b + 1) * SB)
                    u = nn(r.h2f[...], r.w_in[:, pl.ds(pl.multiple_of((lo + 2 * k) * FC + b * SB, SB), SB)])
                    for m in range(T // GR):
                        rr = slice(m * GR, (m + 1) * GR)
                        um = u[rr, :]
                        th = jnp.tanh(um * (GELU_C + (GELU_C * GELU_K) * (um * um)))
                        r.af[k, rr, cols] = (um * (0.5 + 0.5 * th)).astype(BF)
        for k in range(NW):
            r.at[k, :, 0:T] = nt(r.sc[...], r.a[lo + 2 * k if fused else k]).astype(BF)
            if fused:
                r.at[k, :, T : 2 * T] = nt(r.sc[...], r.af[k]).astype(BF)
            c_at(k).start()

    def grad_wb():
        c_dy.wait()
        for k in range(NW):
            c_at(k).wait()
        for k in range(NW):
            r.wb[k] = (nn(r.at[k], r.dyh[c]) + nn(r.atr[k], r.dyr[...])).astype(BF)
        if fused:
            for k in range(NW):
                y_wb(k).start()

    def back(k):
        rows = slice(k * FC, (k + 1) * FC)
        part_d = nt(r.duf[k % 2], r.w_in[:, rows])
        part_o = nn(r.a[k, 0:H, :], r.w_back[rows, :])
        if k == 0:
            r.oacc[...] = part_o
            r.dacc[...] = part_d
        else:
            r.oacc[...] += part_o
            r.dacc[...] += part_d

    NB = FC // SB

    def hidden(k, b):
        off = k * FC + b * SB
        cols = slice(b * SB, (b + 1) * SB)
        r.u[k % 2, :, cols] = nn(r.h2[...], r.w_in[:, off : off + SB])
        r.g[k % 2, :, cols] = nt(r.dyb[...], r.w_back[off : off + SB, :])

    def gelu(k, b):
        cols = slice(b * SB, (b + 1) * SB)
        for m in range(T // GR):
            rr = slice(m * GR, (m + 1) * GR)
            um = r.u[k % 2, rr, cols]
            u2 = um * um
            th = jnp.tanh(um * (GELU_C + (GELU_C * GELU_K) * u2))
            half = 0.5 + 0.5 * th
            act = um * half
            r.a[k, rr, cols] = act.astype(BF)
            slope = half + act * ((1.0 - th) * (GELU_C + (3.0 * GELU_C * GELU_K) * u2))
            r.duf[k % 2, rr, cols] = (slope * r.g[k % 2, rr, cols]).astype(BF)

    for b in range(NB):
        hidden(0, b)
    for k in range(NF):
        for b in range(NB):
            if k + 1 < NF:
                hidden(k + 1, b)
            gelu(k, b)
        if k > 0:
            back(k - 1)
            if fused:
                pump(FFN_PUMPS[k])
            if k == 1:
                c_h2t.wait()
            c_du(k - 1).wait()
            dense(k - 1)
        else:
            r.h2t[0] = nt(r.sa[...], r.h2[...]).astype(BF)
        r.du[k, 0] = r.duf[k % 2, :, 0:HC]
        r.du[k, 1] = r.duf[k % 2, :, HC : 2 * HC]
        c_du(k).start()
        if k > 0:
            send_dense(k - 1)
        else:
            c_h2t.start()
    back(NF - 1)
    r.ctt[0] = nt(r.sa[...], r.ctx[...]).astype(BF)
    r.h1t[0] = nt(r.sa[...], r.h1[...]).astype(BF)
    c_ctt.start()
    c_h1t.start()

    c_du(NF - 1).wait()
    dense(NF - 1)
    if fused:
        pump(MID_PUMPS[0])
    gsum = None
    for i in range(T // NR):
        rows = slice(i * NR, (i + 1) * NR)
        dn, xh = r.dacc[rows, :], r.xh2[rows, :]
        part = jnp.sum(dn * xh, axis=0, keepdims=True)
        gsum = part if gsum is None else gsum + part
        dg = dn * gf
        m1 = jnp.sum(dg, axis=1, keepdims=True) * inv_d
        m2 = jnp.sum(dg * xh, axis=1, keepdims=True) * inv_d
        dmid = r.dyb[rows, :].astype(F32) + r.rs2[rows, 0:1] * (dg - m1 - xh * m2)
        r.dmid[rows, :] = dmid
        b = dmid.astype(BF)
        r.dmb[0, rows, :] = b[:, 0:HC]
        r.dmb[1, rows, :] = b[:, HC : 2 * HC]
    r.gvec[1:2, :] = gsum
    c_dm = rc(sl.c_dm, r.dmb.at[1 - c], r.dmr, to_core)
    c_dm.start()
    send_dense(NF - 1)
    r.dctx[...] = (nt(r.dmb[0], r.wo[:, 0:HC]) + nt(r.dmb[1], r.wo[:, HC : 2 * HC])).astype(BF)
    r.s_layer[...] = (r.mid[0:H, :] + r.oacc[...]).astype(BF)
    outs = [pltpu.make_async_copy(r.s_layer, r.o_layer, r.osem.at[0]), pltpu.make_async_copy(r.s_x, r.o_x, r.osem.at[1])]
    outs[0].start()
    if fused:
        pump(MID_PUMPS[1])

    act_rows()

    def c_ds(g):
        pair = pl.ds(2 * g, 2)
        return rc(sl.c_ds + g, r.pd.at[pair], r.pdr.at[pair], to_core)

    def bwd_dp(i):
        cols = slice(i * 128, (i + 1) * 128)
        dc2 = r.dctx[:, cols]
        return nt(r.sv[:, cols], jnp.concatenate([dc2 * head_mask[0], dc2 * head_mask[1]], axis=0))

    def bwd_soft(i, dpf):
        for m in range(2 * T // 128):
            h, tc = m * 128 // T, slice(m * 128 % T, m * 128 % T + 128)
            pf = r.pt[i, h * J : (h + 1) * J, tc].astype(F32)
            dp = dpf[:, m * 128 : (m + 1) * 128]
            ds = pf * (dp - jnp.sum(pf * dp, axis=0, keepdims=True))
            r.draw[i % 2, h * J : (h + 1) * J, tc] = (ds * scale).astype(BF)

    def bwd_out(i):
        cols = slice(i * 128, (i + 1) * 128)
        q2, dc2, sk2 = r.q[:, cols], r.dctx[:, cols], r.sk[:, cols]
        draw = r.draw[i % 2]
        dsv = nn(r.pt[i, 0:J], dc2 * head_mask[0]) + nn(r.pt[i, J : 2 * J], dc2 * head_mask[1])
        dsk = nn(draw[0:J], q2 * head_mask[0]) + nn(draw[J : 2 * J], q2 * head_mask[1])
        r.pd[i, 0] = dsk.astype(BF)
        r.pd[i, 1] = dsv.astype(BF)
        stack = jnp.concatenate([sk2 * head_mask[0], sk2 * head_mask[1]], axis=0)
        r.dqkv[0, i // 3, :, (i % 3) * 128 : (i % 3 + 1) * 128] = tn(draw, stack).astype(BF)
        if i % 2:
            c_ds(i // 2).start()

    dpf = bwd_dp(0)
    for i in range(NP):
        nxt = bwd_dp(i + 1) if i + 1 < NP else None
        bwd_soft(i, dpf)
        if i > 0:
            bwd_out(i - 1)
        dpf = nxt
        if i == 0:
            c_ctt.wait()
            c_dm.wait()
            swapped(r.go, nn(r.ctt[0], r.dmb[c]) + nn(r.ctt[1], r.dmr[...]), LYH if fused else YLH, U)
            if fused:
                st_copy(chain_o, 0).start()
        if i == 1:
            grad_wb()
        if fused:
            pump(ATT_PUMPS[i])
    bwd_out(NP - 1)

    def c_g(i):
        return rc(sl.c_g + i, r.dqkv.at[i, 1 - c], r.dqr.at[i], to_core)

    c_g(0).start()
    r.dacc[...] = nt(r.dqkv[0, 0], r.wq[:, 0:HC]) + nt(r.dqkv[0, 1], r.wq[:, HC : 2 * HC])
    for i in range(D // 128):
        cols = slice(i * 128, (i + 1) * 128)
        if i % 2 == 0:
            c_ds(i // 2).wait()
        r.dsk[:, cols] = (r.pd[i, 0].astype(F32) + r.pdr[i, 0].astype(F32)).astype(BF)
        r.dsv[:, cols] = (r.pd[i, 1].astype(F32) + r.pdr[i, 1].astype(F32)).astype(BF)

    dk = nn(r.me[...], r.dsk[...]).astype(BF)
    dv = nn(r.me[...], r.dsv[...]).astype(BF)
    r.dqkv[1, 0] = dk[:, 0:HC]
    r.dqkv[1, 1] = dk[:, HC : 2 * HC]
    r.dqkv[2, 0] = dv[:, 0:HC]
    r.dqkv[2, 1] = dv[:, HC : 2 * HC]
    c_g(1).start()
    c_g(2).start()

    def wgrad(i):
        return (nn(r.h1t[0], r.dqkv[i, c]) + nn(r.h1t[1], r.dqr[i])).astype(BF)

    c_h1t.wait()
    c_g(0).wait()
    swapped(r.gq, wgrad(0), LYH if fused else YLH, U)
    if fused:
        st_copy(chain_q, 0).start()
        pump(KV_PUMPS[0])
    de = nt(r.dsk[...], r.k[0:H, :]) + nt(r.dsv[...], r.v[0:H, :])
    de = jnp.where(r.sel_t[:, 0:H] > 0.5, de, 0.0).astype(BF)
    for b in range(8):
        b2, b1, b0 = b // 4, (b // 2) % 2, b % 2
        j = 4 * b0 + 2 * b2 + b1
        r.ge[b * EB : (b + 1) * EB, :] = de[j * EB : (j + 1) * EB, :]
    c_g(1).wait()
    c_g(2).wait()
    swapped(r.gk, wgrad(1), YLH, U)
    gv = wgrad(2)
    swapped(r.gva, gv[:, 0:VW], YLH, U)
    swapped(r.gvb, gv[:, VW:HC], LYH if fused else YLH, U)
    if fused:
        st_copy(chain_k, 0).start()
        st_copy(chain_va, 0).start()
        st_copy(chain_vb, 0).start()
        st_copy(chain_e, 0).start()
        pump(KV_PUMPS[1])
    acc = r.dacc[...]
    for i, w in ((1, r.wk), (2, r.wv)):
        for hf in range(2):
            acc = acc + nt(r.dqkv[i, hf], w[:, hf * HC : (hf + 1) * HC])
    r.dacc[...] = acc

    gsum = None
    for i in range(T // NR):
        rows = slice(i * NR, (i + 1) * NR)
        dn, xh = r.dacc[rows, :], r.xh1[rows, :]
        part = jnp.sum(dn * xh, axis=0, keepdims=True)
        gsum = part if gsum is None else gsum + part
        if i < H // NR:
            dg = dn * ga
            m1 = jnp.sum(dg, axis=1, keepdims=True) * inv_d
            m2 = jnp.sum(dg * xh, axis=1, keepdims=True) * inv_d
            r.s_x[rows, :] = r.dmid[rows, :] + r.rs1[rows, 0:1] * (dg - m1 - xh * m2)
    outs[1].start()
    r.gvec[0:1, :] = gsum
    if fused:
        pump(KV_PUMPS[2])
    gains = jnp.concatenate([r.gvec[0:2, :], jnp.zeros((126, D), F32)], axis=0).astype(BF)
    r.gg[...] = nt(r.sa[...], gains).astype(BF)
    if fused:
        st_copy(chain_g, 0).start()

    if not fused:
        for cp in outs:
            cp.wait()
        return

    pump(END_PUMPS)

    fin = r.fin
    half = U // 2
    mine = pl.ds(pl.multiple_of(c * half, 8), half)
    first = (w0, w1, w2, w3, chain_o, chain_q, chain_k)
    homes = [(r.s_in, k * FC) for k in range(NF)] + [(r.s_out, 0), (r.s_q, 0), (r.s_k, 0), (r.s_v, 0)]
    n1 = len(first) * HC

    def send_out(src, dst):
        cp = pltpu.make_async_copy(src, dst, r.osem.at[len(outs)])
        cp.start()
        outs.append(cp)

    def c_fin(i):
        cols = pl.ds(0, n1) if i == 0 else pl.ds(n1, HC + GN)
        rows = pl.ds(pl.multiple_of((1 - c) * half, 8), half)
        return rc(sl.c_fin + i, fin.at[rows, cols], r.finr.at[:, cols], to_core)

    def put(i):
        dst, base = homes[i]
        at = i * HC
        dst[:, pl.ds(pl.multiple_of(base + c * HC, 128), HC)] = fin[mine, at : at + HC]
        dst[:, pl.ds(pl.multiple_of(base + (1 - c) * HC, 128), HC)] = r.finr[:, at : at + HC]

    def take(i):
        fin[:, i * HC : (i + 1) * HC] = st_last(first[i])

    for i in (0, 1, 2, 3):
        take(i)
    hi_wb().wait()
    r.finb[...] = r.wb[hi, rows16(y * 2 * Q, 2 * Q), :].astype(F32) + r.wb2[...].astype(F32)
    c_finb = rc(sl.c_finb, r.finb.at[pl.ds(pl.multiple_of((1 - c) * Q, 8), Q)], r.finbr, to_core)
    c_finb.start()
    for i in (4, 6):
        take(i)
    fin[:, n1 : n1 + VW] = st_last(chain_va)
    take(5)
    c_fin(0).start()
    fin[:, n1 + VW : n1 + HC] = st_last(chain_vb)
    r.s_e[...] = st_last(chain_e)
    send_out(r.s_e, r.o_e)
    fin[:, n1 + HC : n1 + HC + GN] = st_last(chain_g)
    c_fin(1).start()
    c_finb.wait()
    r.s_back[:, pl.ds(pl.multiple_of(c * HC, 128), HC)] = r.finb[pl.ds(pl.multiple_of(c * Q, 8), Q), :]
    r.s_back[:, pl.ds(pl.multiple_of((1 - c) * HC, 128), HC)] = r.finbr[...]
    send_out(r.s_back, r.o_back)
    c_fin(0).wait()
    for i in range(len(first)):
        put(i)
    for src, dst in ((r.s_in, r.o_in), (r.s_out, r.o_out), (r.s_q, r.o_q), (r.s_k, r.o_k)):
        send_out(src, dst)
    c_fin(1).wait()
    put(len(first))
    at = n1 + HC
    r.s_g[...] = fin[mine, at : at + 128] + r.finr[:, at : at + 128]
    send_out(r.s_v, r.o_v)
    send_out(r.s_g, r.o_g)
    for cp in outs:
        cp.wait()


def staged(name):
    return f"s{name[1:]}"


def hand_over(r, names):
    copies = []
    for i, (src, dst) in enumerate(names):
        cp = pltpu.make_async_copy(src, dst, r.sem.at[i])
        cp.start()
        copies.append(cp)
    g = jnp.concatenate([r.s_g[...], jnp.zeros((128 - r.s_g.shape[0], 128), F32)], axis=0).T
    n = r.s_g.shape[0]
    r.d_ga[...] = g[0, 0:n]
    r.d_gf[...] = g[1, 0:n]
    for cp in copies:
        cp.wait()


def run_layer(mesh_shape, tokens, seg_ids, slot_doc, proj_e, g_attn, w_query, w_key, w_value, w_out, g_ffn, w_in,
              w_back, cotangent):
    n_dp, n_seq = mesh_shape
    rows, H, D = tokens.shape
    J = proj_e.shape[1]
    FF = w_in.shape[1]
    fused = n_dp == 8
    T = 2 * H
    HC, U, NF, Q = D // 2, D // 16, FF // D, FF // 32
    EB = J // 8
    NW, TW = (2, 2 * T) if fused else (NF, T)
    GN, VW = 128, 256
    sel_a, sel_c = (jnp.asarray(m, BF) for m in selections(D, FF))

    inputs = dict(
        x_in=(tokens.reshape(H, D), False),
        seg_in=(seg_ids.reshape(1, H), False),
        slot_in=(slot_doc.reshape(1, J), False),
        e_in=(proj_e, False),
        ga=(g_attn, True),
        wq_in=(w_query, False),
        wk_in=(w_key, False),
        wv_in=(w_value, False),
        wo_in=(w_out, False),
        gf=(g_ffn, True),
        w_in_in=(w_in, False),
        w_back_in=(w_back, False),
        dy_in=(cotangent.reshape(H, D), False),
        sa_in=(sel_a, False),
        sc_in=(sel_c, False),
    )
    parts = dict(
        wb=((NW, 4 * Q, HC), BF),
        wi=((NF, D // 2, HC), BF),
        go=((D // 2, HC), BF),
        gq=((D // 2, HC), BF),
        gk=((D // 2, HC), BF),
        gva=((D // 2, VW), BF),
        gvb=((D // 2, HC - VW), BF),
        gg=((D // 2, GN), BF),
        ge=((J, H), BF),
    )
    outs = dict(o_layer=((H, D), BF), o_x=((H, D), F32))
    if fused:
        outs.update(
            o_g=((U // 2, 128), F32),
            o_q=((U // 2, D), F32),
            o_k=((U // 2, D), F32),
            o_v=((U // 2, D), F32),
            o_out=((U // 2, D), F32),
            o_in=((U // 2, FF), F32),
            o_back=((Q, D), F32),
            o_e=((EB, H), F32),
        )
    else:
        outs.update(parts)
    scratch = dict(
        xb=((T, D), BF), eb=((T, J), BF), segs=((2, 1, H), jnp.int32), slot=((1, J), jnp.int32),
        wq=((D, D), BF), wk=((D, D), BF), wv=((D, D), BF), wo=((D, D), BF),
        w_in=((D, FF), BF), w_back=((FF, D), BF),
        dyb=((T, D), BF), dyh=((2, TW, HC), BF), dyr=((TW, HC), BF),
        sa=((D // 2, D), BF), sc=((4 * Q, FF // 4), BF),
        eye=((T, T), BF),
        h1=((T, D), BF), xh1=((T, D), F32), rs1=((T, 128), F32),
        q=((T, D), BF), k=((T, D), BF), v=((T, D), BF),
        sel_t=((J, T), F32), me=((T, J), BF), met=((J, T), BF),
        pk=((2, J, D), BF), pkr=((2, J, D), BF), sk=((J, D), BF), sv=((J, D), BF),

        pt=((D // 128, 2 * J, T), BF), ctx=((T, D), BF),
        mid=((T, D), F32), xh2=((T, D), F32), rs2=((T, 128), F32), h2=((T, D), BF),
        h1t=((2, D // 2, T), BF), h2t=((2, D // 2, T), BF), ctt=((2, D // 2, T), BF),
        a=((NF, T, D), BF), duf=((2, T, D), BF), u=((2, T, D), F32), g=((2, T, D), F32), du=((NF, 2, T, HC), BF), dur=((NF, T, HC), BF),
        at=((NW, 4 * Q, TW), BF), atr=((NW, 4 * Q, TW), BF),
        oacc=((H, D), F32), dacc=((T, D), F32), dmid=((T, D), F32), gvec=((8, D), F32),
        dmb=((2, T, HC), BF), dmr=((T, HC), BF), dctx=((T, D), BF), draw=((2, 2 * J, T), BF),
        pd=((D // 128, 2, J, 128), BF), pdr=((D // 128, 2, J, 128), BF),
        dsk=((J, D), BF), dsv=((J, D), BF),
        dqkv=((3, 2, T, HC), BF), dqr=((3, T, HC), BF),
    )
    if fused:
        scratch.update(
            parts,
            wb1=((2, 2 * Q, HC), BF), wb2=((2 * Q, HC), BF), finb=((2 * Q, HC), F32), finbr=((Q, HC), F32),
            h2f=((T, D), BF), dyf=((T, D), BF), af=((2, T, D), BF),
            wi1=((NF, 4 * U, HC), BF), wi2=((NF, 2 * U, HC), BF), wi3=((NF, U, HC), BF),
            go1=((4 * U, HC), BF), go2=((2 * U, HC), BF), go3=((U, HC), BF),
            gq1=((4 * U, HC), BF), gq2=((2 * U, HC), BF), gq3=((U, HC), BF),
            gk1=((4 * U, HC), BF), gk2=((2 * U, HC), BF), gk3=((U, HC), BF),
            gva1=((4 * U, VW), BF), gva2=((2 * U, VW), BF), gva3=((U, VW), BF),
            gvb1=((4 * U, HC - VW), BF), gvb2=((2 * U, HC - VW), BF), gvb3=((U, HC - VW), BF),
            gg1=((4 * U, GN), BF), gg2=((2 * U, GN), BF), gg3=((U, GN), BF),
            ge1=((4 * EB, H), BF), ge2=((2 * EB, H), BF), ge3=((EB, H), BF),
            fin=((U, NF * HC + 4 * HC + GN), F32), finr=((U // 2, NF * HC + 4 * HC + GN), F32),
        )
    counts = dict(
        x_seg=1, x_e=1, x_x=1, x_dy=1, c_pk=1, c_pv=1, c_h1t=1, c_h2t=1, c_dy=1, c_ctt=1, c_at=NF, c_du=NF, c_dm=1,
        c_ds=D // 256, c_g=3, y_wb=NF, wi=3 * NF, hi_wb=1, l_dy=1, x_dyf=1, l_h2=2, x_h2=2, c_finb=1, go=3, gq=3, gk=3, gva=3, gvb=3, gg=3, ge=3, c_fin=2,
    )
    sl, count = SimpleNamespace(), 0
    for name, n in counts.items():
        setattr(sl, name, count)
        count += n
    scratch.update((staged(n), v) for n, v in outs.items() if n[0] == "o")
    names = [*inputs, *outs, *scratch]

    def body(*refs):
        r = SimpleNamespace(**dict(zip(names, refs)))
        r.osem, r.lsem, r.ssem, r.rsem = refs[len(names) :]
        layer_body(fused, r, sl)

    res = pl.pallas_call(
        body,
        out_shape=[jax.ShapeDtypeStruct(sh, dt) for sh, dt in outs.values()],
        in_specs=[pl.BlockSpec(memory_space=pltpu.VMEM if v else pl.ANY) for _, v in inputs.values()],
        out_specs=[pl.BlockSpec(memory_space=pl.ANY if n[0] == "o" else pltpu.VMEM) for n in outs],
        scratch_shapes=[pltpu.VMEM(sh, dt) for sh, dt in scratch.values()]
        + [pltpu.SemaphoreType.DMA((10,))]
        + [pltpu.SemaphoreType.DMA((13,)), pltpu.SemaphoreType.DMA((count,)), pltpu.SemaphoreType.DMA((count,))],
        compiler_params=pltpu.CompilerParams(
            collective_id=0, has_side_effects=True, vmem_limit_bytes=60 * 1024 * 1024
        ),
        cost_estimate=pl.CostEstimate(flops=12 * 10**9, bytes_accessed=24 * 10**6, transcendentals=2 * 10**6),
    )(*[v for v, _ in inputs.values()])
    o = SimpleNamespace(**dict(zip(outs, res)))
    if fused:
        src = dict(s_layer=o.o_layer, s_x=o.o_x, s_q=o.o_q, s_k=o.o_k, s_v=o.o_v, s_out=o.o_out, s_in=o.o_in,
                   s_back=o.o_back, s_e=o.o_e, s_g=o.o_g)
        n_copy = len(src) - 1
        dst = dict(
            d_layer=((rows, H, D), BF), d_x=((rows, H, D), F32), d_q=((U // 2, D), F32), d_k=((U // 2, D), F32),
            d_v=((U // 2, D), F32), d_out=((U // 2, D), F32), d_in=((U // 2, FF), F32), d_back=((Q, D), F32),
            d_e=((EB, H), F32), d_ga=((U // 2,), F32), d_gf=((U // 2,), F32),
        )

        def tail(*refs):
            r = SimpleNamespace(**dict(zip([*src, *dst], refs)))
            r.sem = refs[-1]
            r.d_layer, r.d_x = r.d_layer.at[0], r.d_x.at[0]
            pairs = list(zip(vars(r).values(), list(vars(r).values())[len(src) :]))[:n_copy]
            hand_over(r, pairs)

        res = pl.pallas_call(
            tail,
            out_shape=[jax.ShapeDtypeStruct(sh, dt) for sh, dt in dst.values()],
            in_specs=[pl.BlockSpec(memory_space=pl.ANY)] * n_copy + [pl.BlockSpec(memory_space=pltpu.VMEM)],
            out_specs=[pl.BlockSpec(memory_space=pltpu.VMEM)] * len(dst),
            scratch_shapes=[pltpu.SemaphoreType.DMA((n_copy,))],
        )(*src.values())
        o = SimpleNamespace(**dict(zip(dst, res)))
        return o.d_layer, o.d_x, o.d_ga, o.d_q, o.d_k, o.d_v, o.d_out, o.d_gf, o.d_in, o.d_back, o.d_e.T

    layer = o.o_layer.reshape(rows, H, D)
    x_grad = o.o_x.reshape(rows, H, D)

    s = lax.axis_index(SEQ)
    x, c = s // 2, s % 2
    both = (DP, SEQ)

    def scatter(v):
        return lax.psum_scatter(v, both, scatter_dimension=0, tiled=True)

    def rows_back(v, y_first):
        v = v.astype(F32).reshape(2, 2, 2, U, v.shape[-1])
        v = v.transpose(2, 1, 0, 3, 4) if y_first else v.transpose(2, 0, 1, 3, 4)
        return v.reshape(8, U, v.shape[-1])

    def whole(v, y_first):
        v = rows_back(v, y_first)
        full = jnp.zeros((8, 2, U, 2, HC), F32)
        full = lax.dynamic_update_slice(full, v[:, None, :, None, :], (0, x, 0, c, 0))
        return full.reshape(D, 2 * HC)

    wi = jnp.stack([whole(o.wi[f], True) for f in range(NF)], axis=1).reshape(D, FF)
    wo = whole(o.go, True)
    gv = jnp.concatenate([o.gva, o.gvb], axis=1)
    wqkv = [whole(o.gq, True), whole(o.gk, True), whole(gv, True)]
    gains = rows_back(o.gg, True)
    gfull = lax.dynamic_update_slice(jnp.zeros((8, 2, U, 128), F32), gains[:, None], (0, x, 0, 0)).reshape(D, 128)
    wb = o.wb.astype(F32).reshape(NF * 2, 1, 2 * Q, 1, HC)
    wb = lax.dynamic_update_slice(jnp.zeros((NF * 2, 2, 2 * Q, 2, HC), F32), wb, (0, x, 0, c, 0)).reshape(FF, D)
    ge = o.ge.astype(F32).reshape(2, 2, 2, EB, H).transpose(2, 0, 1, 3, 4).reshape(J, H).T
    return (
        layer, x_grad, scatter(gfull[:, 0]), scatter(wqkv[0]), scatter(wqkv[1]), scatter(wqkv[2]), scatter(wo),
        scatter(gfull[:, 1]), scatter(wi), scatter(wb), lax.psum_scatter(ge, DP, scatter_dimension=1, tiled=True),
    )


def solution(mesh):
    shape = (mesh.shape[DP], mesh.shape[SEQ])
    both = (DP, SEQ)
    in_specs = (
        P(DP, SEQ, None), P(DP, SEQ), P(DP, None), P(SEQ, None),
        P(), P(), P(), P(), P(), P(), P(), P(), P(DP, SEQ, None),
    )
    out_specs = (
        P(DP, SEQ, None), P(DP, SEQ, None), P(both), P(both, None), P(both, None), P(both, None),
        P(both, None), P(both), P(both, None), P(both, None), P(SEQ, DP),
    )
    return jax.shard_map(
        functools.partial(run_layer, shape), mesh=mesh, in_specs=in_specs, out_specs=out_specs, check_vma=False
    )
```

```python
import functools
from types import SimpleNamespace

import jax
import jax.numpy as jnp
import numpy as np
from jax import lax
from jax.experimental import pallas as pl
from jax.experimental.pallas import tpu as pltpu
from jax.sharding import PartitionSpec as P

HEAD_DIM = 64
DP, SEQ = "dp", "seq"
YLH, LYH = "ylh", "lyh"
BF = jnp.bfloat16
F32 = jnp.float32
MESH = pl.DeviceIdType.MESH
GELU_C = 0.7978845608028654
GELU_K = 0.044715


def nn(a, b):
    return lax.dot_general(a, b, (((1,), (0,)), ((), ())), preferred_element_type=F32)


def tn(a, b):
    return lax.dot_general(a, b, (((0,), (0,)), ((), ())), preferred_element_type=F32)


def nt(a, b):
    return lax.dot_general(a, b, (((1,), (1,)), ((), ())), preferred_element_type=F32)


def selections(d_model, ff):
    unit = d_model // 16
    sel_a = np.zeros((2, d_model // 2, d_model), np.float32)
    for x in range(2):
        for b in range(8):
            j = 4 * (b % 2) + 2 * ((b // 2) % 2) + b // 4
            for o in range(unit):
                sel_a[x, b * unit + o, (2 * j + x) * unit + o] = 1
    q = ff // 32
    sel_c = np.zeros((2, 4 * q, ff // 4), np.float32)
    for x in range(2):
        for b in range(4):
            for o in range(q):
                sel_c[x, b * q + o, (b // 2 * 4 + x * 2 + b % 2) * q + o] = 1
    return sel_a, sel_c


def layer_body(fused, r, sl):
    d, s = lax.axis_index(DP), lax.axis_index(SEQ)
    x, c = s // 2, s % 2
    y, lo, hi = d % 2, (d // 2) % 2, d // 4
    to_core = (d, s + 1 - 2 * c)
    to_x = (d, s + 2 - 4 * x)
    to_y = (d + 1 - 2 * y, s)
    to_lo = (d + 2 - 4 * lo, s)
    to_hi = (d + 4 - 8 * hi, s)
    lsem, ssem, rsem = r.lsem, r.ssem, r.rsem
    D = r.h1.shape[1]
    T = r.h1.shape[0]
    H = T // 2
    J = r.sk.shape[0]
    FC = D
    NF = r.w_in.shape[1] // FC
    HC = D // 2
    U = D // 16
    Q = r.wb.shape[1] // 4
    scale = HEAD_DIM ** (-0.5)

    loads = []

    def load(src, dst):
        cp = pltpu.make_async_copy(src, dst, lsem.at[len(loads)])
        loads.append(cp)
        cp.start()
        return cp

    def rc(i, src, dst, dev):
        return pltpu.make_async_remote_copy(
            src_ref=src, dst_ref=dst, send_sem=ssem.at[i], recv_sem=rsem.at[i], device_id=dev, device_id_type=MESH
        )

    partners = [to_core, to_x] + ([to_y, to_lo, to_hi] if fused else [])
    barrier = pltpu.get_barrier_semaphore()
    for dev in partners:
        pl.semaphore_signal(barrier, inc=1, device_id=dev, device_id_type=MESH)
    l_x = load(r.x_in, r.xb.at[pl.ds(0, H)])
    l_seg = load(r.seg_in, r.segs.at[0])
    l_slot = load(r.slot_in, r.slot)
    l_e = load(r.e_in, r.eb.at[pl.ds(0, H)])
    l_wq = load(r.wq_in, r.wq)
    l_wk = load(r.wk_in, r.wk)
    l_wv = load(r.wv_in, r.wv)
    l_dy = load(r.dy_in, r.dyb.at[pl.ds(0, H)])
    l_sa = load(r.sa_in.at[x], r.sa)
    l_wo = load(r.wo_in, r.wo)
    l_sc = load(r.sc_in.at[x], r.sc)
    l_w_in = load(r.w_in_in, r.w_in)
    l_w_back = load(r.w_back_in, r.w_back)

    pl.semaphore_wait(barrier, len(partners))

    x_seg = rc(sl.x_seg, r.seg_in, r.segs.at[1], to_x)
    x_e = rc(sl.x_e, r.e_in, r.eb.at[pl.ds(H, H)], to_x)
    x_x = rc(sl.x_x, r.x_in, r.xb.at[pl.ds(H, H)], to_x)
    x_dy = rc(sl.x_dy, r.dy_in, r.dyb.at[pl.ds(H, H)], to_x)
    x_x.start()
    if fused:
        own_rows, far_rows = pl.ds(0, H), pl.ds(H, H)
        l_dyf = rc(sl.l_dy, r.dy_in, r.dyf.at[own_rows], to_lo)
        x_dyf = rc(sl.x_dyf, r.dyf.at[own_rows], r.dyf.at[far_rows], to_x)
        l_dyf.start()

    rows_i = lax.broadcasted_iota(jnp.int32, (T, T), 0)
    cols_i = lax.broadcasted_iota(jnp.int32, (T, T), 1)
    eye = jnp.where(rows_i == cols_i, 1.0, 0.0).astype(BF)
    r.eye[...] = eye
    ga = r.ga[...].astype(F32).reshape(1, D)
    gf = r.gf[...].astype(F32).reshape(1, D)
    inv_d = 1.0 / D
    NR = 64

    def norm_rows(v):
        cen = v - jnp.sum(v, axis=1, keepdims=True) * inv_d
        rstd = lax.rsqrt(jnp.sum(cen * cen, axis=1, keepdims=True) * inv_d + 1e-5)
        return cen * rstd, rstd

    def norm_into(src, gain, xh_ref, rs_ref, h_ref, start, count):
        for i in range(start // NR, (start + count) // NR):
            rows = slice(i * NR, (i + 1) * NR)
            xh, rstd = norm_rows(src[rows, :].astype(F32))
            xh_ref[rows, :] = xh
            rs_ref[rows, :] = jnp.broadcast_to(rstd, (NR, 128))
            h_ref[rows, :] = (xh * gain).astype(BF)

    l_x.wait()
    norm_into(r.xb, ga, r.xh1, r.rs1, r.h1, 0, H)
    x_seg.start()
    x_e.start()
    l_slot.wait()
    slot_row = r.slot[...].astype(F32)
    slot_col = nt(eye, jnp.broadcast_to(slot_row, (T, J)).astype(BF))
    l_wq.wait()
    l_wk.wait()
    l_wv.wait()
    own, far = slice(0, H), slice(H, T)
    r.k[own, :] = nn(r.h1[own, :], r.wk[...]).astype(BF)
    r.v[own, :] = nn(r.h1[own, :], r.wv[...]).astype(BF)
    r.q[own, :] = nn(r.h1[own, :], r.wq[...]).astype(BF)
    l_e.wait()
    l_sa.wait()
    l_seg.wait()

    def masks(part, at):
        row = r.segs[part].astype(F32)
        col = nt(eye[0:H, 0:H], jnp.broadcast_to(row, (J, H)).astype(BF))
        r.sel_t[:, at] = jnp.where(slot_col[:, 0:H] == row, 1.0, 0.0)
        r.me[at, :] = jnp.where(col == slot_row, r.eb[at, :].astype(F32), 0.0).astype(BF)
        r.met[:, at] = nt(eye, r.me[at, :]).astype(BF)

    masks(0, own)
    x_x.wait()
    x_dy.start()
    norm_into(r.xb, ga, r.xh1, r.rs1, r.h1, H, H)
    r.k[far, :] = nn(r.h1[far, :], r.wk[...]).astype(BF)

    x_seg.wait()
    x_e.wait()
    masks(1, far)

    c_pk = rc(sl.c_pk, r.pk.at[0], r.pkr.at[0], to_core)
    c_pv = rc(sl.c_pv, r.pk.at[1], r.pkr.at[1], to_core)
    r.pk[0] = nn(r.met[...], r.k[...]).astype(BF)
    c_pk.start()
    r.v[far, :] = nn(r.h1[far, :], r.wv[...]).astype(BF)
    r.pk[1] = nn(r.met[...], r.v[...]).astype(BF)
    c_pv.start()
    r.q[far, :] = nn(r.h1[far, :], r.wq[...]).astype(BF)
    c_h1t = rc(sl.c_h1t, r.h1t.at[0], r.h1t.at[1], to_core)

    lane = lax.broadcasted_iota(jnp.int32, (T, 128), 1)
    head_mask = [jnp.where(lane < 64, 1.0, 0.0).astype(BF), jnp.where(lane < 64, 0.0, 1.0).astype(BF)]

    NP = D // 128

    def fwd_raw(i):
        cols = slice(i * 128, (i + 1) * 128)
        q2 = r.q[:, cols]
        return nt(r.sk[:, cols], jnp.concatenate([q2 * head_mask[0], q2 * head_mask[1]], axis=0))

    def fwd_soft(i, raw):
        for m in range(2 * T // 128):
            h, tc = m * 128 // T, slice(m * 128 % T, m * 128 % T + 128)
            sc = jnp.where(r.sel_t[:, tc] > 0.5, raw[:, m * 128 : (m + 1) * 128] * scale, -1e30)
            e = jnp.exp(sc - jnp.max(sc, axis=0, keepdims=True))
            r.pt[i, h * J : (h + 1) * J, tc] = (e * (1.0 / jnp.sum(e, axis=0, keepdims=True))).astype(BF)

    def fwd_ctx(i):
        cols = slice(i * 128, (i + 1) * 128)
        sv2 = r.sv[:, cols]
        stack = jnp.concatenate([sv2 * head_mask[0], sv2 * head_mask[1]], axis=0)
        r.ctx[:, cols] = tn(r.pt[i], stack).astype(BF)

    c_pk.wait()
    r.sk[...] = (r.pk[0].astype(F32) + r.pkr[0].astype(F32)).astype(BF)
    raw = fwd_raw(0)
    for i in range(NP):
        nxt = fwd_raw(i + 1) if i + 1 < NP else None
        fwd_soft(i, raw)
        if i == 0:
            c_pv.wait()
            r.sv[...] = (r.pk[1].astype(F32) + r.pkr[1].astype(F32)).astype(BF)
        if i > 0:
            fwd_ctx(i - 1)
        raw = nxt
    fwd_ctx(NP - 1)

    if fused:
        l_dyf.wait()
        x_dyf.start()

    def l_h2(p):
        rows = pl.ds(p * NR, NR)
        return rc(sl.l_h2 + p, r.h2.at[rows], r.h2f.at[rows], to_lo)

    def x_h2(p):
        return rc(sl.x_h2 + p, r.h2f.at[pl.ds(p * NR, NR)], r.h2f.at[pl.ds(H + p * NR, NR)], to_x)

    l_wo.wait()
    for rows in (own, far):
        r.mid[rows, :] = r.xb[rows, :].astype(F32) + nn(r.ctx[rows, :], r.wo[...])
    norm_into(r.mid, gf, r.xh2, r.rs2, r.h2, 0, H)
    if fused:
        for p in range(H // NR):
            l_h2(p).start()
    norm_into(r.mid, gf, r.xh2, r.rs2, r.h2, H, H)
    x_dy.wait()
    l_dy.wait()
    c_dy = rc(sl.c_dy, r.dyh.at[1 - c], r.dyr, to_core)
    l_w_in.wait()
    l_w_back.wait()
    l_sc.wait()
    c_h2t = rc(sl.c_h2t, r.h2t.at[0], r.h2t.at[1], to_core)
    c_ctt = rc(sl.c_ctt, r.ctt.at[0], r.ctt.at[1], to_core)

    def c_at(k):
        return rc(sl.c_at + k, r.at.at[k], r.atr.at[k], to_core)

    def c_du(f):
        return rc(sl.c_du + f, r.du.at[f, 1 - c], r.dur.at[f], to_core)

    def y_wb(k):
        return rc(sl.y_wb + k, r.wb.at[k, rows16((1 - y) * 2 * Q, 2 * Q)], r.wb1.at[k], to_y)

    bits = dict(y=(y, to_y), l=(lo, to_lo), h=(hi, to_hi))

    def span(order, unit, stage):
        start, n = 0, 4 * unit
        for i in range(stage + 1):
            bit = bits[order[i]][0]
            kept, sent = start + bit * n, start + (1 - bit) * n
            if i < stage:
                start, n = kept, n // 2
        return kept, sent, n

    def rows16(start, n):
        return pl.ds(pl.multiple_of(start, 16), n)

    GN = 128
    VW = 256
    EB = J // 8
    if fused:
        chain_w = [
            (LYH if k in (1, 3) else YLH, r.wi.at[k], (r.wi1.at[k], r.wi2.at[k], r.wi3.at[k]), sl.wi + 3 * k, U)
            for k in range(NF)
        ]
        chain_o = (LYH, r.go, (r.go1, r.go2, r.go3), sl.go, U)
        chain_q = (LYH, r.gq, (r.gq1, r.gq2, r.gq3), sl.gq, U)
        chain_k = (YLH, r.gk, (r.gk1, r.gk2, r.gk3), sl.gk, U)
        chain_va = (YLH, r.gva, (r.gva1, r.gva2, r.gva3), sl.gva, U)
        chain_vb = (LYH, r.gvb, (r.gvb1, r.gvb2, r.gvb3), sl.gvb, U)
        chain_g = (YLH, r.gg, (r.gg1, r.gg2, r.gg3), sl.gg, U)
        chain_e = (LYH, r.ge, (r.ge1, r.ge2, r.ge3), sl.ge, EB)

    def add_into(dst, idx, src):
        dst[idx] = (dst[idx].astype(F32) + src.astype(F32)).astype(BF)

    def hi_wb():
        return rc(sl.hi_wb, r.wb.at[1 - hi, rows16(y * 2 * Q, 2 * Q)], r.wb2, to_hi)

    def pump_wb(k):
        if k < 2:
            y_wb(k).wait()
            add_into(r.wb, (k, rows16(y * 2 * Q, 2 * Q), slice(None)), r.wb1[k])

            @pl.when(hi == 1 - k)
            def _():
                hi_wb().start()
        else:
            l_h2(k - 2).wait()
            x_h2(k - 2).start()

    def pump(steps):
        for step in steps:
            if step[0] is None:
                pump_wb(step[1])
            else:
                st_next(step[0], step[1])

    def st_copy(chain, stage):
        order, buf, got, slot, unit = chain
        _, sent, n = span(order, unit, stage)
        return rc(slot + stage, buf.at[rows16(sent, n)], got[stage], bits[order[stage]][1])

    def st_next(chain, stage):
        order, buf, got, _, unit = chain
        st_copy(chain, stage).wait()
        kept, _, n = span(order, unit, stage)
        add_into(buf, (rows16(kept, n), slice(None)), got[stage][...])
        st_copy(chain, stage + 1).start()

    def st_last(chain):
        order, buf, got, _, unit = chain
        st_copy(chain, 2).wait()
        kept, _, n = span(order, unit, 2)
        return buf[rows16(kept, n), :].astype(F32) + got[2][...].astype(F32)

    def swap_rows(buf, cols, val, unit):
        q = 2 * unit
        for b in range(4):
            to = (b % 2) * 2 + b // 2
            buf[to * q : (to + 1) * q, cols] = val[b * q : (b + 1) * q, :].astype(BF)

    SB = 256
    GR = 32

    if fused:
        b0, b1, h0, h1 = [(None, k) for k in range(4)]
        w0, w1, w2, w3 = chain_w
        FFN_PUMPS = [[], [], [h0], [h1]]
        MID_PUMPS = [[(w0, 0)], [(w1, 0)]]
        ATT_PUMPS = [[(w2, 0)], [(w0, 1), (w3, 0)], [], [], [(w1, 1)], []]
        KV_PUMPS = [[(chain_o, 0)], [b0, (w2, 1)], [b1, (chain_q, 0)]]
        END_PUMPS = [(w3, 1), (chain_vb, 0), (chain_e, 0), (chain_o, 1), (chain_k, 0), (chain_q, 1), (chain_va, 0), (chain_k, 1), (chain_g, 0), (chain_va, 1), (chain_vb, 1), (chain_e, 1), (chain_g, 1)]

    def swapped(buf, val, order, unit):
        if order == YLH:
            buf[...] = val.astype(BF)
        else:
            swap_rows(buf, slice(0, val.shape[1]), val, unit)

    def dense(k):
        wi = nn(r.h2t[0], r.du[k, c]) + nn(r.h2t[1], r.dur[k])
        if fused:
            swapped(chain_w[k][1], wi, chain_w[k][0], U)
        else:
            r.wi[k] = wi.astype(BF)

    def send_dense(k):
        if fused:
            st_copy(chain_w[k], 0).start()

    NW = r.wb.shape[0]

    def act_rows():
        for h in range(2):
            r.dyh[h, 0:T, :] = r.dyb[:, h * HC : (h + 1) * HC]
        if fused:
            x_dyf.wait()
            for h in range(2):
                r.dyh[h, T : 2 * T, :] = r.dyf[:, h * HC : (h + 1) * HC]
        c_dy.start()
        if fused:
            for p in range(H // NR):
                x_h2(p).wait()
            for k in range(NW):
                for b in range(NB):
                    cols = slice(b * SB, (b + 1) * SB)
                    u = nn(r.h2f[...], r.w_in[:, pl.ds(pl.multiple_of((lo + 2 * k) * FC + b * SB, SB), SB)])
                    for m in range(T // GR):
                        rr = slice(m * GR, (m + 1) * GR)
                        um = u[rr, :]
                        th = jnp.tanh(um * (GELU_C + (GELU_C * GELU_K) * (um * um)))
                        r.af[k, rr, cols] = (um * (0.5 + 0.5 * th)).astype(BF)
        for k in range(NW):
            r.at[k, :, 0:T] = nt(r.sc[...], r.a[lo + 2 * k if fused else k]).astype(BF)
            if fused:
                r.at[k, :, T : 2 * T] = nt(r.sc[...], r.af[k]).astype(BF)
            c_at(k).start()

    def grad_wb():
        c_dy.wait()
        for k in range(NW):
            c_at(k).wait()
        for k in range(NW):
            r.wb[k] = (nn(r.at[k], r.dyh[c]) + nn(r.atr[k], r.dyr[...])).astype(BF)
        if fused:
            for k in range(NW):
                y_wb(k).start()

    def back(k):
        rows = slice(k * FC, (k + 1) * FC)
        part_d = nt(r.duf[k % 2], r.w_in[:, rows])
        part_o = nn(r.a[k, 0:H, :], r.w_back[rows, :])
        if k == 0:
            r.oacc[...] = part_o
            r.dacc[...] = part_d
        else:
            r.oacc[...] += part_o
            r.dacc[...] += part_d

    NB = FC // SB

    def hidden(k, b):
        off = k * FC + b * SB
        cols = slice(b * SB, (b + 1) * SB)
        r.u[k % 2, :, cols] = nn(r.h2[...], r.w_in[:, off : off + SB])
        r.g[k % 2, :, cols] = nt(r.dyb[...], r.w_back[off : off + SB, :])

    def gelu(k, b):
        cols = slice(b * SB, (b + 1) * SB)
        for m in range(T // GR):
            rr = slice(m * GR, (m + 1) * GR)
            um = r.u[k % 2, rr, cols]
            u2 = um * um
            th = jnp.tanh(um * (GELU_C + (GELU_C * GELU_K) * u2))
            half = 0.5 + 0.5 * th
            act = um * half
            r.a[k, rr, cols] = act.astype(BF)
            slope = half + act * ((1.0 - th) * (GELU_C + (3.0 * GELU_C * GELU_K) * u2))
            r.duf[k % 2, rr, cols] = (slope * r.g[k % 2, rr, cols]).astype(BF)

    for b in range(NB):
        hidden(0, b)
    for k in range(NF):
        for b in range(NB):
            if k + 1 < NF:
                hidden(k + 1, b)
            gelu(k, b)
        if k > 0:
            back(k - 1)
            if fused:
                pump(FFN_PUMPS[k])
            if k == 1:
                c_h2t.wait()
            c_du(k - 1).wait()
            dense(k - 1)
        else:
            r.h2t[0] = nt(r.sa[...], r.h2[...]).astype(BF)
        r.du[k, 0] = r.duf[k % 2, :, 0:HC]
        r.du[k, 1] = r.duf[k % 2, :, HC : 2 * HC]
        c_du(k).start()
        if k > 0:
            send_dense(k - 1)
        else:
            c_h2t.start()
    back(NF - 1)
    r.ctt[0] = nt(r.sa[...], r.ctx[...]).astype(BF)
    r.h1t[0] = nt(r.sa[...], r.h1[...]).astype(BF)
    c_ctt.start()
    c_h1t.start()

    c_du(NF - 1).wait()
    dense(NF - 1)
    if fused:
        pump(MID_PUMPS[0])
    gsum = None
    for i in range(T // NR):
        rows = slice(i * NR, (i + 1) * NR)
        dn, xh = r.dacc[rows, :], r.xh2[rows, :]
        part = jnp.sum(dn * xh, axis=0, keepdims=True)
        gsum = part if gsum is None else gsum + part
        dg = dn * gf
        m1 = jnp.sum(dg, axis=1, keepdims=True) * inv_d
        m2 = jnp.sum(dg * xh, axis=1, keepdims=True) * inv_d
        dmid = r.dyb[rows, :].astype(F32) + r.rs2[rows, 0:1] * (dg - m1 - xh * m2)
        r.dmid[rows, :] = dmid
        b = dmid.astype(BF)
        r.dmb[0, rows, :] = b[:, 0:HC]
        r.dmb[1, rows, :] = b[:, HC : 2 * HC]
    r.gvec[1:2, :] = gsum
    c_dm = rc(sl.c_dm, r.dmb.at[1 - c], r.dmr, to_core)
    c_dm.start()
    send_dense(NF - 1)
    r.dctx[...] = (nt(r.dmb[0], r.wo[:, 0:HC]) + nt(r.dmb[1], r.wo[:, HC : 2 * HC])).astype(BF)
    r.s_layer[...] = (r.mid[0:H, :] + r.oacc[...]).astype(BF)
    outs = [pltpu.make_async_copy(r.s_layer, r.o_layer, r.osem.at[0]), pltpu.make_async_copy(r.s_x, r.o_x, r.osem.at[1])]
    outs[0].start()
    if fused:
        pump(MID_PUMPS[1])

    act_rows()

    def c_ds(g):
        pair = pl.ds(2 * g, 2)
        return rc(sl.c_ds + g, r.pd.at[pair], r.pdr.at[pair], to_core)

    def bwd_dp(i):
        cols = slice(i * 128, (i + 1) * 128)
        dc2 = r.dctx[:, cols]
        return nt(r.sv[:, cols], jnp.concatenate([dc2 * head_mask[0], dc2 * head_mask[1]], axis=0))

    def bwd_soft(i, dpf):
        for m in range(2 * T // 128):
            h, tc = m * 128 // T, slice(m * 128 % T, m * 128 % T + 128)
            pf = r.pt[i, h * J : (h + 1) * J, tc].astype(F32)
            dp = dpf[:, m * 128 : (m + 1) * 128]
            ds = pf * (dp - jnp.sum(pf * dp, axis=0, keepdims=True))
            r.draw[i % 2, h * J : (h + 1) * J, tc] = (ds * scale).astype(BF)

    def bwd_out(i):
        cols = slice(i * 128, (i + 1) * 128)
        q2, dc2, sk2 = r.q[:, cols], r.dctx[:, cols], r.sk[:, cols]
        draw = r.draw[i % 2]
        dsv = nn(r.pt[i, 0:J], dc2 * head_mask[0]) + nn(r.pt[i, J : 2 * J], dc2 * head_mask[1])
        dsk = nn(draw[0:J], q2 * head_mask[0]) + nn(draw[J : 2 * J], q2 * head_mask[1])
        r.pd[i, 0] = dsk.astype(BF)
        r.pd[i, 1] = dsv.astype(BF)
        stack = jnp.concatenate([sk2 * head_mask[0], sk2 * head_mask[1]], axis=0)
        r.dqkv[0, i // 3, :, (i % 3) * 128 : (i % 3 + 1) * 128] = tn(draw, stack).astype(BF)
        if i % 2:
            c_ds(i // 2).start()

    dpf = bwd_dp(0)
    for i in range(NP):
        nxt = bwd_dp(i + 1) if i + 1 < NP else None
        bwd_soft(i, dpf)
        if i > 0:
            bwd_out(i - 1)
        dpf = nxt
        if i == 0:
            c_ctt.wait()
            c_dm.wait()
            swapped(r.go, nn(r.ctt[0], r.dmb[c]) + nn(r.ctt[1], r.dmr[...]), LYH if fused else YLH, U)
            if fused:
                st_copy(chain_o, 0).start()
        if i == 1:
            grad_wb()
        if fused:
            pump(ATT_PUMPS[i])
    bwd_out(NP - 1)

    def c_g(i):
        return rc(sl.c_g + i, r.dqkv.at[i, 1 - c], r.dqr.at[i], to_core)

    c_g(0).start()
    r.dacc[...] = nt(r.dqkv[0, 0], r.wq[:, 0:HC]) + nt(r.dqkv[0, 1], r.wq[:, HC : 2 * HC])
    for i in range(D // 128):
        cols = slice(i * 128, (i + 1) * 128)
        if i % 2 == 0:
            c_ds(i // 2).wait()
        r.dsk[:, cols] = (r.pd[i, 0].astype(F32) + r.pdr[i, 0].astype(F32)).astype(BF)
        r.dsv[:, cols] = (r.pd[i, 1].astype(F32) + r.pdr[i, 1].astype(F32)).astype(BF)

    dk = nn(r.me[...], r.dsk[...]).astype(BF)
    dv = nn(r.me[...], r.dsv[...]).astype(BF)
    r.dqkv[1, 0] = dk[:, 0:HC]
    r.dqkv[1, 1] = dk[:, HC : 2 * HC]
    r.dqkv[2, 0] = dv[:, 0:HC]
    r.dqkv[2, 1] = dv[:, HC : 2 * HC]
    c_g(1).start()
    c_g(2).start()

    def wgrad(i):
        return (nn(r.h1t[0], r.dqkv[i, c]) + nn(r.h1t[1], r.dqr[i])).astype(BF)

    c_h1t.wait()
    c_g(0).wait()
    swapped(r.gq, wgrad(0), LYH if fused else YLH, U)
    if fused:
        st_copy(chain_q, 0).start()
        pump(KV_PUMPS[0])
    de = nt(r.dsk[...], r.k[0:H, :]) + nt(r.dsv[...], r.v[0:H, :])
    de = jnp.where(r.sel_t[:, 0:H] > 0.5, de, 0.0).astype(BF)
    for b in range(8):
        b2, b1, b0 = b // 4, (b // 2) % 2, b % 2
        j = 4 * b0 + 2 * b2 + b1
        r.ge[b * EB : (b + 1) * EB, :] = de[j * EB : (j + 1) * EB, :]
    c_g(1).wait()
    c_g(2).wait()
    swapped(r.gk, wgrad(1), YLH, U)
    gv = wgrad(2)
    swapped(r.gva, gv[:, 0:VW], YLH, U)
    swapped(r.gvb, gv[:, VW:HC], LYH if fused else YLH, U)
    if fused:
        st_copy(chain_k, 0).start()
        st_copy(chain_va, 0).start()
        st_copy(chain_vb, 0).start()
        st_copy(chain_e, 0).start()
        pump(KV_PUMPS[1])
    acc = r.dacc[...]
    for i, w in ((1, r.wk), (2, r.wv)):
        for hf in range(2):
            acc = acc + nt(r.dqkv[i, hf], w[:, hf * HC : (hf + 1) * HC])
    r.dacc[...] = acc

    gsum = None
    for i in range(T // NR):
        rows = slice(i * NR, (i + 1) * NR)
        dn, xh = r.dacc[rows, :], r.xh1[rows, :]
        part = jnp.sum(dn * xh, axis=0, keepdims=True)
        gsum = part if gsum is None else gsum + part
        if i < H // NR:
            dg = dn * ga
            m1 = jnp.sum(dg, axis=1, keepdims=True) * inv_d
            m2 = jnp.sum(dg * xh, axis=1, keepdims=True) * inv_d
            r.s_x[rows, :] = r.dmid[rows, :] + r.rs1[rows, 0:1] * (dg - m1 - xh * m2)
    outs[1].start()
    r.gvec[0:1, :] = gsum
    if fused:
        pump(KV_PUMPS[2])
    gains = jnp.concatenate([r.gvec[0:2, :], jnp.zeros((126, D), F32)], axis=0).astype(BF)
    r.gg[...] = nt(r.sa[...], gains).astype(BF)
    if fused:
        st_copy(chain_g, 0).start()

    if not fused:
        for cp in outs:
            cp.wait()
        return

    pump(END_PUMPS)

    fin = r.fin
    half = U // 2
    mine = pl.ds(pl.multiple_of(c * half, 8), half)
    first = (w0, w1, w2, w3, chain_o, chain_q, chain_k)
    homes = [(r.s_in, k * FC) for k in range(NF)] + [(r.s_out, 0), (r.s_q, 0), (r.s_k, 0), (r.s_v, 0)]
    n1 = len(first) * HC

    def send_out(src, dst):
        cp = pltpu.make_async_copy(src, dst, r.osem.at[len(outs)])
        cp.start()
        outs.append(cp)

    def c_fin(i):
        cols = pl.ds(0, n1) if i == 0 else pl.ds(n1, HC + GN)
        rows = pl.ds(pl.multiple_of((1 - c) * half, 8), half)
        return rc(sl.c_fin + i, fin.at[rows, cols], r.finr.at[:, cols], to_core)

    def put(i):
        dst, base = homes[i]
        at = i * HC
        dst[:, pl.ds(pl.multiple_of(base + c * HC, 128), HC)] = fin[mine, at : at + HC]
        dst[:, pl.ds(pl.multiple_of(base + (1 - c) * HC, 128), HC)] = r.finr[:, at : at + HC]

    def take(i):
        fin[:, i * HC : (i + 1) * HC] = st_last(first[i])

    for i in (0, 1, 2, 3):
        take(i)
    hi_wb().wait()
    r.finb[...] = r.wb[hi, rows16(y * 2 * Q, 2 * Q), :].astype(F32) + r.wb2[...].astype(F32)
    c_finb = rc(sl.c_finb, r.finb.at[pl.ds(pl.multiple_of((1 - c) * Q, 8), Q)], r.finbr, to_core)
    c_finb.start()
    for i in (4, 6):
        take(i)
    fin[:, n1 : n1 + VW] = st_last(chain_va)
    take(5)
    c_fin(0).start()
    fin[:, n1 + VW : n1 + HC] = st_last(chain_vb)
    r.s_e[...] = st_last(chain_e)
    send_out(r.s_e, r.o_e)
    fin[:, n1 + HC : n1 + HC + GN] = st_last(chain_g)
    c_fin(1).start()
    c_finb.wait()
    r.s_back[:, pl.ds(pl.multiple_of(c * HC, 128), HC)] = r.finb[pl.ds(pl.multiple_of(c * Q, 8), Q), :]
    r.s_back[:, pl.ds(pl.multiple_of((1 - c) * HC, 128), HC)] = r.finbr[...]
    send_out(r.s_back, r.o_back)
    c_fin(0).wait()
    for i in range(len(first)):
        put(i)
    for src, dst in ((r.s_in, r.o_in), (r.s_out, r.o_out), (r.s_q, r.o_q), (r.s_k, r.o_k)):
        send_out(src, dst)
    c_fin(1).wait()
    put(len(first))
    at = n1 + HC
    r.s_g[...] = fin[mine, at : at + 128] + r.finr[:, at : at + 128]
    send_out(r.s_v, r.o_v)
    send_out(r.s_g, r.o_g)
    for cp in outs:
        cp.wait()


def staged(name):
    return f"s{name[1:]}"


def hand_over(r, names):
    copies = []
    for i, (src, dst) in enumerate(names):
        cp = pltpu.make_async_copy(src, dst, r.sem.at[i])
        cp.start()
        copies.append(cp)
    g = jnp.concatenate([r.s_g[...], jnp.zeros((128 - r.s_g.shape[0], 128), F32)], axis=0).T
    n = r.s_g.shape[0]
    r.d_ga[...] = g[0, 0:n]
    r.d_gf[...] = g[1, 0:n]
    for cp in copies:
        cp.wait()


def run_layer(mesh_shape, tokens, seg_ids, slot_doc, proj_e, g_attn, w_query, w_key, w_value, w_out, g_ffn, w_in,
              w_back, cotangent):
    n_dp, n_seq = mesh_shape
    rows, H, D = tokens.shape
    J = proj_e.shape[1]
    FF = w_in.shape[1]
    fused = n_dp == 8
    T = 2 * H
    HC, U, NF, Q = D // 2, D // 16, FF // D, FF // 32
    EB = J // 8
    NW, TW = (2, 2 * T) if fused else (NF, T)
    GN, VW = 128, 256
    sel_a, sel_c = (jnp.asarray(m, BF) for m in selections(D, FF))

    inputs = dict(
        x_in=(tokens.reshape(H, D), False),
        seg_in=(seg_ids.reshape(1, H), False),
        slot_in=(slot_doc.reshape(1, J), False),
        e_in=(proj_e, False),
        ga=(g_attn, True),
        wq_in=(w_query, False),
        wk_in=(w_key, False),
        wv_in=(w_value, False),
        wo_in=(w_out, False),
        gf=(g_ffn, True),
        w_in_in=(w_in, False),
        w_back_in=(w_back, False),
        dy_in=(cotangent.reshape(H, D), False),
        sa_in=(sel_a, False),
        sc_in=(sel_c, False),
    )
    parts = dict(
        wb=((NW, 4 * Q, HC), BF),
        wi=((NF, D // 2, HC), BF),
        go=((D // 2, HC), BF),
        gq=((D // 2, HC), BF),
        gk=((D // 2, HC), BF),
        gva=((D // 2, VW), BF),
        gvb=((D // 2, HC - VW), BF),
        gg=((D // 2, GN), BF),
        ge=((J, H), BF),
    )
    outs = dict(o_layer=((H, D), BF), o_x=((H, D), F32))
    if fused:
        outs.update(
            o_g=((U // 2, 128), F32),
            o_q=((U // 2, D), F32),
            o_k=((U // 2, D), F32),
            o_v=((U // 2, D), F32),
            o_out=((U // 2, D), F32),
            o_in=((U // 2, FF), F32),
            o_back=((Q, D), F32),
            o_e=((EB, H), F32),
        )
    else:
        outs.update(parts)
    scratch = dict(
        xb=((T, D), BF), eb=((T, J), BF), segs=((2, 1, H), jnp.int32), slot=((1, J), jnp.int32),
        wq=((D, D), BF), wk=((D, D), BF), wv=((D, D), BF), wo=((D, D), BF),
        w_in=((D, FF), BF), w_back=((FF, D), BF),
        dyb=((T, D), BF), dyh=((2, TW, HC), BF), dyr=((TW, HC), BF),
        sa=((D // 2, D), BF), sc=((4 * Q, FF // 4), BF),
        eye=((T, T), BF),
        h1=((T, D), BF), xh1=((T, D), F32), rs1=((T, 128), F32),
        q=((T, D), BF), k=((T, D), BF), v=((T, D), BF),
        sel_t=((J, T), F32), me=((T, J), BF), met=((J, T), BF),
        pk=((2, J, D), BF), pkr=((2, J, D), BF), sk=((J, D), BF), sv=((J, D), BF),

        pt=((D // 128, 2 * J, T), BF), ctx=((T, D), BF),
        mid=((T, D), F32), xh2=((T, D), F32), rs2=((T, 128), F32), h2=((T, D), BF),
        h1t=((2, D // 2, T), BF), h2t=((2, D // 2, T), BF), ctt=((2, D // 2, T), BF),
        a=((NF, T, D), BF), duf=((2, T, D), BF), u=((2, T, D), F32), g=((2, T, D), F32), du=((NF, 2, T, HC), BF), dur=((NF, T, HC), BF),
        at=((NW, 4 * Q, TW), BF), atr=((NW, 4 * Q, TW), BF),
        oacc=((H, D), F32), dacc=((T, D), F32), dmid=((T, D), F32), gvec=((8, D), F32),
        dmb=((2, T, HC), BF), dmr=((T, HC), BF), dctx=((T, D), BF), draw=((2, 2 * J, T), BF),
        pd=((D // 128, 2, J, 128), BF), pdr=((D // 128, 2, J, 128), BF),
        dsk=((J, D), BF), dsv=((J, D), BF),
        dqkv=((3, 2, T, HC), BF), dqr=((3, T, HC), BF),
    )
    if fused:
        scratch.update(
            parts,
            wb1=((2, 2 * Q, HC), BF), wb2=((2 * Q, HC), BF), finb=((2 * Q, HC), F32), finbr=((Q, HC), F32),
            h2f=((T, D), BF), dyf=((T, D), BF), af=((2, T, D), BF),
            wi1=((NF, 4 * U, HC), BF), wi2=((NF, 2 * U, HC), BF), wi3=((NF, U, HC), BF),
            go1=((4 * U, HC), BF), go2=((2 * U, HC), BF), go3=((U, HC), BF),
            gq1=((4 * U, HC), BF), gq2=((2 * U, HC), BF), gq3=((U, HC), BF),
            gk1=((4 * U, HC), BF), gk2=((2 * U, HC), BF), gk3=((U, HC), BF),
            gva1=((4 * U, VW), BF), gva2=((2 * U, VW), BF), gva3=((U, VW), BF),
            gvb1=((4 * U, HC - VW), BF), gvb2=((2 * U, HC - VW), BF), gvb3=((U, HC - VW), BF),
            gg1=((4 * U, GN), BF), gg2=((2 * U, GN), BF), gg3=((U, GN), BF),
            ge1=((4 * EB, H), BF), ge2=((2 * EB, H), BF), ge3=((EB, H), BF),
            fin=((U, NF * HC + 4 * HC + GN), F32), finr=((U // 2, NF * HC + 4 * HC + GN), F32),
        )
    counts = dict(
        x_seg=1, x_e=1, x_x=1, x_dy=1, c_pk=1, c_pv=1, c_h1t=1, c_h2t=1, c_dy=1, c_ctt=1, c_at=NF, c_du=NF, c_dm=1,
        c_ds=D // 256, c_g=3, y_wb=NF, wi=3 * NF, hi_wb=1, l_dy=1, x_dyf=1, l_h2=2, x_h2=2, c_finb=1, go=3, gq=3, gk=3, gva=3, gvb=3, gg=3, ge=3, c_fin=2,
    )
    sl, count = SimpleNamespace(), 0
    for name, n in counts.items():
        setattr(sl, name, count)
        count += n
    scratch.update((staged(n), v) for n, v in outs.items() if n[0] == "o")
    names = [*inputs, *outs, *scratch]

    def body(*refs):
        r = SimpleNamespace(**dict(zip(names, refs)))
        r.osem, r.lsem, r.ssem, r.rsem = refs[len(names) :]
        layer_body(fused, r, sl)

    res = pl.pallas_call(
        body,
        out_shape=[jax.ShapeDtypeStruct(sh, dt) for sh, dt in outs.values()],
        in_specs=[pl.BlockSpec(memory_space=pltpu.VMEM if v else pl.ANY) for _, v in inputs.values()],
        out_specs=[pl.BlockSpec(memory_space=pl.ANY if n[0] == "o" else pltpu.VMEM) for n in outs],
        scratch_shapes=[pltpu.VMEM(sh, dt) for sh, dt in scratch.values()]
        + [pltpu.SemaphoreType.DMA((10,))]
        + [pltpu.SemaphoreType.DMA((13,)), pltpu.SemaphoreType.DMA((count,)), pltpu.SemaphoreType.DMA((count,))],
        compiler_params=pltpu.CompilerParams(
            collective_id=0, has_side_effects=True, vmem_limit_bytes=60 * 1024 * 1024
        ),
        cost_estimate=pl.CostEstimate(flops=12 * 10**9, bytes_accessed=24 * 10**6, transcendentals=2 * 10**6),
    )(*[v for v, _ in inputs.values()])
    o = SimpleNamespace(**dict(zip(outs, res)))
    if fused:
        src = dict(s_layer=o.o_layer, s_x=o.o_x, s_q=o.o_q, s_k=o.o_k, s_v=o.o_v, s_out=o.o_out, s_in=o.o_in,
                   s_back=o.o_back, s_e=o.o_e, s_g=o.o_g)
        n_copy = len(src) - 1
        dst = dict(
            d_layer=((rows, H, D), BF), d_x=((rows, H, D), F32), d_q=((U // 2, D), F32), d_k=((U // 2, D), F32),
            d_v=((U // 2, D), F32), d_out=((U // 2, D), F32), d_in=((U // 2, FF), F32), d_back=((Q, D), F32),
            d_e=((EB, H), F32), d_ga=((U // 2,), F32), d_gf=((U // 2,), F32),
        )

        def tail(*refs):
            r = SimpleNamespace(**dict(zip([*src, *dst], refs)))
            r.sem = refs[-1]
            r.d_layer, r.d_x = r.d_layer.at[0], r.d_x.at[0]
            pairs = list(zip(vars(r).values(), list(vars(r).values())[len(src) :]))[:n_copy]
            hand_over(r, pairs)

        res = pl.pallas_call(
            tail,
            out_shape=[jax.ShapeDtypeStruct(sh, dt) for sh, dt in dst.values()],
            in_specs=[pl.BlockSpec(memory_space=pl.ANY)] * n_copy + [pl.BlockSpec(memory_space=pltpu.VMEM)],
            out_specs=[pl.BlockSpec(memory_space=pltpu.VMEM)] * len(dst),
            scratch_shapes=[pltpu.SemaphoreType.DMA((n_copy,))],
        )(*src.values())
        o = SimpleNamespace(**dict(zip(dst, res)))
        return o.d_layer, o.d_x, o.d_ga, o.d_q, o.d_k, o.d_v, o.d_out, o.d_gf, o.d_in, o.d_back, o.d_e.T

    layer = o.o_layer.reshape(rows, H, D)
    x_grad = o.o_x.reshape(rows, H, D)

    s = lax.axis_index(SEQ)
    x, c = s // 2, s % 2
    both = (DP, SEQ)

    def scatter(v):
        return lax.psum_scatter(v, both, scatter_dimension=0, tiled=True)

    def rows_back(v, y_first):
        v = v.astype(F32).reshape(2, 2, 2, U, v.shape[-1])
        v = v.transpose(2, 1, 0, 3, 4) if y_first else v.transpose(2, 0, 1, 3, 4)
        return v.reshape(8, U, v.shape[-1])

    def whole(v, y_first):
        v = rows_back(v, y_first)
        full = jnp.zeros((8, 2, U, 2, HC), F32)
        full = lax.dynamic_update_slice(full, v[:, None, :, None, :], (0, x, 0, c, 0))
        return full.reshape(D, 2 * HC)

    wi = jnp.stack([whole(o.wi[f], True) for f in range(NF)], axis=1).reshape(D, FF)
    wo = whole(o.go, True)
    gv = jnp.concatenate([o.gva, o.gvb], axis=1)
    wqkv = [whole(o.gq, True), whole(o.gk, True), whole(gv, True)]
    gains = rows_back(o.gg, True)
    gfull = lax.dynamic_update_slice(jnp.zeros((8, 2, U, 128), F32), gains[:, None], (0, x, 0, 0)).reshape(D, 128)
    wb = o.wb.astype(F32).reshape(NF * 2, 1, 2 * Q, 1, HC)
    wb = lax.dynamic_update_slice(jnp.zeros((NF * 2, 2, 2 * Q, 2, HC), F32), wb, (0, x, 0, c, 0)).reshape(FF, D)
    ge = o.ge.astype(F32).reshape(2, 2, 2, EB, H).transpose(2, 0, 1, 3, 4).reshape(J, H).T
    return (
        layer, x_grad, scatter(gfull[:, 0]), scatter(wqkv[0]), scatter(wqkv[1]), scatter(wqkv[2]), scatter(wo),
        scatter(gfull[:, 1]), scatter(wi), scatter(wb), lax.psum_scatter(ge, DP, scatter_dimension=1, tiled=True),
    )


def solution(mesh):
    shape = (mesh.shape[DP], mesh.shape[SEQ])
    both = (DP, SEQ)
    in_specs = (
        P(DP, SEQ, None), P(DP, SEQ), P(DP, None), P(SEQ, None),
        P(), P(), P(), P(), P(), P(), P(), P(), P(DP, SEQ, None),
    )
    out_specs = (
        P(DP, SEQ, None), P(DP, SEQ, None), P(both), P(both, None), P(both, None), P(both, None),
        P(both, None), P(both), P(both, None), P(both, None), P(SEQ, DP),
    )
    return jax.shard_map(
        functools.partial(run_layer, shape), mesh=mesh, in_specs=in_specs, out_specs=out_specs, check_vma=False
    )
```

```python
import functools
from types import SimpleNamespace

import jax
import jax.numpy as jnp
import numpy as np
from jax import lax
from jax.experimental import pallas as pl
from jax.experimental.pallas import tpu as pltpu
from jax.sharding import PartitionSpec as P

HEAD_DIM = 64
DP, SEQ = "dp", "seq"
YLH, LYH = "ylh", "lyh"
BF = jnp.bfloat16
F32 = jnp.float32
MESH = pl.DeviceIdType.MESH
GELU_C = 0.7978845608028654
GELU_K = 0.044715


def nn(a, b):
    return lax.dot_general(a, b, (((1,), (0,)), ((), ())), preferred_element_type=F32)


def tn(a, b):
    return lax.dot_general(a, b, (((0,), (0,)), ((), ())), preferred_element_type=F32)


def nt(a, b):
    return lax.dot_general(a, b, (((1,), (1,)), ((), ())), preferred_element_type=F32)


def selections(d_model, ff):
    unit = d_model // 16
    sel_a = np.zeros((2, d_model // 2, d_model), np.float32)
    for x in range(2):
        for b in range(8):
            j = 4 * (b % 2) + 2 * ((b // 2) % 2) + b // 4
            for o in range(unit):
                sel_a[x, b * unit + o, (2 * j + x) * unit + o] = 1
    q = ff // 32
    sel_c = np.zeros((2, 4 * q, ff // 4), np.float32)
    for x in range(2):
        for b in range(4):
            for o in range(q):
                sel_c[x, b * q + o, (b // 2 * 4 + x * 2 + b % 2) * q + o] = 1
    return sel_a, sel_c


def layer_body(fused, r, sl):
    d, s = lax.axis_index(DP), lax.axis_index(SEQ)
    x, c = s // 2, s % 2
    y, lo, hi = d % 2, (d // 2) % 2, d // 4
    to_core = (d, s + 1 - 2 * c)
    to_x = (d, s + 2 - 4 * x)
    to_y = (d + 1 - 2 * y, s)
    to_lo = (d + 2 - 4 * lo, s)
    to_hi = (d + 4 - 8 * hi, s)
    lsem, ssem, rsem = r.lsem, r.ssem, r.rsem
    D = r.h1.shape[1]
    T = r.h1.shape[0]
    H = T // 2
    J = r.sk.shape[0]
    FC = D
    NF = r.w_in.shape[1] // FC
    HC = D // 2
    U = D // 16
    Q = r.wb.shape[1] // 4
    scale = HEAD_DIM ** (-0.5)

    loads = []

    def load(src, dst):
        cp = pltpu.make_async_copy(src, dst, lsem.at[len(loads)])
        loads.append(cp)
        cp.start()
        return cp

    def rc(i, src, dst, dev):
        return pltpu.make_async_remote_copy(
            src_ref=src, dst_ref=dst, send_sem=ssem.at[i], recv_sem=rsem.at[i], device_id=dev, device_id_type=MESH
        )

    partners = [to_core, to_x] + ([to_y, to_lo, to_hi] if fused else [])
    barrier = pltpu.get_barrier_semaphore()
    for dev in partners:
        pl.semaphore_signal(barrier, inc=1, device_id=dev, device_id_type=MESH)
    l_x = load(r.x_in, r.xb.at[pl.ds(0, H)])
    l_seg = load(r.seg_in, r.segs.at[0])
    l_slot = load(r.slot_in, r.slot)
    l_e = load(r.e_in, r.eb.at[pl.ds(0, H)])
    l_wq = load(r.wq_in, r.wq)
    l_wk = load(r.wk_in, r.wk)
    l_wv = load(r.wv_in, r.wv)
    l_dy = load(r.dy_in, r.dyb.at[pl.ds(0, H)])
    l_sa = load(r.sa_in.at[x], r.sa)
    l_wo = load(r.wo_in, r.wo)
    l_sc = load(r.sc_in.at[x], r.sc)
    l_w_in = load(r.w_in_in, r.w_in)
    l_w_back = load(r.w_back_in, r.w_back)

    pl.semaphore_wait(barrier, len(partners))

    x_seg = rc(sl.x_seg, r.seg_in, r.segs.at[1], to_x)
    x_e = rc(sl.x_e, r.e_in, r.eb.at[pl.ds(H, H)], to_x)
    x_x = rc(sl.x_x, r.x_in, r.xb.at[pl.ds(H, H)], to_x)
    x_dy = rc(sl.x_dy, r.dy_in, r.dyb.at[pl.ds(H, H)], to_x)
    x_x.start()
    if fused:
        own_rows, far_rows = pl.ds(0, H), pl.ds(H, H)
        l_dyf = rc(sl.l_dy, r.dy_in, r.dyf.at[own_rows], to_lo)
        x_dyf = rc(sl.x_dyf, r.dyf.at[own_rows], r.dyf.at[far_rows], to_x)
        l_dyf.start()

    rows_i = lax.broadcasted_iota(jnp.int32, (T, T), 0)
    cols_i = lax.broadcasted_iota(jnp.int32, (T, T), 1)
    eye = jnp.where(rows_i == cols_i, 1.0, 0.0).astype(BF)
    r.eye[...] = eye
    ga = r.ga[...].astype(F32).reshape(1, D)
    gf = r.gf[...].astype(F32).reshape(1, D)
    inv_d = 1.0 / D
    NR = 64

    def norm_rows(v):
        cen = v - jnp.sum(v, axis=1, keepdims=True) * inv_d
        rstd = lax.rsqrt(jnp.sum(cen * cen, axis=1, keepdims=True) * inv_d + 1e-5)
        return cen * rstd, rstd

    def norm_into(src, gain, xh_ref, rs_ref, h_ref, start, count):
        for i in range(start // NR, (start + count) // NR):
            rows = slice(i * NR, (i + 1) * NR)
            xh, rstd = norm_rows(src[rows, :].astype(F32))
            xh_ref[rows, :] = xh
            rs_ref[rows, :] = jnp.broadcast_to(rstd, (NR, 128))
            h_ref[rows, :] = (xh * gain).astype(BF)

    l_x.wait()
    norm_into(r.xb, ga, r.xh1, r.rs1, r.h1, 0, H)
    x_seg.start()
    x_e.start()
    l_slot.wait()
    slot_row = r.slot[...].astype(F32)
    slot_col = nt(eye, jnp.broadcast_to(slot_row, (T, J)).astype(BF))
    l_wq.wait()
    l_wk.wait()
    l_wv.wait()
    own, far = slice(0, H), slice(H, T)
    r.k[own, :] = nn(r.h1[own, :], r.wk[...]).astype(BF)
    r.v[own, :] = nn(r.h1[own, :], r.wv[...]).astype(BF)
    r.q[own, :] = nn(r.h1[own, :], r.wq[...]).astype(BF)
    l_e.wait()
    l_sa.wait()
    l_seg.wait()

    def masks(part, at):
        row = r.segs[part].astype(F32)
        col = nt(eye[0:H, 0:H], jnp.broadcast_to(row, (J, H)).astype(BF))
        r.sel_t[:, at] = jnp.where(slot_col[:, 0:H] == row, 1.0, 0.0)
        r.me[at, :] = jnp.where(col == slot_row, r.eb[at, :].astype(F32), 0.0).astype(BF)
        r.met[:, at] = nt(eye, r.me[at, :]).astype(BF)

    masks(0, own)
    x_x.wait()
    x_dy.start()
    norm_into(r.xb, ga, r.xh1, r.rs1, r.h1, H, H)
    r.k[far, :] = nn(r.h1[far, :], r.wk[...]).astype(BF)

    x_seg.wait()
    x_e.wait()
    masks(1, far)

    c_pk = rc(sl.c_pk, r.pk.at[0], r.pkr.at[0], to_core)
    c_pv = rc(sl.c_pv, r.pk.at[1], r.pkr.at[1], to_core)
    r.pk[0] = nn(r.met[...], r.k[...]).astype(BF)
    c_pk.start()
    r.v[far, :] = nn(r.h1[far, :], r.wv[...]).astype(BF)
    r.pk[1] = nn(r.met[...], r.v[...]).astype(BF)
    c_pv.start()
    r.q[far, :] = nn(r.h1[far, :], r.wq[...]).astype(BF)
    c_h1t = rc(sl.c_h1t, r.h1t.at[0], r.h1t.at[1], to_core)

    lane = lax.broadcasted_iota(jnp.int32, (T, 128), 1)
    head_mask = [jnp.where(lane < 64, 1.0, 0.0).astype(BF), jnp.where(lane < 64, 0.0, 1.0).astype(BF)]

    NP = D // 128

    def fwd_raw(i):
        cols = slice(i * 128, (i + 1) * 128)
        q2 = r.q[:, cols]
        return nt(r.sk[:, cols], jnp.concatenate([q2 * head_mask[0], q2 * head_mask[1]], axis=0))

    def fwd_soft(i, raw):
        for m in range(2 * T // 128):
            h, tc = m * 128 // T, slice(m * 128 % T, m * 128 % T + 128)
            sc = jnp.where(r.sel_t[:, tc] > 0.5, raw[:, m * 128 : (m + 1) * 128] * scale, -1e30)
            e = jnp.exp(sc - jnp.max(sc, axis=0, keepdims=True))
            r.pt[i, h * J : (h + 1) * J, tc] = (e * (1.0 / jnp.sum(e, axis=0, keepdims=True))).astype(BF)

    def fwd_ctx(i):
        cols = slice(i * 128, (i + 1) * 128)
        sv2 = r.sv[:, cols]
        stack = jnp.concatenate([sv2 * head_mask[0], sv2 * head_mask[1]], axis=0)
        r.ctx[:, cols] = tn(r.pt[i], stack).astype(BF)

    c_pk.wait()
    r.sk[...] = (r.pk[0].astype(F32) + r.pkr[0].astype(F32)).astype(BF)
    raw = fwd_raw(0)
    for i in range(NP):
        nxt = fwd_raw(i + 1) if i + 1 < NP else None
        fwd_soft(i, raw)
        if i == 0:
            c_pv.wait()
            r.sv[...] = (r.pk[1].astype(F32) + r.pkr[1].astype(F32)).astype(BF)
        if i > 0:
            fwd_ctx(i - 1)
        raw = nxt
    fwd_ctx(NP - 1)

    if fused:
        l_dyf.wait()
        x_dyf.start()

    def l_h2(p):
        rows = pl.ds(p * NR, NR)
        return rc(sl.l_h2 + p, r.h2.at[rows], r.h2f.at[rows], to_lo)

    def x_h2(p):
        return rc(sl.x_h2 + p, r.h2f.at[pl.ds(p * NR, NR)], r.h2f.at[pl.ds(H + p * NR, NR)], to_x)

    l_wo.wait()
    for rows in (own, far):
        r.mid[rows, :] = r.xb[rows, :].astype(F32) + nn(r.ctx[rows, :], r.wo[...])
    norm_into(r.mid, gf, r.xh2, r.rs2, r.h2, 0, H)
    if fused:
        for p in range(H // NR):
            l_h2(p).start()
    norm_into(r.mid, gf, r.xh2, r.rs2, r.h2, H, H)
    x_dy.wait()
    l_dy.wait()
    c_dy = rc(sl.c_dy, r.dyh.at[1 - c], r.dyr, to_core)
    l_w_in.wait()
    l_w_back.wait()
    l_sc.wait()
    c_h2t = rc(sl.c_h2t, r.h2t.at[0], r.h2t.at[1], to_core)
    c_ctt = rc(sl.c_ctt, r.ctt.at[0], r.ctt.at[1], to_core)

    def c_at(k):
        return rc(sl.c_at + k, r.at.at[k], r.atr.at[k], to_core)

    def c_du(f):
        return rc(sl.c_du + f, r.du.at[f, 1 - c], r.dur.at[f], to_core)

    def y_wb(k):
        return rc(sl.y_wb + k, r.wb.at[k, rows16((1 - y) * 2 * Q, 2 * Q)], r.wb1.at[k], to_y)

    bits = dict(y=(y, to_y), l=(lo, to_lo), h=(hi, to_hi))

    def span(order, unit, stage):
        start, n = 0, 4 * unit
        for i in range(stage + 1):
            bit = bits[order[i]][0]
            kept, sent = start + bit * n, start + (1 - bit) * n
            if i < stage:
                start, n = kept, n // 2
        return kept, sent, n

    def rows16(start, n):
        return pl.ds(pl.multiple_of(start, 16), n)

    GN = 128
    VW = 256
    EB = J // 8
    if fused:
        chain_w = [
            (LYH if k in (1, 3) else YLH, r.wi.at[k], (r.wi1.at[k], r.wi2.at[k], r.wi3.at[k]), sl.wi + 3 * k, U)
            for k in range(NF)
        ]
        chain_o = (LYH, r.go, (r.go1, r.go2, r.go3), sl.go, U)
        chain_q = (LYH, r.gq, (r.gq1, r.gq2, r.gq3), sl.gq, U)
        chain_k = (YLH, r.gk, (r.gk1, r.gk2, r.gk3), sl.gk, U)
        chain_va = (YLH, r.gva, (r.gva1, r.gva2, r.gva3), sl.gva, U)
        chain_vb = (LYH, r.gvb, (r.gvb1, r.gvb2, r.gvb3), sl.gvb, U)
        chain_g = (YLH, r.gg, (r.gg1, r.gg2, r.gg3), sl.gg, U)
        chain_e = (LYH, r.ge, (r.ge1, r.ge2, r.ge3), sl.ge, EB)

    def add_into(dst, idx, src):
        dst[idx] = (dst[idx].astype(F32) + src.astype(F32)).astype(BF)

    def hi_wb():
        return rc(sl.hi_wb, r.wb.at[1 - hi, rows16(y * 2 * Q, 2 * Q)], r.wb2, to_hi)

    def pump_wb(k):
        if k < 2:
            y_wb(k).wait()
            add_into(r.wb, (k, rows16(y * 2 * Q, 2 * Q), slice(None)), r.wb1[k])

            @pl.when(hi == 1 - k)
            def _():
                hi_wb().start()
        else:
            l_h2(k - 2).wait()
            x_h2(k - 2).start()

    def pump(steps):
        for step in steps:
            if step[0] is None:
                pump_wb(step[1])
            else:
                st_next(step[0], step[1])

    def st_copy(chain, stage):
        order, buf, got, slot, unit = chain
        _, sent, n = span(order, unit, stage)
        return rc(slot + stage, buf.at[rows16(sent, n)], got[stage], bits[order[stage]][1])

    def st_next(chain, stage):
        order, buf, got, _, unit = chain
        st_copy(chain, stage).wait()
        kept, _, n = span(order, unit, stage)
        add_into(buf, (rows16(kept, n), slice(None)), got[stage][...])
        st_copy(chain, stage + 1).start()

    def st_last(chain):
        order, buf, got, _, unit = chain
        st_copy(chain, 2).wait()
        kept, _, n = span(order, unit, 2)
        return buf[rows16(kept, n), :].astype(F32) + got[2][...].astype(F32)

    def swap_rows(buf, cols, val, unit):
        q = 2 * unit
        for b in range(4):
            to = (b % 2) * 2 + b // 2
            buf[to * q : (to + 1) * q, cols] = val[b * q : (b + 1) * q, :].astype(BF)

    SB = 256
    GR = 32

    if fused:
        b0, b1, h0, h1 = [(None, k) for k in range(4)]
        w0, w1, w2, w3 = chain_w
        FFN_PUMPS = [[], [], [h0], [h1]]
        MID_PUMPS = [[(w0, 0)], [(w1, 0)]]
        ATT_PUMPS = [[(w2, 0)], [(w0, 1), (w3, 0)], [], [], [(w1, 1)], []]
        KV_PUMPS = [[(chain_o, 0)], [b0, (w2, 1)], [b1, (chain_q, 0)]]
        END_PUMPS = [(w3, 1), (chain_vb, 0), (chain_e, 0), (chain_o, 1), (chain_k, 0), (chain_q, 1), (chain_va, 0), (chain_k, 1), (chain_g, 0), (chain_va, 1), (chain_vb, 1), (chain_e, 1), (chain_g, 1)]

    def swapped(buf, val, order, unit):
        if order == YLH:
            buf[...] = val.astype(BF)
        else:
            swap_rows(buf, slice(0, val.shape[1]), val, unit)

    def dense(k):
        wi = nn(r.h2t[0], r.du[k, c]) + nn(r.h2t[1], r.dur[k])
        if fused:
            swapped(chain_w[k][1], wi, chain_w[k][0], U)
        else:
            r.wi[k] = wi.astype(BF)

    def send_dense(k):
        if fused:
            st_copy(chain_w[k], 0).start()

    NW = r.wb.shape[0]

    def act_rows():
        for h in range(2):
            r.dyh[h, 0:T, :] = r.dyb[:, h * HC : (h + 1) * HC]
        if fused:
            x_dyf.wait()
            for h in range(2):
                r.dyh[h, T : 2 * T, :] = r.dyf[:, h * HC : (h + 1) * HC]
        c_dy.start()
        if fused:
            for p in range(H // NR):
                x_h2(p).wait()
            for k in range(NW):
                for b in range(NB):
                    cols = slice(b * SB, (b + 1) * SB)
                    u = nn(r.h2f[...], r.w_in[:, pl.ds(pl.multiple_of((lo + 2 * k) * FC + b * SB, SB), SB)])
                    for m in range(T // GR):
                        rr = slice(m * GR, (m + 1) * GR)
                        um = u[rr, :]
                        th = jnp.tanh(um * (GELU_C + (GELU_C * GELU_K) * (um * um)))
                        r.af[k, rr, cols] = (um * (0.5 + 0.5 * th)).astype(BF)
        for k in range(NW):
            r.at[k, :, 0:T] = nt(r.sc[...], r.a[lo + 2 * k if fused else k]).astype(BF)
            if fused:
                r.at[k, :, T : 2 * T] = nt(r.sc[...], r.af[k]).astype(BF)
            c_at(k).start()

    def grad_wb():
        c_dy.wait()
        for k in range(NW):
            c_at(k).wait()
        for k in range(NW):
            r.wb[k] = (nn(r.at[k], r.dyh[c]) + nn(r.atr[k], r.dyr[...])).astype(BF)
        if fused:
            for k in range(NW):
                y_wb(k).start()

    def back(k):
        rows = slice(k * FC, (k + 1) * FC)
        part_d = nt(r.duf[k % 2], r.w_in[:, rows])
        part_o = nn(r.a[k, 0:H, :], r.w_back[rows, :])
        if k == 0:
            r.oacc[...] = part_o
            r.dacc[...] = part_d
        else:
            r.oacc[...] += part_o
            r.dacc[...] += part_d

    NB = FC // SB

    def hidden(k, b):
        off = k * FC + b * SB
        cols = slice(b * SB, (b + 1) * SB)
        r.u[k % 2, :, cols] = nn(r.h2[...], r.w_in[:, off : off + SB])
        r.g[k % 2, :, cols] = nt(r.dyb[...], r.w_back[off : off + SB, :])

    def gelu(k, b):
        cols = slice(b * SB, (b + 1) * SB)
        for m in range(T // GR):
            rr = slice(m * GR, (m + 1) * GR)
            um = r.u[k % 2, rr, cols]
            u2 = um * um
            th = jnp.tanh(um * (GELU_C + (GELU_C * GELU_K) * u2))
            half = 0.5 + 0.5 * th
            act = um * half
            r.a[k, rr, cols] = act.astype(BF)
            slope = half + act * ((1.0 - th) * (GELU_C + (3.0 * GELU_C * GELU_K) * u2))
            r.duf[k % 2, rr, cols] = (slope * r.g[k % 2, rr, cols]).astype(BF)

    for b in range(NB):
        hidden(0, b)
    for k in range(NF):
        for b in range(NB):
            if k + 1 < NF:
                hidden(k + 1, b)
            gelu(k, b)
        if k > 0:
            back(k - 1)
            if fused:
                pump(FFN_PUMPS[k])
            if k == 1:
                c_h2t.wait()
            c_du(k - 1).wait()
            dense(k - 1)
        else:
            r.h2t[0] = nt(r.sa[...], r.h2[...]).astype(BF)
        r.du[k, 0] = r.duf[k % 2, :, 0:HC]
        r.du[k, 1] = r.duf[k % 2, :, HC : 2 * HC]
        c_du(k).start()
        if k > 0:
            send_dense(k - 1)
        else:
            c_h2t.start()
    back(NF - 1)
    r.ctt[0] = nt(r.sa[...], r.ctx[...]).astype(BF)
    r.h1t[0] = nt(r.sa[...], r.h1[...]).astype(BF)
    c_ctt.start()
    c_h1t.start()

    c_du(NF - 1).wait()
    dense(NF - 1)
    if fused:
        pump(MID_PUMPS[0])
    gsum = None
    for i in range(T // NR):
        rows = slice(i * NR, (i + 1) * NR)
        dn, xh = r.dacc[rows, :], r.xh2[rows, :]
        part = jnp.sum(dn * xh, axis=0, keepdims=True)
        gsum = part if gsum is None else gsum + part
        dg = dn * gf
        m1 = jnp.sum(dg, axis=1, keepdims=True) * inv_d
        m2 = jnp.sum(dg * xh, axis=1, keepdims=True) * inv_d
        dmid = r.dyb[rows, :].astype(F32) + r.rs2[rows, 0:1] * (dg - m1 - xh * m2)
        r.dmid[rows, :] = dmid
        b = dmid.astype(BF)
        r.dmb[0, rows, :] = b[:, 0:HC]
        r.dmb[1, rows, :] = b[:, HC : 2 * HC]
    r.gvec[1:2, :] = gsum
    c_dm = rc(sl.c_dm, r.dmb.at[1 - c], r.dmr, to_core)
    c_dm.start()
    send_dense(NF - 1)
    r.dctx[...] = (nt(r.dmb[0], r.wo[:, 0:HC]) + nt(r.dmb[1], r.wo[:, HC : 2 * HC])).astype(BF)
    r.s_layer[...] = (r.mid[0:H, :] + r.oacc[...]).astype(BF)
    outs = [pltpu.make_async_copy(r.s_layer, r.o_layer, r.osem.at[0]), pltpu.make_async_copy(r.s_x, r.o_x, r.osem.at[1])]
    outs[0].start()
    if fused:
        pump(MID_PUMPS[1])

    act_rows()

    def c_ds(g):
        pair = pl.ds(2 * g, 2)
        return rc(sl.c_ds + g, r.pd.at[pair], r.pdr.at[pair], to_core)

    def bwd_dp(i):
        cols = slice(i * 128, (i + 1) * 128)
        dc2 = r.dctx[:, cols]
        return nt(r.sv[:, cols], jnp.concatenate([dc2 * head_mask[0], dc2 * head_mask[1]], axis=0))

    def bwd_soft(i, dpf):
        for m in range(2 * T // 128):
            h, tc = m * 128 // T, slice(m * 128 % T, m * 128 % T + 128)
            pf = r.pt[i, h * J : (h + 1) * J, tc].astype(F32)
            dp = dpf[:, m * 128 : (m + 1) * 128]
            ds = pf * (dp - jnp.sum(pf * dp, axis=0, keepdims=True))
            r.draw[i % 2, h * J : (h + 1) * J, tc] = (ds * scale).astype(BF)

    def bwd_out(i):
        cols = slice(i * 128, (i + 1) * 128)
        q2, dc2, sk2 = r.q[:, cols], r.dctx[:, cols], r.sk[:, cols]
        draw = r.draw[i % 2]
        dsv = nn(r.pt[i, 0:J], dc2 * head_mask[0]) + nn(r.pt[i, J : 2 * J], dc2 * head_mask[1])
        dsk = nn(draw[0:J], q2 * head_mask[0]) + nn(draw[J : 2 * J], q2 * head_mask[1])
        r.pd[i, 0] = dsk.astype(BF)
        r.pd[i, 1] = dsv.astype(BF)
        stack = jnp.concatenate([sk2 * head_mask[0], sk2 * head_mask[1]], axis=0)
        r.dqkv[0, i // 3, :, (i % 3) * 128 : (i % 3 + 1) * 128] = tn(draw, stack).astype(BF)
        if i % 2:
            c_ds(i // 2).start()

    dpf = bwd_dp(0)
    for i in range(NP):
        nxt = bwd_dp(i + 1) if i + 1 < NP else None
        bwd_soft(i, dpf)
        if i > 0:
            bwd_out(i - 1)
        dpf = nxt
        if i == 0:
            c_ctt.wait()
            c_dm.wait()
            swapped(r.go, nn(r.ctt[0], r.dmb[c]) + nn(r.ctt[1], r.dmr[...]), LYH if fused else YLH, U)
            if fused:
                st_copy(chain_o, 0).start()
        if i == 1:
            grad_wb()
        if fused:
            pump(ATT_PUMPS[i])
    bwd_out(NP - 1)

    def c_g(i):
        return rc(sl.c_g + i, r.dqkv.at[i, 1 - c], r.dqr.at[i], to_core)

    c_g(0).start()
    r.dacc[...] = nt(r.dqkv[0, 0], r.wq[:, 0:HC]) + nt(r.dqkv[0, 1], r.wq[:, HC : 2 * HC])
    for i in range(D // 128):
        cols = slice(i * 128, (i + 1) * 128)
        if i % 2 == 0:
            c_ds(i // 2).wait()
        r.dsk[:, cols] = (r.pd[i, 0].astype(F32) + r.pdr[i, 0].astype(F32)).astype(BF)
        r.dsv[:, cols] = (r.pd[i, 1].astype(F32) + r.pdr[i, 1].astype(F32)).astype(BF)

    dk = nn(r.me[...], r.dsk[...]).astype(BF)
    dv = nn(r.me[...], r.dsv[...]).astype(BF)
    r.dqkv[1, 0] = dk[:, 0:HC]
    r.dqkv[1, 1] = dk[:, HC : 2 * HC]
    r.dqkv[2, 0] = dv[:, 0:HC]
    r.dqkv[2, 1] = dv[:, HC : 2 * HC]
    c_g(1).start()
    c_g(2).start()

    def wgrad(i):
        return (nn(r.h1t[0], r.dqkv[i, c]) + nn(r.h1t[1], r.dqr[i])).astype(BF)

    c_h1t.wait()
    c_g(0).wait()
    swapped(r.gq, wgrad(0), LYH if fused else YLH, U)
    if fused:
        st_copy(chain_q, 0).start()
        pump(KV_PUMPS[0])
    de = nt(r.dsk[...], r.k[0:H, :]) + nt(r.dsv[...], r.v[0:H, :])
    de = jnp.where(r.sel_t[:, 0:H] > 0.5, de, 0.0).astype(BF)
    for b in range(8):
        b2, b1, b0 = b // 4, (b // 2) % 2, b % 2
        j = 4 * b0 + 2 * b2 + b1
        r.ge[b * EB : (b + 1) * EB, :] = de[j * EB : (j + 1) * EB, :]
    c_g(1).wait()
    c_g(2).wait()
    swapped(r.gk, wgrad(1), YLH, U)
    gv = wgrad(2)
    swapped(r.gva, gv[:, 0:VW], YLH, U)
    swapped(r.gvb, gv[:, VW:HC], LYH if fused else YLH, U)
    if fused:
        st_copy(chain_k, 0).start()
        st_copy(chain_va, 0).start()
        st_copy(chain_vb, 0).start()
        st_copy(chain_e, 0).start()
        pump(KV_PUMPS[1])
    acc = r.dacc[...]
    for i, w in ((1, r.wk), (2, r.wv)):
        for hf in range(2):
            acc = acc + nt(r.dqkv[i, hf], w[:, hf * HC : (hf + 1) * HC])
    r.dacc[...] = acc

    gsum = None
    for i in range(T // NR):
        rows = slice(i * NR, (i + 1) * NR)
        dn, xh = r.dacc[rows, :], r.xh1[rows, :]
        part = jnp.sum(dn * xh, axis=0, keepdims=True)
        gsum = part if gsum is None else gsum + part
        if i < H // NR:
            dg = dn * ga
            m1 = jnp.sum(dg, axis=1, keepdims=True) * inv_d
            m2 = jnp.sum(dg * xh, axis=1, keepdims=True) * inv_d
            r.s_x[rows, :] = r.dmid[rows, :] + r.rs1[rows, 0:1] * (dg - m1 - xh * m2)
    outs[1].start()
    r.gvec[0:1, :] = gsum
    if fused:
        pump(KV_PUMPS[2])
    gains = jnp.concatenate([r.gvec[0:2, :], jnp.zeros((126, D), F32)], axis=0).astype(BF)
    r.gg[...] = nt(r.sa[...], gains).astype(BF)
    if fused:
        st_copy(chain_g, 0).start()

    if not fused:
        for cp in outs:
            cp.wait()
        return

    pump(END_PUMPS)

    fin = r.fin
    half = U // 2
    mine = pl.ds(pl.multiple_of(c * half, 8), half)
    first = (w0, w1, w2, w3, chain_o, chain_q, chain_k)
    homes = [(r.s_in, k * FC) for k in range(NF)] + [(r.s_out, 0), (r.s_q, 0), (r.s_k, 0), (r.s_v, 0)]
    n1 = len(first) * HC
    n0 = (NF + 1) * HC

    def send_out(src, dst):
        cp = pltpu.make_async_copy(src, dst, r.osem.at[len(outs)])
        cp.start()
        outs.append(cp)

    def c_fin(i):
        cols = (pl.ds(n0, n1 + VW - n0), pl.ds(n1 + VW, HC - VW + GN), pl.ds(0, n0))[i]
        rows = pl.ds(pl.multiple_of((1 - c) * half, 8), half)
        return rc(sl.c_fin + i, fin.at[rows, cols], r.finr.at[:, cols], to_core)

    def put(i):
        dst, base = homes[i]
        at = i * HC
        dst[:, pl.ds(pl.multiple_of(base + c * HC, 128), HC)] = fin[mine, at : at + HC]
        dst[:, pl.ds(pl.multiple_of(base + (1 - c) * HC, 128), HC)] = r.finr[:, at : at + HC]

    def take(i):
        fin[:, i * HC : (i + 1) * HC] = st_last(first[i])

    for i in (0, 1, 2, 3):
        take(i)
    hi_wb().wait()
    r.finb[...] = r.wb[hi, rows16(y * 2 * Q, 2 * Q), :].astype(F32) + r.wb2[...].astype(F32)
    c_finb = rc(sl.c_finb, r.finb.at[pl.ds(pl.multiple_of((1 - c) * Q, 8), Q)], r.finbr, to_core)
    c_finb.start()
    take(4)
    c_fin(2).start()
    take(6)
    fin[:, n1 : n1 + VW] = st_last(chain_va)
    take(5)
    c_fin(0).start()
    fin[:, n1 + VW : n1 + HC] = st_last(chain_vb)
    r.s_e[...] = st_last(chain_e)
    send_out(r.s_e, r.o_e)
    fin[:, n1 + HC : n1 + HC + GN] = st_last(chain_g)
    c_fin(1).start()
    c_finb.wait()
    r.s_back[:, pl.ds(pl.multiple_of(c * HC, 128), HC)] = r.finb[pl.ds(pl.multiple_of(c * Q, 8), Q), :]
    r.s_back[:, pl.ds(pl.multiple_of((1 - c) * HC, 128), HC)] = r.finbr[...]
    send_out(r.s_back, r.o_back)
    c_fin(2).wait()
    for i in range(NF + 1):
        put(i)
    send_out(r.s_in, r.o_in)
    send_out(r.s_out, r.o_out)
    c_fin(0).wait()
    for i in (NF + 1, NF + 2):
        put(i)
    send_out(r.s_q, r.o_q)
    send_out(r.s_k, r.o_k)
    c_fin(1).wait()
    put(len(first))
    at = n1 + HC
    r.s_g[...] = fin[mine, at : at + 128] + r.finr[:, at : at + 128]
    send_out(r.s_v, r.o_v)
    send_out(r.s_g, r.o_g)
    for cp in outs:
        cp.wait()


def staged(name):
    return f"s{name[1:]}"


def hand_over(r, names):
    for src, dst in names:
        dst[...] = src[...]
    g = jnp.concatenate([r.s_g[...], jnp.zeros((128 - r.s_g.shape[0], 128), F32)], axis=0).T
    n = r.s_g.shape[0]
    r.d_ga[...] = g[0, 0:n]
    r.d_gf[...] = g[1, 0:n]


def run_layer(mesh_shape, tokens, seg_ids, slot_doc, proj_e, g_attn, w_query, w_key, w_value, w_out, g_ffn, w_in,
              w_back, cotangent):
    n_dp, n_seq = mesh_shape
    rows, H, D = tokens.shape
    J = proj_e.shape[1]
    FF = w_in.shape[1]
    fused = n_dp == 8
    T = 2 * H
    HC, U, NF, Q = D // 2, D // 16, FF // D, FF // 32
    EB = J // 8
    NW, TW = (2, 2 * T) if fused else (NF, T)
    GN, VW = 128, 256
    sel_a, sel_c = (jnp.asarray(m, BF) for m in selections(D, FF))

    inputs = dict(
        x_in=(tokens.reshape(H, D), False),
        seg_in=(seg_ids.reshape(1, H), False),
        slot_in=(slot_doc.reshape(1, J), False),
        e_in=(proj_e, False),
        ga=(g_attn, True),
        wq_in=(w_query, False),
        wk_in=(w_key, False),
        wv_in=(w_value, False),
        wo_in=(w_out, False),
        gf=(g_ffn, True),
        w_in_in=(w_in, False),
        w_back_in=(w_back, False),
        dy_in=(cotangent.reshape(H, D), False),
        sa_in=(sel_a, False),
        sc_in=(sel_c, False),
    )
    parts = dict(
        wb=((NW, 4 * Q, HC), BF),
        wi=((NF, D // 2, HC), BF),
        go=((D // 2, HC), BF),
        gq=((D // 2, HC), BF),
        gk=((D // 2, HC), BF),
        gva=((D // 2, VW), BF),
        gvb=((D // 2, HC - VW), BF),
        gg=((D // 2, GN), BF),
        ge=((J, H), BF),
    )
    outs = dict(o_layer=((H, D), BF), o_x=((H, D), F32))
    if fused:
        outs.update(
            o_g=((U // 2, 128), F32),
            o_q=((U // 2, D), F32),
            o_k=((U // 2, D), F32),
            o_v=((U // 2, D), F32),
            o_out=((U // 2, D), F32),
            o_in=((U // 2, FF), F32),
            o_back=((Q, D), F32),
            o_e=((EB, H), F32),
        )
    else:
        outs.update(parts)
    scratch = dict(
        xb=((T, D), BF), eb=((T, J), BF), segs=((2, 1, H), jnp.int32), slot=((1, J), jnp.int32),
        wq=((D, D), BF), wk=((D, D), BF), wv=((D, D), BF), wo=((D, D), BF),
        w_in=((D, FF), BF), w_back=((FF, D), BF),
        dyb=((T, D), BF), dyh=((2, TW, HC), BF), dyr=((TW, HC), BF),
        sa=((D // 2, D), BF), sc=((4 * Q, FF // 4), BF),
        eye=((T, T), BF),
        h1=((T, D), BF), xh1=((T, D), F32), rs1=((T, 128), F32),
        q=((T, D), BF), k=((T, D), BF), v=((T, D), BF),
        sel_t=((J, T), F32), me=((T, J), BF), met=((J, T), BF),
        pk=((2, J, D), BF), pkr=((2, J, D), BF), sk=((J, D), BF), sv=((J, D), BF),

        pt=((D // 128, 2 * J, T), BF), ctx=((T, D), BF),
        mid=((T, D), F32), xh2=((T, D), F32), rs2=((T, 128), F32), h2=((T, D), BF),
        h1t=((2, D // 2, T), BF), h2t=((2, D // 2, T), BF), ctt=((2, D // 2, T), BF),
        a=((NF, T, D), BF), duf=((2, T, D), BF), u=((2, T, D), F32), g=((2, T, D), F32), du=((NF, 2, T, HC), BF), dur=((NF, T, HC), BF),
        at=((NW, 4 * Q, TW), BF), atr=((NW, 4 * Q, TW), BF),
        oacc=((H, D), F32), dacc=((T, D), F32), dmid=((T, D), F32), gvec=((8, D), F32),
        dmb=((2, T, HC), BF), dmr=((T, HC), BF), dctx=((T, D), BF), draw=((2, 2 * J, T), BF),
        pd=((D // 128, 2, J, 128), BF), pdr=((D // 128, 2, J, 128), BF),
        dsk=((J, D), BF), dsv=((J, D), BF),
        dqkv=((3, 2, T, HC), BF), dqr=((3, T, HC), BF),
    )
    if fused:
        scratch.update(
            parts,
            wb1=((2, 2 * Q, HC), BF), wb2=((2 * Q, HC), BF), finb=((2 * Q, HC), F32), finbr=((Q, HC), F32),
            h2f=((T, D), BF), dyf=((T, D), BF), af=((2, T, D), BF),
            wi1=((NF, 4 * U, HC), BF), wi2=((NF, 2 * U, HC), BF), wi3=((NF, U, HC), BF),
            go1=((4 * U, HC), BF), go2=((2 * U, HC), BF), go3=((U, HC), BF),
            gq1=((4 * U, HC), BF), gq2=((2 * U, HC), BF), gq3=((U, HC), BF),
            gk1=((4 * U, HC), BF), gk2=((2 * U, HC), BF), gk3=((U, HC), BF),
            gva1=((4 * U, VW), BF), gva2=((2 * U, VW), BF), gva3=((U, VW), BF),
            gvb1=((4 * U, HC - VW), BF), gvb2=((2 * U, HC - VW), BF), gvb3=((U, HC - VW), BF),
            gg1=((4 * U, GN), BF), gg2=((2 * U, GN), BF), gg3=((U, GN), BF),
            ge1=((4 * EB, H), BF), ge2=((2 * EB, H), BF), ge3=((EB, H), BF),
            fin=((U, NF * HC + 4 * HC + GN), F32), finr=((U // 2, NF * HC + 4 * HC + GN), F32),
        )
    counts = dict(
        x_seg=1, x_e=1, x_x=1, x_dy=1, c_pk=1, c_pv=1, c_h1t=1, c_h2t=1, c_dy=1, c_ctt=1, c_at=NF, c_du=NF, c_dm=1,
        c_ds=D // 256, c_g=3, y_wb=NF, wi=3 * NF, hi_wb=1, l_dy=1, x_dyf=1, l_h2=2, x_h2=2, c_finb=1, go=3, gq=3, gk=3, gva=3, gvb=3, gg=3, ge=3, c_fin=3,
    )
    sl, count = SimpleNamespace(), 0
    for name, n in counts.items():
        setattr(sl, name, count)
        count += n
    scratch.update((staged(n), v) for n, v in outs.items() if n[0] == "o")
    names = [*inputs, *outs, *scratch]

    def body(*refs):
        r = SimpleNamespace(**dict(zip(names, refs)))
        r.osem, r.lsem, r.ssem, r.rsem = refs[len(names) :]
        layer_body(fused, r, sl)

    res = pl.pallas_call(
        body,
        out_shape=[jax.ShapeDtypeStruct(sh, dt) for sh, dt in outs.values()],
        in_specs=[pl.BlockSpec(memory_space=pltpu.VMEM if v else pl.ANY) for _, v in inputs.values()],
        out_specs=[pl.BlockSpec(memory_space=pl.ANY if n[0] == "o" else pltpu.VMEM) for n in outs],
        scratch_shapes=[pltpu.VMEM(sh, dt) for sh, dt in scratch.values()]
        + [pltpu.SemaphoreType.DMA((10,))]
        + [pltpu.SemaphoreType.DMA((13,)), pltpu.SemaphoreType.DMA((count,)), pltpu.SemaphoreType.DMA((count,))],
        compiler_params=pltpu.CompilerParams(
            collective_id=0, has_side_effects=True, vmem_limit_bytes=60 * 1024 * 1024
        ),
        cost_estimate=pl.CostEstimate(flops=12 * 10**9, bytes_accessed=24 * 10**6, transcendentals=2 * 10**6),
    )(*[v for v, _ in inputs.values()])
    o = SimpleNamespace(**dict(zip(outs, res)))
    if fused:
        src = dict(s_layer=o.o_layer, s_x=o.o_x, s_q=o.o_q, s_k=o.o_k, s_v=o.o_v, s_out=o.o_out, s_in=o.o_in,
                   s_back=o.o_back, s_e=o.o_e, s_g=o.o_g)
        n_copy = len(src) - 1
        dst = dict(
            d_layer=((rows, H, D), BF), d_x=((rows, H, D), F32), d_q=((U // 2, D), F32), d_k=((U // 2, D), F32),
            d_v=((U // 2, D), F32), d_out=((U // 2, D), F32), d_in=((U // 2, FF), F32), d_back=((Q, D), F32),
            d_e=((EB, H), F32), d_ga=((U // 2,), F32), d_gf=((U // 2,), F32),
        )

        def tail(*refs):
            r = SimpleNamespace(**dict(zip([*src, *dst], refs)))
            r.sem = refs[-1]
            r.d_layer, r.d_x = r.d_layer.at[0], r.d_x.at[0]
            pairs = list(zip(vars(r).values(), list(vars(r).values())[len(src) :]))[:n_copy]
            hand_over(r, pairs)

        res = pl.pallas_call(
            tail,
            out_shape=[jax.ShapeDtypeStruct(sh, dt) for sh, dt in dst.values()],
            in_specs=[pl.BlockSpec(memory_space=pltpu.VMEM)] * len(src),
            out_specs=[pl.BlockSpec(memory_space=pltpu.VMEM)] * len(dst),
            scratch_shapes=[pltpu.SemaphoreType.DMA((n_copy,))],
        )(*src.values())
        o = SimpleNamespace(**dict(zip(dst, res)))
        return o.d_layer, o.d_x, o.d_ga, o.d_q, o.d_k, o.d_v, o.d_out, o.d_gf, o.d_in, o.d_back, o.d_e.T

    layer = o.o_layer.reshape(rows, H, D)
    x_grad = o.o_x.reshape(rows, H, D)

    s = lax.axis_index(SEQ)
    x, c = s // 2, s % 2
    both = (DP, SEQ)

    def scatter(v):
        return lax.psum_scatter(v, both, scatter_dimension=0, tiled=True)

    def rows_back(v, y_first):
        v = v.astype(F32).reshape(2, 2, 2, U, v.shape[-1])
        v = v.transpose(2, 1, 0, 3, 4) if y_first else v.transpose(2, 0, 1, 3, 4)
        return v.reshape(8, U, v.shape[-1])

    def whole(v, y_first):
        v = rows_back(v, y_first)
        full = jnp.zeros((8, 2, U, 2, HC), F32)
        full = lax.dynamic_update_slice(full, v[:, None, :, None, :], (0, x, 0, c, 0))
        return full.reshape(D, 2 * HC)

    wi = jnp.stack([whole(o.wi[f], True) for f in range(NF)], axis=1).reshape(D, FF)
    wo = whole(o.go, True)
    gv = jnp.concatenate([o.gva, o.gvb], axis=1)
    wqkv = [whole(o.gq, True), whole(o.gk, True), whole(gv, True)]
    gains = rows_back(o.gg, True)
    gfull = lax.dynamic_update_slice(jnp.zeros((8, 2, U, 128), F32), gains[:, None], (0, x, 0, 0)).reshape(D, 128)
    wb = o.wb.astype(F32).reshape(NF * 2, 1, 2 * Q, 1, HC)
    wb = lax.dynamic_update_slice(jnp.zeros((NF * 2, 2, 2 * Q, 2, HC), F32), wb, (0, x, 0, c, 0)).reshape(FF, D)
    ge = o.ge.astype(F32).reshape(2, 2, 2, EB, H).transpose(2, 0, 1, 3, 4).reshape(J, H).T
    return (
        layer, x_grad, scatter(gfull[:, 0]), scatter(wqkv[0]), scatter(wqkv[1]), scatter(wqkv[2]), scatter(wo),
        scatter(gfull[:, 1]), scatter(wi), scatter(wb), lax.psum_scatter(ge, DP, scatter_dimension=1, tiled=True),
    )


def solution(mesh):
    shape = (mesh.shape[DP], mesh.shape[SEQ])
    both = (DP, SEQ)
    in_specs = (
        P(DP, SEQ, None), P(DP, SEQ), P(DP, None), P(SEQ, None),
        P(), P(), P(), P(), P(), P(), P(), P(), P(DP, SEQ, None),
    )
    out_specs = (
        P(DP, SEQ, None), P(DP, SEQ, None), P(both), P(both, None), P(both, None), P(both, None),
        P(both, None), P(both), P(both, None), P(both, None), P(SEQ, DP),
    )
    return jax.shard_map(
        functools.partial(run_layer, shape), mesh=mesh, in_specs=in_specs, out_specs=out_specs, check_vma=False
    )
```
